32 devices in a mesh: batch: 8 (over z, y), fsdp: 4 (over x, core).
Axes of the slice: x: 2, y: 2, z: 4, core: 2. Of those that a mesh axis runs over, the one named last changes fastest.
Arguments:
- incoming_hidden_matrix: bfloat16 [32, 1024, 768], P(('batch', 'fsdp')), may hold values from -6 to 6
- sequence_membership: int32 [32, 1024], P(('batch', 'fsdp')), may hold values from 0 to 7, never falling along the last dimension, each value on 1 to 512 neighbouring positions
- matching_passages: int32 [32, 4], P(('batch', 'fsdp')), may hold values from 0 to 127
- softness_scale: float32 [], replicated, may hold values from 0.03 to 0.06
- combined_projection_matrix: bfloat16 [768, 2304], P('fsdp'), may hold values from -0.21875 to 0.21875
- mixer_projection_matrix: bfloat16 [768, 768], P('fsdp'), may hold values from -0.625 to 0.625
- widening_matrix: bfloat16 [768, 3072], P('fsdp'), may hold values from -0.21875 to 0.21875
- gating_matrix: bfloat16 [768, 3072], P('fsdp'), may hold values from -0.21875 to 0.21875
- narrowing_matrix: bfloat16 [3072, 768], P('fsdp'), may hold values from -0.109375 to 0.109375
- mixer_scaling_factor: bfloat16 [768], P('fsdp'), may hold values from 0.5 to 1.5
- mixer_scaling_offset: bfloat16 [768], P('fsdp'), may hold values from -0.59765625 to 0.59765625
- perceptron_scaling_factor: bfloat16 [768], P('fsdp'), may hold values from 0.5 to 1.5
- perceptron_scaling_offset: bfloat16 [768], P('fsdp'), may hold values from -0.59765625 to 0.59765625
Outputs:
- query_loss: float32 [32, 4], P(('batch', 'fsdp'))
- grad_input: float32 [32, 1024, 768], P(('batch', 'fsdp'))
- grad_w_qkv: float32 [768, 2304], P('fsdp')
- grad_w_out: float32 [768, 768], P('fsdp')
- grad_w_up: float32 [768, 3072], P('fsdp')
- grad_w_gate: float32 [768, 3072], P('fsdp')
- grad_w_down: float32 [3072, 768], P('fsdp')
- grad_gain_attn: float32 [768], P('fsdp')
- grad_bias_attn: float32 [768], P('fsdp')
- grad_gain_ffn: float32 [768], P('fsdp')
- grad_bias_ffn: float32 [768], P('fsdp')
The draws below stay inside these ranges and needn't reach their ends.
Inputs may be any that keep to these rules, and one draw needn't show every extreme that they name: `sequence_membership`: along each row the numbers never fall; every number appears in every row, on 1 to 512 tokens, and one segment of each row has exactly 512 tokens.
All inputs are finite; a program needn't handle non-finite values.
Results may differ from the reference program's by a relative error of at most 0.013.
Values may be sent and summed in bfloat16 or wider, within the bound.
No kernel may reach another device: no remote copies, remote signals or barrier semaphores. Data moves between devices by JAX's collectives and lax.ppermute only.
A program may use at most 256 MiB of HBM per device.

```python
import math
import jax
import jax.numpy as jnp
import numpy as np
from jax import lax

D = 768
HEADS = 12
HD = 64
FF = 3072
ROW = 1024
QSEG = 4
SEGS = 8
MOST = 512
ROWS_ALL = 32
DOCS = 128


def with_ends(array, own_key, low, top_value):
    longest = array.shape.index(max(array.shape))
    spots = []
    for shift in (0, 1):
        where = [jax.random.randint(jax.random.fold_in(own_key, axis), (), 0, length) for axis, length in enumerate(array.shape)]
        where[longest] = (where[longest] + shift) % array.shape[longest]
        spots.append(tuple(where))
    return array.at[spots[0]].set(low).at[spots[1]].set(top_value)


def shard_levels(rng, shape, pieces, least, largest):
    gain = 1.0
    for dim, parts in pieces:
        heights = jax.random.uniform(jax.random.fold_in(jax.random.fold_in(rng, 6), dim), (parts,), jnp.float32, least / len(pieces), largest / len(pieces))
        gain = gain * jnp.repeat(jnp.exp(heights), shape[dim] // parts).reshape((-1,) + (1,) * (len(shape) - 1 - dim))
    return gain


def split_up(amount, total, limit, lean):
    loads = [(1 << 20) // math.isqrt(grade ** lean) + 1 for grade in range(2, amount + 1)]
    rest, given = total - limit - (amount - 1), [1] * (amount - 1)
    while rest > 0:
        movable = [i for i in range(amount - 1) if given[i] < limit]
        mass, budget = sum([loads[i] for i in movable]), rest
        for i in movable:
            extra = min(limit - given[i], max(1, budget * loads[i] // mass), rest)
            given[i] = given[i] + extra
            rest = rest - extra
    return np.array([limit] + given)


def uneven(stream_key, count, total, bound, skew):
    if count == 2:
        one = jax.random.randint(stream_key, (), max(1, total - bound), min(bound, total - 1) + 1)
        return jnp.stack([one, total - one])
    lengths = jnp.asarray(split_up(count, total, bound, skew), jnp.int32)
    couples = (count - 1) // 2
    giver, taker = lengths[1:1 + 2 * couples:2], lengths[2:2 + 2 * couples:2]
    margin = jnp.minimum(giver - 1, bound - taker)
    moved = jax.random.randint(jax.random.fold_in(stream_key, 1), (couples,), 0, 1 << 20) % (margin + 1)
    lengths = lengths.at[1:1 + 2 * couples:2].set(giver - moved).at[2:2 + 2 * couples:2].set(taker + moved)
    return lengths[jax.random.permutation(jax.random.fold_in(stream_key, 2), count)]


def scatter_about(own_key, extent, scale, reach, split=(), kind=jnp.bfloat16):
    array = scale * jax.random.normal(own_key, extent, jnp.float32)
    if split:
        array = array * shard_levels(own_key, extent, split, -0.22, 0.18)
    return jnp.clip(array, -reach, reach).astype(kind)


def setup_inputs(seed: int = 0) -> dict:
    splits = jax.random.split(jax.random.key(seed), 14)
    return {
        "incoming_hidden_matrix": scatter_about(splits[0], (ROWS_ALL, ROW, D), 1.0, 6.0, ((0, 32),)),
        "sequence_membership": jax.vmap(lambda own: jnp.searchsorted(jnp.cumsum(uneven(own, SEGS, ROW, MOST, 2)), jnp.arange(ROW), side="right"))(jax.random.split(splits[1], ROWS_ALL)).reshape((ROWS_ALL, ROW)).astype(jnp.int32),
        "matching_passages": with_ends(jax.random.randint(splits[2], (ROWS_ALL, QSEG), 0, DOCS), jax.random.fold_in(splits[2], 1), 0, DOCS - 1).astype(jnp.int32),
        "softness_scale": jnp.clip(jax.random.uniform(splits[3], (), jnp.float32, 0.03, 0.06), 0.03, 0.06),
        "combined_projection_matrix": scatter_about(splits[4], (D, 3 * D), D ** -0.5, 0.21875, ((0, 4),)),
        "mixer_projection_matrix": scatter_about(splits[5], (D, D), (D // 8) ** -0.5, 0.625, ((0, 4),)),
        "widening_matrix": scatter_about(splits[6], (D, FF), D ** -0.5, 0.21875, ((0, 4),)),
        "gating_matrix": scatter_about(splits[7], (D, FF), D ** -0.5, 0.21875, ((0, 4),)),
        "narrowing_matrix": scatter_about(splits[8], (FF, D), FF ** -0.5, 0.109375, ((0, 4),)),
        "mixer_scaling_factor": jnp.clip(1.0 + 0.1 * jax.random.normal(splits[9], (D,), jnp.float32), 0.5, 1.5).astype(jnp.bfloat16),
        "mixer_scaling_offset": scatter_about(splits[10], (D,), 0.1, 0.59765625, ((0, 4),)),
        "perceptron_scaling_factor": jnp.clip(1.0 + 0.1 * jax.random.normal(splits[11], (D,), jnp.float32), 0.5, 1.5).astype(jnp.bfloat16),
        "perceptron_scaling_offset": scatter_about(splits[12], (D,), 0.1, 0.59765625, ((0, 4),)),
    }


@jax.custom_vjp
def low(v):
    return lax.optimization_barrier(v.astype(jnp.bfloat16)).astype(jnp.float32)

@jax.custom_vjp
def low_back(v):
    return v

def low_keep(v):
    return (low(v), None)

def low_pass(kept, grad):
    return (grad,)

def back_keep(v):
    return (v, None)

def back_low(kept, grad):
    return (low(grad),)
low.defvjp(low_keep, low_pass)
low_back.defvjp(back_keep, back_low)
EPSILON = 1e-06
HIGHEST = lax.Precision.HIGHEST

def rounded(value_in):
    return low(low_back(value_in))

def exact_matrix_multiply(left_op, right_op):
    return jnp.dot(left_op, right_op, precision=HIGHEST, preferred_element_type=jnp.float32)

def layer_norm(value_in, gain_vec, offset_vec):
    center = value_in - lax.optimization_barrier(jnp.mean(value_in, axis=-1, keepdims=True))
    spread = lax.optimization_barrier(jnp.mean(center * center, axis=-1, keepdims=True))
    return center * lax.rsqrt(spread + EPSILON) * gain_vec + offset_vec

def rotary_tables(segment_row):
    row_len = segment_row.shape[0]
    seg_marks = (segment_row[:, None] == jnp.arange(SEGS, dtype=jnp.int32)[None, :]).astype(jnp.int32)
    seg_sizes = lax.optimization_barrier(jnp.sum(seg_marks, axis=0))
    firsts = jnp.cumsum(seg_sizes) - seg_sizes
    positions = jnp.arange(row_len, dtype=jnp.int32) - lax.optimization_barrier(jnp.sum(seg_marks * firsts[None, :], axis=1))
    inverse = 1000.0 ** (-(jnp.arange(HD // 2, dtype=jnp.float32) * 2.0) / HD)
    angles = positions.astype(jnp.float32)[:, None] * inverse[None, :]
    return (jnp.cos(angles), jnp.sin(angles))

def rotate(tensor, cosine, sine_tab):
    middle = tensor.shape[-1] // 2
    first_part = tensor[..., :middle]
    second_part = tensor[..., middle:]
    cos_b = cosine[:, None, :]
    sin_b = sine_tab[:, None, :]
    return jnp.concatenate([first_part * cos_b - second_part * sin_b, second_part * cos_b + first_part * sin_b], axis=-1)

def embed_row(tokens, segment_row, parameter_collection):
    combined_projection_matrix, mixer_projection_matrix, widening_matrix, gating_matrix, narrowing_matrix, mixer_scaling_factor, mixer_scaling_offset, perceptron_scaling_factor, perceptron_scaling_offset = parameter_collection
    row_len = tokens.shape[0]
    scale_factor = 1.0 / math.sqrt(HD)
    cosine, sine_tab = rotary_tables(segment_row)
    joined = low_back(exact_matrix_multiply(tokens, combined_projection_matrix)).reshape(row_len, 3, HEADS, HD)
    queries = low(rotate(joined[:, 0], cosine, sine_tab))
    keys_all = low(rotate(joined[:, 1], cosine, sine_tab))
    values = low(joined[:, 2])
    scores = low_back(jnp.einsum('qhd,khd->hqk', queries, keys_all, precision=HIGHEST) * scale_factor)
    same_seg = segment_row[:, None] == segment_row[None, :]
    scores = jnp.where(same_seg[None], scores, -1e+30)
    attn_probs = low(jax.nn.softmax(scores, axis=-1))
    attended = rounded(jnp.einsum('hqk,khd->qhd', attn_probs, values, precision=HIGHEST).reshape(row_len, D))
    branch = low_back(exact_matrix_multiply(attended, mixer_projection_matrix))
    hidden_one = layer_norm(tokens + branch, mixer_scaling_factor, mixer_scaling_offset)
    hidden_low = low(hidden_one)
    up_proj = low_back(exact_matrix_multiply(hidden_low, widening_matrix))
    gate_proj = low_back(exact_matrix_multiply(hidden_low, gating_matrix))
    product = low(jax.nn.silu(gate_proj) * up_proj)
    ffn_out = low_back(exact_matrix_multiply(product, narrowing_matrix))
    hidden_two = layer_norm(hidden_one + ffn_out, perceptron_scaling_factor, perceptron_scaling_offset)
    seg_marks = (segment_row[:, None] == jnp.arange(SEGS, dtype=jnp.int32)[None, :]).astype(jnp.float32)
    pooled = lax.dot_general(seg_marks, hidden_two, (((0,), (0,)), ((), ())), precision=HIGHEST, preferred_element_type=jnp.float32)
    pooled = pooled / lax.optimization_barrier(jnp.sum(seg_marks, axis=0))[:, None]
    normed = pooled * lax.rsqrt(lax.optimization_barrier(jnp.sum(pooled * pooled, axis=-1, keepdims=True)) + EPSILON)
    return low(normed)

def apply_whole_stack(word_piece_codes_whole, parameter_collection, softness_scale, sequence_membership, matching_passages):

    def one_row(inputs):
        return embed_row(inputs[0], inputs[1], parameter_collection)
    embeds = lax.map(jax.checkpoint(one_row), (word_piece_codes_whole, sequence_membership))
    question_embedding_rows = embeds[:, :QSEG].reshape(-1, D)
    passage_embedding_rows = embeds[:, QSEG:].reshape(-1, D)
    pairwise_match_scores = exact_matrix_multiply(question_embedding_rows, passage_embedding_rows.T) / softness_scale
    log_sums = jax.nn.logsumexp(pairwise_match_scores, axis=-1)
    chosen = jnp.take_along_axis(pairwise_match_scores, matching_passages.reshape(-1, 1).astype(jnp.int32), axis=1)[:, 0]
    return (log_sums - chosen).reshape(matching_passages.shape[0], QSEG)

def reference(incoming_hidden_matrix, sequence_membership, matching_passages, softness_scale, combined_projection_matrix, mixer_projection_matrix, widening_matrix, gating_matrix, narrowing_matrix, mixer_scaling_factor, mixer_scaling_offset, perceptron_scaling_factor, perceptron_scaling_offset):
    parameter_collection = tuple((weight_arr.astype(jnp.float32) for weight_arr in (combined_projection_matrix, mixer_projection_matrix, widening_matrix, gating_matrix, narrowing_matrix, mixer_scaling_factor, mixer_scaling_offset, perceptron_scaling_factor, perceptron_scaling_offset)))
    tokens = incoming_hidden_matrix.astype(jnp.float32)

    def total_fn(word_piece_operand, parameter_operand):
        return apply_whole_stack(word_piece_operand, parameter_operand, softness_scale, sequence_membership, matching_passages)
    losses, pullback = jax.vjp(total_fn, tokens, parameter_collection)
    grad_tokens, grad_weights = pullback(jnp.ones_like(losses))
    return (losses, grad_tokens, grad_weights[0], grad_weights[1], grad_weights[2], grad_weights[3], grad_weights[4], grad_weights[5], grad_weights[6], grad_weights[7], grad_weights[8])
```

```python
import functools
import math

import jax
import jax.numpy as jnp
from jax import lax
from jax.experimental import pallas as pl
from jax.experimental.pallas import tpu as pltpu
from jax.sharding import PartitionSpec as P

HEADS = 12
HD = 64
QSEG = 4
SEGS = 8
EPSILON = 1e-06
NEG = -1e30
LANE = 128
BLOCK = 256
PAIRS = HEADS // 2
PART = 384
SMALL = 16
MIB = 2**20

bf16 = jnp.bfloat16
f32 = jnp.float32


def dot(left, right, left_dim, right_dim):
    return lax.dot_general(
        left, right, (((left_dim,), (right_dim,)), ((), ())), preferred_element_type=f32
    )


def split_three(value):
    high = value.astype(bf16)
    rest = value - high.astype(f32)
    middle = rest.astype(bf16)
    low = (rest - middle.astype(f32)).astype(bf16)
    return high, middle, low


def params(limit=60):
    return dict(
        compiler_params=pltpu.CompilerParams(vmem_limit_bytes=limit * MIB),
        cost_estimate=pl.CostEstimate(flops=1, bytes_accessed=1, transcendentals=0),
    )


def shape(dims, dtype):
    return jax.ShapeDtypeStruct(dims, dtype)


ANY = pl.BlockSpec(memory_space=pl.ANY)


def whole(dims):
    return pl.BlockSpec(dims, lambda *_: (0,) * len(dims))


def swap_halves(tile):
    lane = lax.broadcasted_iota(jnp.int32, (1, LANE), 1)
    in_first = (lane & 63) < 32
    return jnp.where(in_first, pltpu.roll(tile, 96, 1), pltpu.roll(tile, 32, 1))


def norm_parts(value):
    center = value - jnp.mean(value, axis=1, keepdims=True)
    spread = jnp.mean(center * center, axis=1, keepdims=True)
    inv = lax.rsqrt(spread + EPSILON)
    return center * inv, inv


def norm_back(scaled, xhat, inv):
    mean_one = jnp.mean(scaled, axis=1, keepdims=True)
    mean_two = jnp.mean(scaled * xhat, axis=1, keepdims=True)
    return inv * (scaled - mean_one - xhat * mean_two)


def piece_copies(row_of, pieces, scratch, sems):
    return [
        pltpu.make_async_copy(
            piece, scratch.at[pl.ds(pl.multiple_of(row_of(k), 32), piece.shape[0])], sems.at[k]
        )
        for k, piece in enumerate(pieces)
    ]


def store_turned(ref, value, own, columns=slice(None)):
    rows = ref.shape[0] // 4
    turned = value.T
    for shard in range(4):
        at = pl.ds(pl.multiple_of((shard ^ own) * rows, 64), rows)
        ref[at, columns] = turned[shard * rows : (shard + 1) * rows]


def qkv_kernel(rows_ref, x_ref, cos_ref, sin_ref, *refs):
    pieces = refs[:4]
    out_ref, xt_ref, weight, sems = refs[4:]
    step = pl.program_id(0)
    width = x_ref.shape[1]

    @pl.when(step == 0)
    def _():
        copies = piece_copies(lambda k: rows_ref[k], pieces, weight, sems)
        for copy in copies:
            copy.start()
        store_turned(xt_ref, x_ref[...], rows_ref[6])
        for copy in copies:
            copy.wait()

    joined = dot(x_ref[...], weight[:, pl.ds(pl.multiple_of(step * width, LANE), width)], 1, 0)

    @pl.when(step < 2)
    def _():
        scale = jnp.where(step == 0, 1.0 / math.sqrt(HD), 1.0)
        cos, sin = cos_ref[...] * scale, sin_ref[...] * scale
        for t in range(width // LANE):
            tile = joined[:, t * LANE : (t + 1) * LANE]
            out_ref[:, t * LANE : (t + 1) * LANE] = (tile * cos + swap_halves(tile) * sin).astype(bf16)

    @pl.when(step == 2)
    def _():
        out_ref[...] = joined.astype(bf16)


def key_range(first, count, total):
    blocks = (count + 1) >> 1
    first = jnp.minimum(first, total // LANE - 2 * blocks)
    return pl.multiple_of(first * LANE, LANE), blocks


def attend_kernel(lo_ref, n_ref, q_ref, k_ref, v_ref, mq_ref, mk_ref, o_ref, lse_ref):
    step = pl.program_id(0)
    lo, count = key_range(lo_ref[step], n_ref[step], k_ref.shape[0])
    first = lax.broadcasted_iota(jnp.int32, (1, LANE), 1) < HD
    zero = jnp.zeros((), bf16)
    mask_q = mq_ref[...]

    def run(width):
        keys = pl.ds(lo, width)
        mask_k = mk_ref[keys, :]

        def pair(p, _):
            cols = pl.ds(pl.multiple_of(p * LANE, LANE), LANE)
            q_pair, k_pair, v_pair = q_ref[:, cols], k_ref[keys, cols], v_ref[keys, cols]
            k_ext = jnp.concatenate([k_pair, mask_k], axis=1)
            outs, sums = [], []
            for h in range(2):
                q_one = jnp.where(first if h == 0 else ~first, q_pair, zero)
                scores = dot(jnp.concatenate([q_one, mask_q], axis=1), k_ext, 1, 1)
                peak = jnp.max(scores, axis=1, keepdims=True)
                weight = jnp.exp(scores - peak)
                total = jnp.sum(weight, axis=1, keepdims=True)
                outs.append(dot(weight.astype(bf16), v_pair, 1, 0) * (1.0 / total))
                sums.append(peak + jnp.log(total))
            o_ref[:, cols] = jnp.where(first, outs[0], outs[1]).astype(bf16)
            turned = jnp.where(first, sums[0], sums[1]).T
            lse_ref[p, 0:1, :] = turned[0:1]
            lse_ref[p, 1:2, :] = turned[HD : HD + 1]
            return 0

        lax.fori_loop(0, PAIRS // 2, pair, 0, unroll=True)

    for n in range(1, k_ref.shape[0] // BLOCK + 1):
        pl.when(count == n)(functools.partial(run, n * BLOCK))


def attend_back_kernel(
    lo_ref, n_ref, q_ref, k_ref, v_ref, do_ref, lse_ref, dl_ref, mq_ref, mk_ref, cos_ref, sin_ref, cosb_ref, sinb_ref,
    gq_ref, gk_ref, gv_ref, dq_acc,
):
    step = pl.program_id(0)

    @pl.when(step == 0)
    def _():
        dq_acc[...] = jnp.zeros_like(dq_acc)

    lo, count = key_range(lo_ref[step], n_ref[step], q_ref.shape[0])
    first = lax.broadcasted_iota(jnp.int32, (1, LANE), 1) < HD
    zero = jnp.zeros((), bf16)
    mask_k = mk_ref[...]
    cosb, sinb = cosb_ref[...], sinb_ref[...]

    def run(width):
        queries = pl.ds(lo, width)
        mask_q = mq_ref[queries, :]

        def pair(p, _):
            cols = pl.ds(pl.multiple_of(p * LANE, LANE), LANE)
            k_pair, v_pair = k_ref[:, cols], v_ref[:, cols]
            q_pair, do_pair = q_ref[queries, cols], do_ref[queries, cols]
            q_ext = jnp.concatenate([q_pair, mask_q], axis=1)
            k_turned = k_pair.T
            dk, dv = [], []
            for h in range(2):
                mine = first if h == 0 else ~first
                k_one, v_one = jnp.where(mine, k_pair, zero), jnp.where(mine, v_pair, zero)
                scores = dot(jnp.concatenate([k_one, mask_k], axis=1), q_ext, 1, 1)
                probs = jnp.exp(scores - lse_ref[p, h : h + 1, queries])
                dprobs = dot(v_one, do_pair, 1, 1)
                dscores = (probs * (dprobs - dl_ref[p, h : h + 1, queries])).astype(bf16)
                dv.append(dot(probs.astype(bf16), do_pair, 1, 0))
                dk.append(dot(dscores, q_pair, 1, 0))
                rows = pl.ds(pl.multiple_of(p * LANE + h * HD, HD), HD)
                dq_acc[rows, queries] += dot(k_turned[h * HD : (h + 1) * HD], dscores, 1, 0)
            gv_ref[:, cols] = jnp.where(first, dv[0], dv[1]).astype(bf16)
            grad = jnp.where(first, dk[0], dk[1])
            gk_ref[:, cols] = (grad * cosb - swap_halves(grad) * sinb).astype(bf16)
            return 0

        lax.fori_loop(0, PAIRS // 2, pair, 0, unroll=True)

    for n in range(1, q_ref.shape[0] // BLOCK + 1):
        pl.when(count == n)(functools.partial(run, n * BLOCK))

    @pl.when(step == pl.num_programs(0) - 1)
    def _():
        cos, sin = cos_ref[...], sin_ref[...]
        for p in range(PAIRS // 2):
            grad = dq_acc[p * LANE : (p + 1) * LANE, :].T * (1.0 / math.sqrt(HD))
            gq_ref[:, p * LANE : (p + 1) * LANE] = (grad * cos - swap_halves(grad) * sin).astype(bf16)


def mixer_kernel(rows_ref, att0_ref, att1_ref, x_ref, vec_ref, *refs):
    pieces = refs[:6]
    xhat_ref, inv_ref, low_ref, lowt_ref, full_ref, weight, sems, out_sem = refs[7:]
    step = pl.program_id(0)
    out_copy = pltpu.make_async_copy(weight, full_ref, out_sem)

    @pl.when(step == 0)
    def _():
        copies = piece_copies(lambda k: rows_ref[k], pieces, weight, sems)
        for copy in copies:
            copy.start()
        for copy in copies:
            copy.wait()
        out_copy.start()

    branch = dot(att0_ref[...], weight[0:PART, :], 1, 0) + dot(att1_ref[...], weight[PART:, :], 1, 0)
    xhat, inv = norm_parts(x_ref[...].astype(f32) + branch)
    low = (xhat * vec_ref[0:1] + vec_ref[1:2]).astype(bf16)
    xhat_ref[...] = xhat
    inv_ref[...] = jnp.broadcast_to(inv, inv_ref.shape)
    low_ref[...] = low
    store_turned(lowt_ref, low, rows_ref[6])

    @pl.when(step == pl.num_programs(0) - 1)
    def _():
        out_copy.wait()


def ffn_kernel(rows_ref, low_ref, xhat_ref, vec_ref, mark_ref, cnt_ref, *refs):
    up_pieces, gate_pieces, down_pieces = refs[0:6], refs[6:12], refs[12:18]
    up_fac_ref, gate_fac_ref, prod_ref, xhat2_ref, inv2_ref, pool_ref, emb_ref = refs[18:25]
    full_up, full_gate, full_down = refs[25:28]
    w_up, w_gate, w_down, sems, down_sems, out_sems, pooled, total = refs[28:]
    step = pl.program_id(0)
    own = rows_ref[6]
    tokens, width = low_ref.shape
    wide = prod_ref.shape[1]
    steps = 4

    def in_copies(rel):
        cols = pl.ds(pl.multiple_of((own ^ rel) * wide, LANE), wide)
        copies = []
        for which, (pieces, scratch) in enumerate(((up_pieces, w_up), (gate_pieces, w_gate))):
            for k, piece in enumerate(pieces):
                rows = pl.ds(pl.multiple_of(rows_ref[k], 32), piece.shape[0])
                copies.append(
                    pltpu.make_async_copy(piece.at[:, cols], scratch.at[rel, rows], sems.at[rel * 12 + which * 6 + k])
                )
        for k in ((0,), (1,), (2, 3), (4, 5))[rel]:
            piece = down_pieces[k]
            start = 0 if k < 2 else pl.multiple_of(rows_ref[7 + (k & 1)], 32)
            copies.append(
                pltpu.make_async_copy(piece, w_down.at[rel, pl.ds(start, piece.shape[0])], down_sems.at[k])
            )
        return copies

    def out_copies(rel):
        cols = pl.ds(pl.multiple_of((own ^ rel) * wide, LANE), wide)
        return [
            pltpu.make_async_copy(w_up.at[rel], full_up.at[:, cols], out_sems.at[rel * 3]),
            pltpu.make_async_copy(w_gate.at[rel], full_gate.at[:, cols], out_sems.at[rel * 3 + 1]),
            pltpu.make_async_copy(w_down.at[rel], full_down.at[cols], out_sems.at[rel * 3 + 2]),
        ]

    @pl.when(step == 0)
    def _():
        for rel in range(2):
            for copy in in_copies(rel):
                copy.start()
        pooled[...] = jnp.zeros_like(pooled)

    for rel in range(steps):

        @pl.when(step == rel)
        def _(rel=rel):
            for copy in in_copies(rel):
                copy.wait()
            for copy in out_copies(rel):
                copy.start()
            if 0 < rel < steps - 1:
                for copy in in_copies(rel + 1):
                    copy.start()

    rows_at = 512

    def rows_block(i, _):
        rows = pl.ds(pl.multiple_of(i * rows_at, rows_at), rows_at)
        low = low_ref[rows, :]
        up = dot(low, w_up[step], 1, 0)
        gate = dot(low, w_gate[step], 1, 0)
        sig = 0.5 * jnp.tanh(0.5 * gate) + 0.5
        act = gate * sig
        up_fac_ref[rows, :] = act.astype(bf16)
        gate_fac_ref[rows, :] = (up * (sig + act * (1.0 - sig))).astype(bf16)
        prod = (act * up).astype(bf16)
        prod_ref[rows, :] = prod
        ffn = dot(prod, w_down[step], 1, 0)

        total[rows, :] = jnp.where(step == 0, ffn, total[rows, :] + ffn)
        return 0

    lax.fori_loop(0, tokens // rows_at, rows_block, 0, unroll=True)

    @pl.when(step == steps - 1)
    def _():
        def norm_block(i, _):
            rows = pl.ds(pl.multiple_of(i * BLOCK, BLOCK), BLOCK)
            xhat, inv = norm_parts(xhat_ref[rows, :] * vec_ref[0:1] + vec_ref[1:2] + total[rows, :])
            xhat2_ref[rows, :] = xhat
            inv2_ref[rows, :] = jnp.broadcast_to(inv, (BLOCK, LANE))
            marks = mark_ref[:, rows]
            part = jnp.zeros(pooled.shape, f32)
            for piece in split_three(xhat):
                part += dot(marks, piece, 1, 0)
            pooled[...] += part
            return 0

        lax.fori_loop(0, tokens // BLOCK, norm_block, 0)
        mean_xhat = pooled[0:SEGS] / cnt_ref[:, 0:1]
        pool = mean_xhat * vec_ref[2:3] + vec_ref[3:4]
        inv_len = lax.rsqrt(jnp.sum(pool * pool, axis=1, keepdims=True) + EPSILON)
        pool_ref[0:SEGS] = mean_xhat
        pool_ref[SEGS:] = pool
        emb_ref[...] = (pool * inv_len).astype(bf16)
        for rel in range(steps):
            for copy in out_copies(rel):
                copy.wait()


def loss_kernel(soft_ref, blk_ref, all_ref, ids_ref, pool_ref, cnt_ref, loss_ref, rows_ref, small_ref, acc):
    step = pl.program_id(0)
    soft = soft_ref[0]
    width = acc.shape[1]
    block, everyone = blk_ref[:, 0:width], all_ref[:, 0:width]
    target = blk_ref[:, width : width + LANE].astype(f32)
    target = target[:, 0:1] * 32.0 + target[:, 1:2]
    row = lax.broadcasted_iota(jnp.int32, (block.shape[0], 1), 0)
    asks = (row & (SEGS - 1)) < QSEG
    ids = ids_ref[0:1, :]
    logits = jnp.where(ids >= 0, dot(block, everyone, 1, 1) / soft, NEG)
    hit = asks & (target == ids)
    peak = jnp.max(logits, axis=1, keepdims=True)
    lse = peak + jnp.log(jnp.sum(jnp.exp(logits - peak), axis=1, keepdims=True))
    grad = (jnp.exp(logits - lse) - jnp.where(hit, 1.0, 0.0)) / soft
    grad = jnp.where(asks, grad, 0.0)
    turned = grad[:, 0:LANE].T[0:SEGS]
    part = jnp.zeros(acc.shape, f32)
    for piece in split_three(turned):
        part += dot(piece, block, 1, 0)

    @pl.when(step == 0)
    def _():
        own = part
        for piece in split_three(grad[0:SEGS]):
            own += dot(piece, everyone, 1, 0)
        acc[...] = own
        chosen = jnp.sum(jnp.where(hit, logits, 0.0), axis=1, keepdims=True)
        loss_ref[...] = jnp.broadcast_to((lse - chosen)[0:SEGS], loss_ref.shape)

    @pl.when(step > 0)
    def _():
        acc[...] += part

    @pl.when(step == pl.num_programs(0) - 1)
    def _():
        g = acc[...]
        mean_xhat, pool = pool_ref[0:SEGS], pool_ref[SEGS:]
        inv_len = lax.rsqrt(jnp.sum(pool * pool, axis=1, keepdims=True) + EPSILON)
        back = inv_len * g - inv_len * inv_len * inv_len * pool * jnp.sum(pool * g, axis=1, keepdims=True)
        rows_ref[...] = jnp.zeros_like(rows_ref)
        rows_ref[0:SEGS] = back / cnt_ref[:, 0:1]
        small_ref[...] = jnp.zeros_like(small_ref)
        small_ref[0:1] = jnp.sum(back * mean_xhat, axis=0, keepdims=True)
        small_ref[1:2] = jnp.sum(back, axis=0, keepdims=True)


def norm_two_back_kernel(mq_ref, rows_ref, xhat_ref, inv_ref, vec_ref, sum_ref, low_ref, lowt_ref):
    marks = mq_ref[...]
    scaled = jnp.zeros(xhat_ref.shape, f32)
    for piece in split_three(rows_ref[...] * vec_ref[2:3]):
        scaled += dot(marks, piece, 1, 0)
    grad = norm_back(scaled, xhat_ref[...], inv_ref[:, 0:1])
    sum_ref[...] = grad
    low = grad.astype(bf16)
    low_ref[...] = low
    lowt_ref[...] = low.T


def ffn_back_kernel(
    g, groups, info_ref, prod_any, up_fac_any, gate_fac_any, low_any, lowt_any, hidt_any, wu_any, wg_any, wd_any, hid_any,
    *refs,
):
    out_any, keep_any, send_any = refs[-18:-15]
    prod, up_fac, gate_fac, low, lowt, hidt, wu, wg, wd, hid, keep, send, total, sems, out_sems = refs[-15:]
    own = info_ref[4]
    rows = keep.shape[3]
    targets = [(keep, 0), (send, 0), (keep, 1), (send, 1)]

    def strip(index):
        if isinstance(index, int):
            return pl.ds((index * groups + g) * BLOCK, BLOCK)
        return pl.ds(pl.multiple_of((index * groups + g) * BLOCK, BLOCK), BLOCK)

    def blocks(source, to, first, relative=False, by_rows=False):
        copies = []
        for k in range(4):
            here, there = strip(info_ref[k] if relative else k), pl.ds(k * BLOCK, BLOCK)
            if by_rows:
                copy = pltpu.make_async_copy(source.at[here], to.at[there], sems.at[first + k])
            else:
                copy = pltpu.make_async_copy(source.at[:, here], to.at[:, there], sems.at[first + k])
            copies.append(copy)
        return copies

    def one(source, to, first):
        return [pltpu.make_async_copy(source, to, sems.at[first])]

    loads = dict(
        low=one(low_any, low, 0),
        wd=blocks(wd_any, wd, 4, by_rows=True),
        up_fac=blocks(up_fac_any, up_fac, 8),
        hidt=one(hidt_any, hidt, 1),
        gate_fac=blocks(gate_fac_any, gate_fac, 12),
        lowt=one(lowt_any, lowt, 2),
        prod=blocks(prod_any, prod, 16, relative=True),
        wu=blocks(wu_any, wu, 20),
        wg=blocks(wg_any, wg, 24),
        hid=one(hid_any, hid, 3),
    )
    for copies in loads.values():
        for copy in copies:
            copy.start()

    def arrive(*names):
        for name in names:
            for copy in loads[name]:
                copy.wait()

    def store(rel, tile, value):
        ref, across = targets[rel]
        away = (tile // 3) ^ own
        ref[across, away & 1, away >> 1, :, tile % 3 * LANE : (tile % 3 + 1) * LANE] = value.astype(bf16)

    def store_columns(kind, value):
        for rel in range(4):
            for t in range(8):
                store(rel, kind * 8 + t, value[rel * rows : (rel + 1) * rows, t * LANE : (t + 1) * LANE])

    arrive("low", "wd", "up_fac")
    dprod = dot(low[...], wd[...], 1, 1)
    dup = (dprod * up_fac[...].astype(f32)).astype(bf16)
    arrive("gate_fac")
    dgate = (dprod * gate_fac[...].astype(f32)).astype(bf16)
    arrive("hidt")
    store_columns(0, dot(hidt[...], dup, 1, 0))
    store_columns(1, dot(hidt[...], dgate, 1, 0))
    arrive("lowt", "prod")
    down = dot(lowt[...], prod[...], 1, 0)
    for rel in range(4):
        for k in range(4):
            for t in range(2):
                at = rel * BLOCK + t * LANE
                store(rel, 16 + 2 * k + t, down[k * rows : (k + 1) * rows, at : at + LANE])
    outs = [
        pltpu.make_async_copy(send, send_any, out_sems.at[0]),
        pltpu.make_async_copy(keep, keep_any, out_sems.at[1]),
        pltpu.make_async_copy(total, out_any, out_sems.at[2]),
    ]
    outs[0].start()
    outs[1].start()
    arrive("wu", "wg", "hid")
    total[...] = hid[...] + dot(dup, wu[...], 1, 1) + dot(dgate, wg[...], 1, 1)
    outs[2].start()
    for copy in outs:
        copy.wait()


def mixer_back_kernel(info_ref, grad_ref, xhat_ref, inv_ref, vec_ref, att0_ref, att1_ref, w_ref, heads_ref, *refs):
    sum_ref, low_ref, datt_ref, dl_ref, attt_ref, small_ref = refs[-6:]
    step = pl.program_id(0)
    grad, xhat = grad_ref[...], xhat_ref[...]
    out = norm_back(grad * vec_ref[0:1], xhat, inv_ref[:, 0:1])
    sum_ref[...] = out
    low = out.astype(bf16)
    low_ref[...] = low
    datt = dot(low, w_ref[...], 1, 1).astype(bf16)
    datt_ref[...] = datt
    att = jnp.concatenate([att0_ref[...], att1_ref[...]], axis=1)
    store_turned(attt_ref, att, info_ref[0])
    inner = datt.astype(f32) * att.astype(f32)
    heads = heads_ref[...]
    rows = jnp.zeros((heads.shape[0], inner.shape[0]), f32)
    for piece in split_three(inner)[:2]:
        rows += dot(heads, piece, 1, 1)
    for p in range(PAIRS):
        dl_ref[p] = rows[p * 8 : (p + 1) * 8]

    @pl.when(step == 0)
    def _():
        small_ref[...] = jnp.zeros_like(small_ref)

    small_ref[0:1] += jnp.sum(grad * xhat, axis=0, keepdims=True)
    small_ref[1:2] += jnp.sum(grad, axis=0, keepdims=True)


def qkv_back_kernel(extra, info_ref, xt_ref, attt_ref, gq_ref, gk_ref, gv_ref, gb_ref, small_ref, *refs):
    keep_ref, send_ref = refs[-2:]
    step = pl.program_id(0)
    half = keep_ref.shape[3] - extra
    own_y = info_ref[4] & 1
    targets = [(keep_ref, 0), (send_ref, 0), (keep_ref, 1), (send_ref, 1)]

    def run(left_ref, right_ref):
        value = dot(left_ref[...], right_ref[...], 1, 0).astype(bf16)
        for rel, (ref, across) in enumerate(targets):
            for y in range(2):
                at = (2 * rel + y) * half
                ref[across, y ^ own_y, 0, 0:half, :] = value[at : at + half]
                if extra:
                    ref[across, y ^ own_y, 0, half:, :] = small_ref[info_ref[rel], y].astype(bf16)

    for which, right_ref in enumerate((gq_ref, gk_ref, gv_ref, gb_ref)):
        pl.when(step == which)(functools.partial(run, xt_ref if which < 3 else attt_ref, right_ref))


BIT = dict(y=0, z0=1, z1=2)


def copy_part(order, own, part, pair, write):
    away = part ^ own
    one, two, three = [(away >> BIT[axis]) & 1 for axis in order if axis != "x"]
    for which in range(2):

        @pl.when(one == which)
        def _(which=which):
            write(pair[which][two * 2 + three].astype(f32))


def ffn_out_kernel(orders, info_ref, *refs):
    groups = (len(refs) - 3) // 2
    up_ref, gate_ref, down_ref = refs[-3:]
    own = info_ref[4]
    rows = up_ref.shape[0]
    for g in range(groups):
        for part in range(8):

            def write(value, g=g, part=part):
                for t in range(3):
                    tile = part * 3 + t
                    block = value[:, t * LANE : (t + 1) * LANE]
                    kind, within = tile // 8, tile % 8
                    if kind < 2:
                        at = ((within // 2) * groups + g) * BLOCK + (within % 2) * LANE
                        (up_ref, gate_ref)[kind][:, at : at + LANE] = block
                    else:
                        at = g * BLOCK + (within % 2) * LANE
                        col = (within // 2) * rows
                        down_ref[at : at + LANE, col : col + rows] = block.T

            copy_part(orders[g], own, part, refs[2 * g : 2 * g + 2], write)


def qkv_out_kernel(orders, info_ref, *refs):
    qkv_ref, out_ref, small_ref = refs[-3:]
    own = info_ref[4]
    half = qkv_ref.shape[0] // 2
    width = out_ref.shape[1]
    for h in range(2):
        for part in range(8):

            def write(value, h=h, part=part):
                y, c = part & 1, part >> 1
                rows = slice(y * half, (y + 1) * half)
                if c < 3:
                    at = c * width + h * PART
                    qkv_ref[rows, at : at + PART] = value[0:half]
                else:
                    out_ref[rows, h * PART : (h + 1) * PART] = value[0:half]
                if h == 0 and c == 0:
                    small_ref[y * 8 : y * 8 + 8] = value[half : half + 8]

            copy_part(orders[h], own, part, refs[2 * h : 2 * h + 2], write)


def input_back_kernel(rows_ref, gq0, gk0, gv0, gq1, gk1, gv1, sum_ref, *refs):
    pieces = refs[:4]
    out_ref, weight, sems = refs[-3:]
    width = sum_ref.shape[1]

    @pl.when(pl.program_id(0) == 0)
    def _():
        copies = piece_copies(lambda k: rows_ref[k], pieces, weight, sems)
        for copy in copies:
            copy.start()
        for copy in copies:
            copy.wait()

    total = sum_ref[...]
    for half, parts in enumerate(((gq0, gk0, gv0), (gq1, gk1, gv1))):
        for part, ref in enumerate(parts):
            at = part * width + half * PART
            total += dot(ref[...], weight[:, at : at + PART], 1, 1)
    out_ref[...] = total


def xor_permute(value, axis, size, bits):
    return lax.ppermute(value, axis, [(i, i ^ bits) for i in range(size)])


def drop_last(kernel, count, inputs, *refs):
    return kernel(*refs[:inputs], *refs[inputs + count :])


def gather_relative(value, axis, size):
    if size <= 8:
        return jnp.stack([value] + [xor_permute(value, axis, size, k) for k in range(1, size)])
    everyone = lax.all_gather(value, axis, axis=0)
    return jnp.take(everyone, jnp.arange(size) ^ lax.axis_index(axis), axis=0)


def absolute(stacked, own, bits):
    count = stacked.shape[0]
    for bit in range(bits):
        step = 1 << bit
        view = stacked.reshape((count // (2 * step), 2, step) + stacked.shape[1:])
        view = jnp.where((own >> bit) & 1 == 1, view[:, ::-1], view)
        stacked = view.reshape(stacked.shape)
    return stacked


def per_device(
    sizes,
    incoming_hidden_matrix,
    sequence_membership,
    matching_passages,
    softness_scale,
    combined_projection_matrix,
    mixer_projection_matrix,
    widening_matrix,
    gating_matrix,
    narrowing_matrix,
    mixer_scaling_factor,
    mixer_scaling_offset,
    perceptron_scaling_factor,
    perceptron_scaling_offset,
):
    nb, nf = sizes
    b, f = lax.axis_index("batch"), lax.axis_index("fsdp")
    x = incoming_hidden_matrix[0]
    segment = sequence_membership[0]
    T, D = x.shape
    FF = widening_matrix.shape[1]
    R = D // nf
    nblk = T // BLOCK
    y_bit = b & 1

    def tie(value, *others):
        return lax.optimization_barrier((value,) + others)[0]

    def halves_across(own):
        rows = own.shape[0]
        return xor_permute(lax.dynamic_slice_in_dim(own, y_bit * (rows // 2), rows // 2, 0), "fsdp", nf, 2)

    def gather_rest(own, mine, *others):
        mine = tie(mine, *others)
        other = xor_permute(mine, "batch", nb, 1)
        return (
            own,
            xor_permute(tie(own, *others), "fsdp", nf, 1),
            mine,
            other,
            xor_permute(mine, "fsdp", nf, 1),
            xor_permute(other, "fsdp", nf, 1),
        )

    def piece_rows(rows, share):
        half = rows // 2
        y = y_bit if share else 0 * y_bit
        two, three = (f ^ 2) * rows, (f ^ 3) * rows
        halves = [y * half, (1 - y) * half]
        starts = [f * rows, (f ^ 1) * rows, two + halves[0], two + halves[1], three + halves[0], three + halves[1]]
        down = [y * (FF // nf // 2), (1 - y) * (FF // nf // 2)]
        return jnp.stack(starts + [f] + down).astype(jnp.int32)

    rows = combined_projection_matrix.shape[0]
    beyond = xor_permute(combined_projection_matrix, "fsdp", nf, 2)
    beside = xor_permute(combined_projection_matrix, "fsdp", nf, 1)
    far = xor_permute(beyond, "fsdp", nf, 1)
    qkv_pieces = (combined_projection_matrix, beside, beyond, far)
    later = lax.optimization_barrier(
        (beyond, mixer_projection_matrix, widening_matrix, gating_matrix, narrowing_matrix)
    )[1:]
    up_half, out_half, gate_half, down_half = [halves_across(later[k]) for k in (1, 0, 2, 3)]
    vectors = jnp.stack(
        [mixer_scaling_factor, mixer_scaling_offset, perceptron_scaling_factor, perceptron_scaling_offset]
    )

    marks = (segment[:, None] == jnp.arange(SEGS, dtype=jnp.int32)[None, :]).astype(jnp.int32)
    counts = jnp.sum(marks, axis=0)
    ends = jnp.cumsum(counts)
    firsts = ends - counts
    start_of = jnp.sum(marks * firsts[None, :], axis=1)
    end_of = jnp.sum(marks * ends[None, :], axis=1)
    positions = jnp.arange(T, dtype=jnp.int32) - start_of
    inverse = 1000.0 ** (-(jnp.arange(HD // 2, dtype=f32) * 2.0) / HD)
    angles = positions.astype(f32)[:, None] * inverse[None, :]
    cosine, sine = jnp.cos(angles), jnp.sin(angles)
    cosine = jnp.concatenate([cosine] * 4, axis=1)
    sine = jnp.concatenate([-sine, sine, -sine, sine], axis=1)
    same = segment[:, None] == jnp.arange(LANE, dtype=jnp.int32)[None, :]
    mask_q = same.astype(bf16)
    mask_k = jnp.where(same | (jnp.arange(LANE)[None, :] >= SEGS), 0.0, NEG).astype(bf16)
    mark_rows = (jnp.arange(16, dtype=jnp.int32)[:, None] == segment[None, :]).astype(bf16)
    lo = (start_of.reshape(nblk, BLOCK)[:, 0] // LANE).astype(jnp.int32)
    hi = ((end_of.reshape(nblk, BLOCK)[:, -1] + LANE - 1) // LANE).astype(jnp.int32)
    spans = hi - lo
    count_rows = jnp.broadcast_to(counts.astype(f32)[:, None], (SEGS, LANE))

    def rowblk(width, rows=BLOCK):
        return pl.BlockSpec((rows, width), lambda i, *_: (i, 0))

    def colblk(height, cols=BLOCK):
        return pl.BlockSpec((height, cols), lambda i, *_: (0, i))

    whole_rows = jnp.stack([f * R, (f ^ 1) * R, (f ^ 2) * R, (f ^ 3) * R, f, f, f]).astype(jnp.int32)
    qkv, x_turned = pl.pallas_call(
        qkv_kernel,
        grid_spec=pltpu.PrefetchScalarGridSpec(
            num_scalar_prefetch=1,
            grid=(3,),
            in_specs=[whole((T, D)), whole((T, LANE)), whole((T, LANE))] + [ANY] * 4,
            out_specs=[pl.BlockSpec((T, D), lambda i, *_: (0, i)), whole((D, T))],
            scratch_shapes=[pltpu.VMEM((D, 3 * D), bf16), pltpu.SemaphoreType.DMA((4,))],
        ),
        out_shape=[shape((T, 3 * D), bf16), shape((D, T), bf16)],
        **params(),
    )(whole_rows, x, cosine, sine, *qkv_pieces)

    vectors = absolute(gather_relative(tie(vectors, qkv), "fsdp", nf), f, 2)
    vectors = vectors.transpose(1, 0, 2).reshape(4, D).astype(f32)

    def attend(h, *after):
        def keys(part):
            return pl.BlockSpec((T, PART), lambda i, *_: (0, 2 * part + h))

        return pl.pallas_call(
            functools.partial(drop_last, attend_kernel, len(after), 7),
            grid_spec=pltpu.PrefetchScalarGridSpec(
                num_scalar_prefetch=2,
                grid=(nblk,),
                in_specs=[
                    pl.BlockSpec((BLOCK, PART), lambda i, *_: (i, h)),
                    keys(1),
                    keys(2),
                    rowblk(LANE),
                    whole((T, LANE)),
                ]
                + [ANY] * len(after),
                out_specs=[rowblk(PART), pl.BlockSpec((PAIRS // 2, 8, BLOCK), lambda i, *_: (0, 0, i))],
            ),
            out_shape=[shape((T, PART), bf16), shape((PAIRS // 2, 8, T), f32)],
            **params(),
        )(lo, spans, qkv, qkv, qkv, mask_q, mask_k, *after)

    up_pieces = gather_rest(widening_matrix, up_half, qkv)
    attended0, lse0 = attend(0, up_pieces[2])
    out_pieces = gather_rest(mixer_projection_matrix, out_half, attended0)
    gate_pieces = gather_rest(gating_matrix, gate_half, attended0)
    attended1, lse1 = attend(1, gate_pieces[2], out_pieces[2])
    down_pieces = gather_rest(narrowing_matrix, down_half, attended1)

    shared_rows = piece_rows(R, True)
    xhat1, inv1, low1, low1_turned, full_out = pl.pallas_call(
        mixer_kernel,
        grid_spec=pltpu.PrefetchScalarGridSpec(
            num_scalar_prefetch=1,
            grid=(nblk,),
            in_specs=[rowblk(PART), rowblk(PART), rowblk(D), whole((4, D))] + [ANY] * 7,
            out_specs=[rowblk(D), rowblk(LANE), rowblk(D), colblk(D), ANY],
            scratch_shapes=[pltpu.VMEM((D, D), bf16), pltpu.SemaphoreType.DMA((6,)), pltpu.SemaphoreType.DMA],
        ),
        out_shape=[shape((T, D), f32), shape((T, LANE), f32), shape((T, D), bf16), shape((D, T), bf16), shape((D, D), bf16)],
        **params(),
    )(shared_rows, attended0, attended1, x, vectors, *out_pieces, down_pieces[2])

    W = FF // nf
    up_fac, gate_fac, prod, xhat2, inv2, pool, embed, full_up, full_gate, full_down = pl.pallas_call(
        ffn_kernel,
        grid_spec=pltpu.PrefetchScalarGridSpec(
            num_scalar_prefetch=1,
            grid=(nf,),
            in_specs=[whole((T, D)), whole((T, D)), whole((4, D)), whole((16, T)), whole((SEGS, LANE))] + [ANY] * 18,
            out_specs=[pl.BlockSpec((T, W), lambda i, rows: (0, rows[6] ^ i))] * 3
            + [whole((T, D)), whole((T, LANE)), whole((2 * SEGS, D)), whole((SEGS, D))]
            + [ANY] * 3,
            scratch_shapes=[
                pltpu.VMEM((nf, D, W), bf16),
                pltpu.VMEM((nf, D, W), bf16),
                pltpu.VMEM((nf, W, D), bf16),
                pltpu.SemaphoreType.DMA((nf * 12,)),
                pltpu.SemaphoreType.DMA((6,)),
                pltpu.SemaphoreType.DMA((nf * 3,)),
                pltpu.VMEM((16, D), f32),
                pltpu.VMEM((T, D), f32),
            ],
        ),
        out_shape=[shape((T, FF), bf16)] * 3
        + [shape((T, D), f32), shape((T, LANE), f32), shape((2 * SEGS, D), f32), shape((SEGS, D), bf16)]
        + [shape((D, FF), bf16), shape((D, FF), bf16), shape((FF, D), bf16)],
        **params(),
    )(shared_rows, low1, xhat1, vectors, mark_rows, count_rows, *up_pieces, *gate_pieces, *down_pieces)

    ranks = nb * nf
    total_rows = ranks * SEGS
    target = jnp.concatenate([matching_passages[0], jnp.zeros((SEGS - QSEG,), jnp.int32)])
    digits = jnp.pad(jnp.stack([target >> 5, target & 31], axis=1), ((0, 0), (0, LANE - 2))).astype(bf16)
    sent = jnp.concatenate([embed, digits], axis=1)
    everyone = gather_relative(sent, "fsdp", nf)
    if nb == 8:
        everyone = jnp.concatenate([everyone, xor_permute(everyone, "batch", nb, 1)])
        everyone = jnp.stack([everyone] + [xor_permute(everyone, "batch", nb, 2 * z) for z in range(1, 4)])
    else:
        everyone = gather_relative(everyone, "batch", nb)
    everyone = everyone.reshape(total_rows, D + LANE)
    rank_of = ((jnp.arange(nb)[:, None] ^ b) * nf + (jnp.arange(nf)[None, :] ^ f)).reshape(ranks, 1)
    place_of = jnp.arange(SEGS)[None, :]
    doc_ids = jnp.where(place_of >= QSEG, rank_of * (SEGS - QSEG) + place_of - QSEG, -1).reshape(1, total_rows)
    doc_ids = jnp.broadcast_to(doc_ids, (8, total_rows)).astype(f32)
    loss_rows, grad_rows, small_two = pl.pallas_call(
        loss_kernel,
        grid=(total_rows // BLOCK,),
        in_specs=[
            pl.BlockSpec(memory_space=pltpu.SMEM),
            rowblk(D + LANE),
            whole((total_rows, D + LANE)),
            whole((8, total_rows)),
            whole((2 * SEGS, D)),
            whole((SEGS, LANE)),
        ],
        out_specs=[whole((SEGS, LANE)), whole((LANE, D)), whole((8, D))],
        out_shape=[shape((SEGS, LANE), f32), shape((LANE, D), f32), shape((8, D), f32)],
        scratch_shapes=[pltpu.VMEM((SEGS, D), f32)],
        **params(),
    )(softness_scale.reshape(1), everyone, everyone, doc_ids, pool, count_rows)
    query_loss = loss_rows[:QSEG, 0].reshape(1, QSEG)

    sum_two, grad_low, grad_low_turned = pl.pallas_call(
        norm_two_back_kernel,
        grid=(nblk,),
        in_specs=[rowblk(LANE), whole((LANE, D)), rowblk(D), rowblk(LANE), whole((4, D))],
        out_specs=[rowblk(D), rowblk(D), colblk(D)],
        out_shape=[shape((T, D), f32), shape((T, D), bf16), shape((D, T), bf16)],
        **params(),
    )(mask_q, grad_rows, xhat2, inv2, vectors)

    def add(*terms):
        return sum([term.astype(f32) for term in terms]).astype(bf16)

    def across(value, axis):
        if axis == "x":
            return xor_permute(value, "fsdp", nf, 2)
        return xor_permute(value, "batch", nb, 1 << BIT[axis])

    class Reduce:
        def __init__(self, keep, send, *order):
            if nb != 8:
                order = ("x", "y", "z0", "z1")
            self.order, self.axes, self.stage = order, ["x", "y", "z1", "z0"], 0
            view = (2, 2, 2, 2) + keep.shape[-2:]
            self.terms = [keep.reshape(view), xor_permute(send, "fsdp", nf, 1).reshape(view)]

        def step(self, *after):
            self.stage += 1
            if nb != 8 and self.stage > 1:
                if self.stage == 2:
                    total = lax.psum(sum([term.astype(f32) for term in self.terms]), "batch").astype(bf16)
                    total = total.swapaxes(1, 2)
                    self.parts = [total[k].reshape((4,) + total.shape[-2:]) for k in range(2)]
                    self.out = self.parts[0]
                return
            self.terms[-1] = tie(self.terms[-1], *after)
            if self.stage <= 4:
                axis = self.order[self.stage - 1]
                at = self.axes.index(axis)
                self.axes.pop(at)
                self.out = add(*[lax.index_in_dim(term, 1, at, keepdims=False) for term in self.terms])
                self.terms = [lax.index_in_dim(term, 0, at, keepdims=False) for term in self.terms]
                self.terms.append(across(self.out, axis))
                return
            axis = [axis for axis in self.order if axis != "x"][7 - self.stage]
            if self.stage == 5:
                self.out = add(*self.terms)[None]
            else:
                self.out = jnp.concatenate(self.terms, axis=0)
            self.terms = [self.out, across(self.out, axis)]
            self.parts = self.terms

    own_part = b if nb == 8 else 0
    info = jnp.stack([f, f ^ 1, f ^ 2, f ^ 3, own_part + 0 * f]).astype(jnp.int32)
    groups = W // BLOCK

    def ffn_back(g, grad_hidden, *after):
        wide = nf * BLOCK
        parts = (2, 2, 4, R, PART)
        return pl.pallas_call(
            functools.partial(ffn_back_kernel, g, groups),
            grid_spec=pltpu.PrefetchScalarGridSpec(
                num_scalar_prefetch=1,
                grid=(1,),
                in_specs=[ANY] * (10 + len(after)),
                out_specs=[ANY] * 3,
                scratch_shapes=[pltpu.VMEM((T, wide), bf16)] * 3
                + [pltpu.VMEM((T, D), bf16), pltpu.VMEM((D, T), bf16), pltpu.VMEM((D, T), bf16)]
                + [pltpu.VMEM((D, wide), bf16)] * 2
                + [pltpu.VMEM((wide, D), bf16), pltpu.VMEM((T, D), f32)]
                + [pltpu.VMEM(parts, bf16)] * 2
                + [pltpu.VMEM((T, D), f32), pltpu.SemaphoreType.DMA((28,)), pltpu.SemaphoreType.DMA((3,))],
            ),
            out_shape=[shape((T, D), f32)] + [shape(parts, bf16)] * 2,
            **params(),
        )(
            info, prod, up_fac, gate_fac, grad_low, grad_low_turned, low1_turned, full_up, full_gate, full_down,
            grad_hidden, *after,
        )

    grad_hidden, keep, send = ffn_back(0, sum_two)
    r0 = Reduce(keep, send, "x", "z0", "y", "z1")
    grad_hidden, keep, send = ffn_back(1, grad_hidden)
    r1 = Reduce(keep, send, "y", "x", "z0", "z1")
    r0.step(grad_hidden)
    grad_hidden, keep, send = ffn_back(2, grad_hidden, r0.out)
    r2 = Reduce(keep, send, "x", "y", "z0", "z1")
    r1.step(grad_hidden)

    heads = (
        (jnp.arange(PAIRS * 8)[:, None] // 8 * 2 + jnp.arange(PAIRS * 8)[:, None] % 8 == jnp.arange(D)[None, :] // HD)
        & (jnp.arange(PAIRS * 8)[:, None] % 8 < 2)
    ).astype(bf16)
    sum_one, grad_branch, grad_att, delta, att_turned, small_one = pl.pallas_call(
        mixer_back_kernel,
        grid_spec=pltpu.PrefetchScalarGridSpec(
            num_scalar_prefetch=1,
            grid=(nblk,),
            in_specs=[
                rowblk(D),
                rowblk(D),
                rowblk(LANE),
                whole((4, D)),
                rowblk(PART),
                rowblk(PART),
                whole((D, D)),
                whole((PAIRS * 8, D)),
                ANY,
            ],
            out_specs=[
                rowblk(D),
                rowblk(D),
                rowblk(D),
                pl.BlockSpec((PAIRS, 8, BLOCK), lambda i, *_: (0, 0, i)),
                colblk(D),
                whole((8, D)),
            ],
        ),
        out_shape=[
            shape((T, D), f32),
            shape((T, D), bf16),
            shape((T, D), bf16),
            shape((PAIRS, 8, T), f32),
            shape((D, T), bf16),
            shape((8, D), f32),
        ],
        **params(),
    )(info, grad_hidden, xhat1, inv1, vectors, attended0, attended1, full_out, heads, r1.out)
    r2.step(grad_branch)
    r0.step(grad_branch)

    def attend_back(h, *after):
        def cols(part, rows=None):
            at = 2 * part + h
            return pl.BlockSpec((rows or T, PART), (lambda i, *_: (i, at)) if rows else (lambda i, *_: (0, at)))

        kernel = functools.partial(drop_last, attend_back_kernel, len(after), 14)
        return pl.pallas_call(
            kernel,
            grid_spec=pltpu.PrefetchScalarGridSpec(
                num_scalar_prefetch=2,
                grid=(nblk,),
                in_specs=[
                    cols(0),
                    cols(1, BLOCK),
                    cols(2, BLOCK),
                    cols(0),
                    whole((PAIRS // 2, 8, T)),
                    pl.BlockSpec((PAIRS // 2, 8, T), lambda i, *_: (h, 0, 0)),
                    whole((T, LANE)),
                    rowblk(LANE),
                    whole((T, LANE)),
                    whole((T, LANE)),
                    rowblk(LANE),
                    rowblk(LANE),
                ]
                + [ANY] * len(after),
                out_specs=[whole((T, PART)), rowblk(PART), rowblk(PART)],
                scratch_shapes=[pltpu.VMEM((PART, T), f32)],
            ),
            out_shape=[shape((T, PART), bf16)] * 3,
            **params(),
        )(lo, spans, qkv, qkv, qkv, grad_att, (lse0, lse1)[h], delta, mask_q, mask_k, cosine, sine, cosine, sine, *after)

    small = jnp.stack([small_one[0], small_one[1], small_two[0], small_two[1]]).reshape(4, nf, R)
    small = small.transpose(1, 0, 2).reshape(nf, 2, 1, 2 * R)
    small = jnp.pad(small, ((0, 0), (0, 0), (0, SMALL - 1), (0, 0)))

    def qkv_back(h, grads, extra, *after):
        dims = (2, 2, 4, R // 2 + extra, PART)
        parts = pl.BlockSpec(dims[:2] + (1,) + dims[3:], lambda c, info: (0, 0, c ^ (info[4] >> 1), 0, 0))
        return pl.pallas_call(
            functools.partial(qkv_back_kernel, extra),
            grid_spec=pltpu.PrefetchScalarGridSpec(
                num_scalar_prefetch=1,
                grid=(4,),
                in_specs=[whole((D, T)), whole((D, T))]
                + [whole((T, PART))] * 3
                + [pl.BlockSpec((T, PART), lambda c, *_: (0, h)), whole((nf, 2, SMALL, PART))]
                + [ANY] * len(after),
                out_specs=[parts, parts],
            ),
            out_shape=[shape(dims, bf16)] * 2,
            **params(),
        )(info, x_turned, att_turned, *grads, grad_branch, small, *after)

    grads0 = attend_back(0, r2.out, r0.out)
    r0.step(grads0[0])
    r1.step(grads0[0])
    keep, send = qkv_back(0, grads0, SMALL, r0.out, r1.out)
    r3 = Reduce(keep, send, "x", "z0", "y", "z1")
    r0.step(keep)
    r2.step(keep)
    grads1 = attend_back(1, r0.out, r2.out)
    r3.step(grads1[0])
    r0.step(grads1[0])
    r1.step(grads1[0])
    r2.step(grads1[0])
    keep, send = qkv_back(1, grads1, 0, r3.out, r0.out, r1.out, r2.out)
    r4 = Reduce(keep, send, "x", "y", "z0", "z1")
    r0.step(keep)
    r1.step(keep)
    r2.step(keep)
    r4.step(r0.out, r1.out, r2.out)

    grad_input = pl.pallas_call(
        input_back_kernel,
        grid_spec=pltpu.PrefetchScalarGridSpec(
            num_scalar_prefetch=1,
            grid=(nblk,),
            in_specs=[rowblk(PART)] * 6 + [rowblk(D)] + [ANY] * 5,
            out_specs=rowblk(D),
            scratch_shapes=[pltpu.VMEM((D, 3 * D), bf16), pltpu.SemaphoreType.DMA((4,))],
        ),
        out_shape=shape((T, D), f32),
        **params(),
    )(whole_rows, *grads0, *grads1, sum_one, *qkv_pieces, r4.out)

    def together(groups, *after):
        for group in groups:
            group.step(*after)
        return [group.out for group in groups]

    last = together([r3, r0, r1, r2], grad_input)
    last = together([r4, r3, r1, r2], *last)
    last = together([r4, r3, r1, r2], *last)
    last = together([r4, r3], *last)
    sum_up, sum_gate, sum_down = pl.pallas_call(
        functools.partial(ffn_out_kernel, (r0.order, r1.order, r2.order)),
        grid_spec=pltpu.PrefetchScalarGridSpec(
            num_scalar_prefetch=1,
            grid=(1,),
            in_specs=[whole((4, R, PART))] * (2 * groups),
            out_specs=[whole((R, FF)), whole((R, FF)), whole((W, D))],
        ),
        out_shape=[shape((R, FF), f32), shape((R, FF), f32), shape((W, D), f32)],
        **params(),
    )(info, *r0.parts, *r1.parts, *r2.parts)
    last = together([r4, r3], *last)
    last = together([r4, r3], sum_up, *last)
    last = together([r4], *last)
    sum_qkv, sum_out, sum_small = pl.pallas_call(
        functools.partial(qkv_out_kernel, (r3.order, r4.order)),
        grid_spec=pltpu.PrefetchScalarGridSpec(
            num_scalar_prefetch=1,
            grid=(1,),
            in_specs=[whole((4, R // 2 + SMALL, PART))] * 2 + [whole((4, R // 2, PART))] * 2,
            out_specs=[whole((R, 3 * D)), whole((R, D)), whole((16, PART))],
        ),
        out_shape=[shape((R, 3 * D), f32), shape((R, D), f32), shape((16, PART), f32)],
        **params(),
    )(info, *r3.parts, *r4.parts)
    return (
        query_loss,
        grad_input[None],
        sum_qkv,
        sum_out,
        sum_up,
        sum_gate,
        sum_down,
        sum_small[0, :R],
        sum_small[0, R : 2 * R],
        sum_small[8, :R],
        sum_small[8, R : 2 * R],
    )


def solution(mesh):
    sizes = (mesh.shape["batch"], mesh.shape["fsdp"])
    return jax.shard_map(
        functools.partial(per_device, sizes),
        mesh=mesh,
        in_specs=(
            P(("batch", "fsdp"), None, None),
            P(("batch", "fsdp"), None),
            P(("batch", "fsdp"), None),
            P(),
            P("fsdp", None),
            P("fsdp", None),
            P("fsdp", None),
            P("fsdp", None),
            P("fsdp", None),
            P("fsdp"),
            P("fsdp"),
            P("fsdp"),
            P("fsdp"),
        ),
        out_specs=(
            P(("batch", "fsdp"), None),
            P(("batch", "fsdp"), None, None),
            P("fsdp", None),
            P("fsdp", None),
            P("fsdp", None),
            P("fsdp", None),
            P("fsdp", None),
            P("fsdp"),
            P("fsdp"),
            P("fsdp"),
            P("fsdp"),
        ),
        check_vma=False,
    )
```

```python
import functools
import math

import jax
import jax.numpy as jnp
from jax import lax
from jax.experimental import pallas as pl
from jax.experimental.pallas import tpu as pltpu
from jax.sharding import PartitionSpec as P

HEADS = 12
HD = 64
QSEG = 4
SEGS = 8
EPSILON = 1e-06
NEG = -1e30
LANE = 128
BLOCK = 256
PAIRS = HEADS // 2
PART = 384
SMALL = 16
MIB = 2**20

bf16 = jnp.bfloat16
f32 = jnp.float32


def dot(left, right, left_dim, right_dim):
    return lax.dot_general(
        left, right, (((left_dim,), (right_dim,)), ((), ())), preferred_element_type=f32
    )


def split_three(value):
    high = value.astype(bf16)
    rest = value - high.astype(f32)
    middle = rest.astype(bf16)
    low = (rest - middle.astype(f32)).astype(bf16)
    return high, middle, low


def params(limit=60):
    return dict(
        compiler_params=pltpu.CompilerParams(vmem_limit_bytes=limit * MIB),
        cost_estimate=pl.CostEstimate(flops=1, bytes_accessed=1, transcendentals=0),
    )


def shape(dims, dtype):
    return jax.ShapeDtypeStruct(dims, dtype)


ANY = pl.BlockSpec(memory_space=pl.ANY)


def whole(dims):
    return pl.BlockSpec(dims, lambda *_: (0,) * len(dims))


def swap_halves(tile):
    lane = lax.broadcasted_iota(jnp.int32, (1, LANE), 1)
    in_first = (lane & 63) < 32
    return jnp.where(in_first, pltpu.roll(tile, 96, 1), pltpu.roll(tile, 32, 1))


def norm_parts(value):
    center = value - jnp.mean(value, axis=1, keepdims=True)
    spread = jnp.mean(center * center, axis=1, keepdims=True)
    inv = lax.rsqrt(spread + EPSILON)
    return center * inv, inv


def norm_back(scaled, xhat, inv):
    mean_one = jnp.mean(scaled, axis=1, keepdims=True)
    mean_two = jnp.mean(scaled * xhat, axis=1, keepdims=True)
    return inv * (scaled - mean_one - xhat * mean_two)


def piece_copies(row_of, pieces, scratch, sems):
    return [
        pltpu.make_async_copy(
            piece, scratch.at[pl.ds(pl.multiple_of(row_of(k), 32), piece.shape[0])], sems.at[k]
        )
        for k, piece in enumerate(pieces)
    ]


def store_turned(ref, value, own, columns=slice(None)):
    rows = ref.shape[0] // 4
    turned = value.T
    for shard in range(4):
        at = pl.ds(pl.multiple_of((shard ^ own) * rows, 64), rows)
        ref[at, columns] = turned[shard * rows : (shard + 1) * rows]


def qkv_kernel(rows_ref, x_ref, cos_ref, sin_ref, *refs):
    pieces = refs[:4]
    out_ref, xt_ref, weight, sems = refs[5:]
    step = pl.program_id(0)
    width = x_ref.shape[1]

    @pl.when(step == 0)
    def _():
        copies = piece_copies(lambda k: rows_ref[k], pieces, weight, sems)
        for copy in copies:
            copy.start()
        store_turned(xt_ref, x_ref[...], rows_ref[6])
        for copy in copies:
            copy.wait()

    joined = dot(x_ref[...], weight[:, pl.ds(pl.multiple_of(step * width, LANE), width)], 1, 0)

    @pl.when(step < 2)
    def _():
        scale = jnp.where(step == 0, 1.0 / math.sqrt(HD), 1.0)
        cos, sin = cos_ref[...] * scale, sin_ref[...] * scale
        for t in range(width // LANE):
            tile = joined[:, t * LANE : (t + 1) * LANE]
            out_ref[:, t * LANE : (t + 1) * LANE] = (tile * cos + swap_halves(tile) * sin).astype(bf16)

    @pl.when(step == 2)
    def _():
        out_ref[...] = joined.astype(bf16)


def key_range(first, count, total):
    blocks = (count + 1) >> 1
    first = jnp.minimum(first, total // LANE - 2 * blocks)
    return pl.multiple_of(first * LANE, LANE), blocks


def attend_kernel(lo_ref, n_ref, q_ref, k_ref, v_ref, mq_ref, mk_ref, o_ref, lse_ref):
    step = pl.program_id(0)
    lo, count = key_range(lo_ref[step], n_ref[step], k_ref.shape[0])
    first = lax.broadcasted_iota(jnp.int32, (1, LANE), 1) < HD
    zero = jnp.zeros((), bf16)
    mask_q = mq_ref[...]

    def run(width):
        keys = pl.ds(lo, width)
        mask_k = mk_ref[keys, :]

        def pair(p, _):
            cols = pl.ds(pl.multiple_of(p * LANE, LANE), LANE)
            q_pair, k_pair, v_pair = q_ref[:, cols], k_ref[keys, cols], v_ref[keys, cols]
            k_ext = jnp.concatenate([k_pair, mask_k], axis=1)
            outs, sums = [], []
            for h in range(2):
                q_one = jnp.where(first if h == 0 else ~first, q_pair, zero)
                scores = dot(jnp.concatenate([q_one, mask_q], axis=1), k_ext, 1, 1)
                peak = jnp.max(scores, axis=1, keepdims=True)
                weight = jnp.exp(scores - peak)
                total = jnp.sum(weight, axis=1, keepdims=True)
                outs.append(dot(weight.astype(bf16), v_pair, 1, 0) * (1.0 / total))
                sums.append(peak + jnp.log(total))
            o_ref[:, cols] = jnp.where(first, outs[0], outs[1]).astype(bf16)
            turned = jnp.where(first, sums[0], sums[1]).T
            lse_ref[p, 0:1, :] = turned[0:1]
            lse_ref[p, 1:2, :] = turned[HD : HD + 1]
            return 0

        lax.fori_loop(0, PAIRS // 2, pair, 0, unroll=True)

    for n in range(1, k_ref.shape[0] // BLOCK + 1):
        pl.when(count == n)(functools.partial(run, n * BLOCK))


def attend_back_kernel(
    lo_ref, n_ref, q_ref, k_ref, v_ref, do_ref, lse_ref, dl_ref, mq_ref, mk_ref, cos_ref, sin_ref, cosb_ref, sinb_ref,
    gq_ref, gk_ref, gv_ref, dq_acc,
):
    step = pl.program_id(0)

    @pl.when(step == 0)
    def _():
        dq_acc[...] = jnp.zeros_like(dq_acc)

    lo, count = key_range(lo_ref[step], n_ref[step], q_ref.shape[0])
    first = lax.broadcasted_iota(jnp.int32, (1, LANE), 1) < HD
    zero = jnp.zeros((), bf16)
    mask_k = mk_ref[...]
    cosb, sinb = cosb_ref[...], sinb_ref[...]

    def run(width):
        queries = pl.ds(lo, width)
        mask_q = mq_ref[queries, :]

        def pair(p, _):
            cols = pl.ds(pl.multiple_of(p * LANE, LANE), LANE)
            k_pair, v_pair = k_ref[:, cols], v_ref[:, cols]
            q_pair, do_pair = q_ref[queries, cols], do_ref[queries, cols]
            q_ext = jnp.concatenate([q_pair, mask_q], axis=1)
            k_turned = k_pair.T
            dk, dv = [], []
            for h in range(2):
                mine = first if h == 0 else ~first
                k_one, v_one = jnp.where(mine, k_pair, zero), jnp.where(mine, v_pair, zero)
                scores = dot(jnp.concatenate([k_one, mask_k], axis=1), q_ext, 1, 1)
                probs = jnp.exp(scores - lse_ref[p, h : h + 1, queries])
                dprobs = dot(v_one, do_pair, 1, 1)
                dscores = (probs * (dprobs - dl_ref[p, h : h + 1, queries])).astype(bf16)
                dv.append(dot(probs.astype(bf16), do_pair, 1, 0))
                dk.append(dot(dscores, q_pair, 1, 0))
                rows = pl.ds(pl.multiple_of(p * LANE + h * HD, HD), HD)
                dq_acc[rows, queries] += dot(k_turned[h * HD : (h + 1) * HD], dscores, 1, 0)
            gv_ref[:, cols] = jnp.where(first, dv[0], dv[1]).astype(bf16)
            grad = jnp.where(first, dk[0], dk[1])
            gk_ref[:, cols] = (grad * cosb - swap_halves(grad) * sinb).astype(bf16)
            return 0

        lax.fori_loop(0, PAIRS // 2, pair, 0, unroll=True)

    for n in range(1, q_ref.shape[0] // BLOCK + 1):
        pl.when(count == n)(functools.partial(run, n * BLOCK))

    @pl.when(step == pl.num_programs(0) - 1)
    def _():
        cos, sin = cos_ref[...], sin_ref[...]
        for p in range(PAIRS // 2):
            grad = dq_acc[p * LANE : (p + 1) * LANE, :].T * (1.0 / math.sqrt(HD))
            gq_ref[:, p * LANE : (p + 1) * LANE] = (grad * cos - swap_halves(grad) * sin).astype(bf16)


def mixer_kernel(rows_ref, att0_ref, att1_ref, x_ref, vec_ref, *refs):
    xhat_ref, inv_ref, low_ref, lowt_ref, full_ref, weight, sems, out_sem = refs[8:]
    width = weight.shape[1]
    pieces = list(refs[:2]) + [piece.at[:, pl.ds(piece.shape[1] - width, width)] for piece in refs[2:6]]
    step = pl.program_id(0)
    out_copy = pltpu.make_async_copy(weight, full_ref, out_sem)

    @pl.when(step == 0)
    def _():
        copies = piece_copies(lambda k: rows_ref[k], pieces, weight, sems)
        for copy in copies:
            copy.start()
        for copy in copies:
            copy.wait()
        out_copy.start()

    branch = dot(att0_ref[...], weight[0:PART, :], 1, 0) + dot(att1_ref[...], weight[PART:, :], 1, 0)
    xhat, inv = norm_parts(x_ref[...].astype(f32) + branch)
    low = (xhat * vec_ref[0:1] + vec_ref[1:2]).astype(bf16)
    xhat_ref[...] = xhat
    inv_ref[...] = jnp.broadcast_to(inv, inv_ref.shape)
    low_ref[...] = low
    store_turned(lowt_ref, low, rows_ref[6])

    @pl.when(step == pl.num_programs(0) - 1)
    def _():
        out_copy.wait()


def ffn_kernel(rows_ref, low_ref, xhat_ref, vec_ref, mark_ref, cnt_ref, *refs):
    up_pieces, gate_pieces, down_pieces = refs[0:6], refs[6:12], refs[12:18]
    up_fac_ref, gate_fac_ref, prod_ref, xhat2_ref, inv2_ref, pool_ref, emb_ref = refs[18:25]
    full_up, full_gate, full_down = refs[25:28]
    w_up, w_gate, w_down, sems, down_sems, out_sems, pooled, total = refs[28:]
    step = pl.program_id(0)
    own = rows_ref[6]
    tokens, width = low_ref.shape
    wide = prod_ref.shape[1]
    steps = 4

    def in_copies(rel):
        cols = pl.ds(pl.multiple_of((own ^ rel) * wide, LANE), wide)
        copies = []
        for which, (pieces, scratch) in enumerate(((up_pieces, w_up), (gate_pieces, w_gate))):
            for k, piece in enumerate(pieces):
                rows = pl.ds(pl.multiple_of(rows_ref[k], 32), piece.shape[0])
                copies.append(
                    pltpu.make_async_copy(piece.at[:, cols], scratch.at[rel, rows], sems.at[rel * 12 + which * 6 + k])
                )
        for k in ((0,), (1,), (2, 3), (4, 5))[rel]:
            piece = down_pieces[k]
            start = 0 if k < 2 else pl.multiple_of(rows_ref[7 + (k & 1)], 32)
            copies.append(
                pltpu.make_async_copy(piece, w_down.at[rel, pl.ds(start, piece.shape[0])], down_sems.at[k])
            )
        return copies

    def out_copies(rel):
        cols = pl.ds(pl.multiple_of((own ^ rel) * wide, LANE), wide)
        return [
            pltpu.make_async_copy(w_up.at[rel], full_up.at[:, cols], out_sems.at[rel * 3]),
            pltpu.make_async_copy(w_gate.at[rel], full_gate.at[:, cols], out_sems.at[rel * 3 + 1]),
            pltpu.make_async_copy(w_down.at[rel], full_down.at[cols], out_sems.at[rel * 3 + 2]),
        ]

    @pl.when(step == 0)
    def _():
        for rel in range(2):
            for copy in in_copies(rel):
                copy.start()
        pooled[...] = jnp.zeros_like(pooled)

    for rel in range(steps):

        @pl.when(step == rel)
        def _(rel=rel):
            for copy in in_copies(rel):
                copy.wait()
            for copy in out_copies(rel):
                copy.start()
            if 0 < rel < steps - 1:
                for copy in in_copies(rel + 1):
                    copy.start()

    rows_at = 512

    def rows_block(i, _):
        rows = pl.ds(pl.multiple_of(i * rows_at, rows_at), rows_at)
        low = low_ref[rows, :]
        up = dot(low, w_up[step], 1, 0)
        gate = dot(low, w_gate[step], 1, 0)
        sig = 0.5 * jnp.tanh(0.5 * gate) + 0.5
        act = gate * sig
        up_fac_ref[rows, :] = act.astype(bf16)
        gate_fac_ref[rows, :] = (up * (sig + act * (1.0 - sig))).astype(bf16)
        prod = (act * up).astype(bf16)
        prod_ref[rows, :] = prod
        ffn = dot(prod, w_down[step], 1, 0)

        total[rows, :] = jnp.where(step == 0, ffn, total[rows, :] + ffn)
        return 0

    lax.fori_loop(0, tokens // rows_at, rows_block, 0, unroll=True)

    @pl.when(step == steps - 1)
    def _():
        def norm_block(i, _):
            rows = pl.ds(pl.multiple_of(i * BLOCK, BLOCK), BLOCK)
            xhat, inv = norm_parts(xhat_ref[rows, :] * vec_ref[0:1] + vec_ref[1:2] + total[rows, :])
            xhat2_ref[rows, :] = xhat
            inv2_ref[rows, :] = jnp.broadcast_to(inv, (BLOCK, LANE))
            marks = mark_ref[:, rows]
            part = jnp.zeros(pooled.shape, f32)
            for piece in split_three(xhat):
                part += dot(marks, piece, 1, 0)
            pooled[...] += part
            return 0

        lax.fori_loop(0, tokens // BLOCK, norm_block, 0)
        mean_xhat = pooled[0:SEGS] / cnt_ref[:, 0:1]
        pool = mean_xhat * vec_ref[2:3] + vec_ref[3:4]
        inv_len = lax.rsqrt(jnp.sum(pool * pool, axis=1, keepdims=True) + EPSILON)
        pool_ref[0:SEGS] = mean_xhat
        pool_ref[SEGS:] = pool
        emb_ref[...] = (pool * inv_len).astype(bf16)
        for rel in range(steps):
            for copy in out_copies(rel):
                copy.wait()


def loss_kernel(soft_ref, blk_ref, all_ref, ids_ref, pool_ref, cnt_ref, loss_ref, rows_ref, small_ref, acc):
    step = pl.program_id(0)
    soft = soft_ref[0]
    width = acc.shape[1]
    block, everyone = blk_ref[:, 0:width], all_ref[:, 0:width]
    target = blk_ref[:, width : width + LANE].astype(f32)
    target = target[:, 0:1] * 32.0 + target[:, 1:2]
    row = lax.broadcasted_iota(jnp.int32, (block.shape[0], 1), 0)
    asks = (row & (SEGS - 1)) < QSEG
    ids = ids_ref[0:1, :]
    logits = jnp.where(ids >= 0, dot(block, everyone, 1, 1) / soft, NEG)
    hit = asks & (target == ids)
    peak = jnp.max(logits, axis=1, keepdims=True)
    lse = peak + jnp.log(jnp.sum(jnp.exp(logits - peak), axis=1, keepdims=True))
    grad = (jnp.exp(logits - lse) - jnp.where(hit, 1.0, 0.0)) / soft
    grad = jnp.where(asks, grad, 0.0)
    turned = grad[:, 0:LANE].T[0:SEGS]
    part = jnp.zeros(acc.shape, f32)
    for piece in split_three(turned):
        part += dot(piece, block, 1, 0)

    @pl.when(step == 0)
    def _():
        own = part
        for piece in split_three(grad[0:SEGS]):
            own += dot(piece, everyone, 1, 0)
        acc[...] = own
        chosen = jnp.sum(jnp.where(hit, logits, 0.0), axis=1, keepdims=True)
        loss_ref[...] = jnp.broadcast_to((lse - chosen)[0:SEGS], loss_ref.shape)

    @pl.when(step > 0)
    def _():
        acc[...] += part

    @pl.when(step == pl.num_programs(0) - 1)
    def _():
        g = acc[...]
        mean_xhat, pool = pool_ref[0:SEGS], pool_ref[SEGS:]
        inv_len = lax.rsqrt(jnp.sum(pool * pool, axis=1, keepdims=True) + EPSILON)
        back = inv_len * g - inv_len * inv_len * inv_len * pool * jnp.sum(pool * g, axis=1, keepdims=True)
        rows_ref[...] = jnp.zeros_like(rows_ref)
        rows_ref[0:SEGS] = back / cnt_ref[:, 0:1]
        small_ref[...] = jnp.zeros_like(small_ref)
        small_ref[0:1] = jnp.sum(back * mean_xhat, axis=0, keepdims=True)
        small_ref[1:2] = jnp.sum(back, axis=0, keepdims=True)


def norm_two_back_kernel(mq_ref, rows_ref, xhat_ref, inv_ref, vec_ref, sum_ref, low_ref, lowt_ref):
    marks = mq_ref[...]
    scaled = jnp.zeros(xhat_ref.shape, f32)
    for piece in split_three(rows_ref[...] * vec_ref[2:3]):
        scaled += dot(marks, piece, 1, 0)
    grad = norm_back(scaled, xhat_ref[...], inv_ref[:, 0:1])
    sum_ref[...] = grad
    low = grad.astype(bf16)
    low_ref[...] = low
    lowt_ref[...] = low.T


BIT = dict(y=0, z0=1, z1=2)


def part_index(order, x, away):
    at = 0
    for axis in order:
        if axis == "z":
            at = at * 4 + (away >> 1)
        else:
            at = at * 2 + (x if axis == "x" else (away >> BIT[axis]) & 1)
    return at


def strips(source, to, sems, first, groups, g, shards, by_rows=False):
    copies = []
    for k, shard in enumerate(shards):
        at = (shard * groups + g) * BLOCK
        here = pl.ds(at if isinstance(at, int) else pl.multiple_of(at, BLOCK), BLOCK)
        there = pl.ds(k * BLOCK, BLOCK)
        if by_rows:
            copies.append(pltpu.make_async_copy(source.at[here], to.at[there], sems.at[first + k]))
        else:
            copies.append(pltpu.make_async_copy(source.at[:, here], to.at[:, there], sems.at[first + k]))
    return copies


def ffn_back_kernel(
    g, order, groups, info_ref, prod_any, up_fac_any, gate_fac_any, low_any, lowt_any, hidt_any, wd_any, *refs
):
    dup_any, dgate_any, keep_any, send_any = refs[-16:-12]
    prod, up_fac, gate_fac, low, lowt, hidt, wd, dups, keep, send, sems, out_sems = refs[-12:]
    own = info_ref[4]
    rows = keep.shape[1]
    targets = [(keep, 0), (send, 0), (keep, 1), (send, 1)]

    def one(source, to, first):
        return [pltpu.make_async_copy(source, to, sems.at[first])]

    plain = range(4)
    loads = dict(
        low=one(low_any, low, 0),
        wd=strips(wd_any, wd, sems, 4, groups, g, plain, by_rows=True),
        up_fac=strips(up_fac_any, up_fac, sems, 8, groups, g, plain),
        hidt=one(hidt_any, hidt, 1),
        gate_fac=strips(gate_fac_any, gate_fac, sems, 12, groups, g, plain),
        lowt=one(lowt_any, lowt, 2),
        prod=strips(prod_any, prod, sems, 16, groups, g, [info_ref[k] for k in range(4)]),
    )
    for copies in loads.values():
        for copy in copies:
            copy.start()

    def arrive(*names):
        for name in names:
            for copy in loads[name]:
                copy.wait()

    def store(rel, tile, value):
        ref, across = targets[rel]
        at = part_index(order, across, (tile // 3) ^ own)
        ref[at, :, tile % 3 * LANE : (tile % 3 + 1) * LANE] = value.astype(bf16)

    def store_columns(kind, value):
        for rel in range(4):
            for t in range(8):
                store(rel, kind * 8 + t, value[rel * rows : (rel + 1) * rows, t * LANE : (t + 1) * LANE])

    outs = [
        pltpu.make_async_copy(dups.at[0], dup_any, out_sems.at[0]),
        pltpu.make_async_copy(dups.at[1], dgate_any, out_sems.at[1]),
        pltpu.make_async_copy(send, send_any, out_sems.at[2]),
        pltpu.make_async_copy(keep, keep_any, out_sems.at[3]),
    ]
    arrive("low", "wd", "up_fac")
    dprod = dot(low[...], wd[...], 1, 1)
    dups[0] = (dprod * up_fac[...].astype(f32)).astype(bf16)
    arrive("gate_fac")
    dups[1] = (dprod * gate_fac[...].astype(f32)).astype(bf16)
    outs[0].start()
    outs[1].start()
    arrive("hidt")
    store_columns(0, dot(hidt[...], dups[0], 1, 0))
    store_columns(1, dot(hidt[...], dups[1], 1, 0))
    arrive("lowt", "prod")
    down = dot(lowt[...], prod[...], 1, 0)
    for rel in range(4):
        for k in range(4):
            for t in range(2):
                at = rel * BLOCK + t * LANE
                store(rel, 16 + 2 * k + t, down[k * rows : (k + 1) * rows, at : at + LANE])
    outs[2].start()
    outs[3].start()
    for copy in outs:
        copy.wait()


def ffn_input_back_kernel(groups, wu_any, wg_any, hid_any, *refs):
    dups = refs[: 2 * groups]
    out_any = refs[-7]
    dup, wu, wg, total, sems, out_sem = refs[-6:]
    plain = range(4)

    def loads(g):
        copies = [
            pltpu.make_async_copy(dups[2 * g + which], dup.at[2 * g + which], sems.at[g * 10 + which])
            for which in range(2)
        ]
        copies += strips(wu_any, wu.at[g], sems, g * 10 + 2, groups, g, plain)
        copies += strips(wg_any, wg.at[g], sems, g * 10 + 6, groups, g, plain)
        return copies

    base = pltpu.make_async_copy(hid_any, total, sems.at[groups * 10])
    for g in range(groups):
        for copy in loads(g):
            copy.start()
        if g == 0:
            base.start()

    def work(g, _):
        for k in range(groups):

            @pl.when(g == k)
            def _(k=k):
                for copy in loads(k):
                    copy.wait()
                if k == 0:
                    base.wait()

        total[...] += dot(dup[2 * g], wu[g], 1, 1) + dot(dup[2 * g + 1], wg[g], 1, 1)
        return 0

    lax.fori_loop(0, groups, work, 0)
    out = pltpu.make_async_copy(total, out_any, out_sem)
    out.start()
    out.wait()


def mixer_back_kernel(info_ref, grad_ref, xhat_ref, inv_ref, vec_ref, att0_ref, att1_ref, w_ref, heads_ref, two_ref, *refs):
    sum_ref, low_ref, datt_ref, dl_ref, attt_ref, small_ref, sums = refs[-7:]
    step = pl.program_id(0)
    grad, xhat = grad_ref[...], xhat_ref[...]
    out = norm_back(grad * vec_ref[0:1], xhat, inv_ref[:, 0:1])
    sum_ref[...] = out
    low = out.astype(bf16)
    low_ref[...] = low
    datt = dot(low, w_ref[...], 1, 1).astype(bf16)
    datt_ref[...] = datt
    att = jnp.concatenate([att0_ref[...], att1_ref[...]], axis=1)
    store_turned(attt_ref, att, info_ref[0])
    inner = datt.astype(f32) * att.astype(f32)
    heads = heads_ref[...]
    rows = jnp.zeros((heads.shape[0], inner.shape[0]), f32)
    for piece in split_three(inner)[:2]:
        rows += dot(heads, piece, 1, 1)
    for p in range(PAIRS):
        dl_ref[p] = rows[p * 8 : (p + 1) * 8]

    @pl.when(step == 0)
    def _():
        small_ref[...] = jnp.zeros_like(small_ref)
        sums[...] = jnp.zeros_like(sums)

    sums[0:1] += jnp.sum(grad * xhat, axis=0, keepdims=True)
    sums[1:2] += jnp.sum(grad, axis=0, keepdims=True)

    @pl.when(step == pl.num_programs(0) - 1)
    def _():
        width = sums.shape[1] // 4
        for y, ref in enumerate((sums, two_ref)):
            for shard in range(4):
                cols = slice(shard * width, (shard + 1) * width)
                small_ref[shard, y, 0:1, 0:width] = ref[0:1, cols]
                small_ref[shard, y, 0:1, width : 2 * width] = ref[1:2, cols]


def qkv_back_kernel(extra, order, info_ref, xt_ref, attt_ref, gq_ref, gk_ref, gv_ref, gb_ref, small_ref, *refs):
    keep_ref, send_ref = refs[-2:]
    step = pl.program_id(0)
    half = keep_ref.shape[1] - extra
    own = info_ref[4]
    targets = [(keep_ref, 0), (send_ref, 0), (keep_ref, 1), (send_ref, 1)]

    def run(left_ref, right_ref):
        value = dot(left_ref[...], right_ref[...], 1, 0).astype(bf16)
        for rel, (ref, across) in enumerate(targets):
            for y in range(2):
                at = (2 * rel + y) * half
                to = part_index(order, across, (2 * step + y) ^ own)
                ref[to, 0:half, :] = value[at : at + half]
                if extra:
                    ref[to, half:, :] = small_ref[info_ref[rel], y].astype(bf16)

    for which, right_ref in enumerate((gq_ref, gk_ref, gv_ref, gb_ref)):
        pl.when(step == which)(functools.partial(run, xt_ref if which < 3 else attt_ref, right_ref))


def copy_part(order, own, part, pair, write):
    away = part ^ own
    one, *rest = [axis for axis in order if axis != "x"]
    at = part_index(rest, 0, away)
    for which in range(2):

        @pl.when((away >> BIT[one]) & 1 == which)
        def _(which=which):
            write(pair[which][at].astype(f32))


def ffn_out_kernel(orders, info_ref, *refs):
    groups = (len(refs) - 3) // 2
    up_ref, gate_ref, down_ref = refs[-3:]
    own = info_ref[4]
    rows = up_ref.shape[0]
    for g in range(groups):
        for part in range(8):

            def write(value, g=g, part=part):
                for t in range(3):
                    tile = part * 3 + t
                    block = value[:, t * LANE : (t + 1) * LANE]
                    kind, within = tile // 8, tile % 8
                    if kind < 2:
                        at = ((within // 2) * groups + g) * BLOCK + (within % 2) * LANE
                        (up_ref, gate_ref)[kind][:, at : at + LANE] = block
                    else:
                        at = g * BLOCK + (within % 2) * LANE
                        col = (within // 2) * rows
                        down_ref[at : at + LANE, col : col + rows] = block.T

            copy_part(orders[g], own, part, refs[2 * g : 2 * g + 2], write)


def qkv_out_kernel(orders, info_ref, *refs):
    qkv_ref, out_ref, small_ref = refs[-3:]
    own = info_ref[4]
    half = qkv_ref.shape[0] // 2
    width = out_ref.shape[1]
    for h in range(2):
        for part in range(8):

            def write(value, h=h, part=part):
                y, c = part & 1, part >> 1
                rows = slice(y * half, (y + 1) * half)
                if c < 3:
                    at = c * width + h * PART
                    qkv_ref[rows, at : at + PART] = value[0:half]
                else:
                    out_ref[rows, h * PART : (h + 1) * PART] = value[0:half]
                if h == 0 and c == 0:
                    small_ref[y * 8 : y * 8 + 8] = value[half : half + 8]

            copy_part(orders[h], own, part, refs[2 * h : 2 * h + 2], write)


def input_back_kernel(rows_ref, gq0, gk0, gv0, gq1, gk1, gv1, sum_ref, *refs):
    pieces = refs[:4]
    out_ref, weight, sems = refs[-3:]
    width = sum_ref.shape[1]

    @pl.when(pl.program_id(0) == 0)
    def _():
        copies = piece_copies(lambda k: rows_ref[k], pieces, weight, sems)
        for copy in copies:
            copy.start()
        for copy in copies:
            copy.wait()

    total = sum_ref[...]
    for half, parts in enumerate(((gq0, gk0, gv0), (gq1, gk1, gv1))):
        for part, ref in enumerate(parts):
            at = part * width + half * PART
            total += dot(ref[...], weight[:, at : at + PART], 1, 1)
    out_ref[...] = total


def xor_permute(value, axis, size, bits):
    return lax.ppermute(value, axis, [(i, i ^ bits) for i in range(size)])


def sums_kernel(plan, *refs):
    outs = refs[len(refs) - len(plan) :]
    for out_ref, pieces in zip(outs, plan, strict=True):
        for offset, terms in pieces:
            total = refs[terms[0]][...].astype(f32)
            for term in terms[1:]:
                total += refs[term][...].astype(f32)
            out_ref[offset : offset + total.shape[0]] = total.astype(bf16)


def sums_of(wanted, after):
    inputs, specs, plan, shapes = [], [], [], []
    for pieces in wanted:
        offset, steps = 0, []
        for terms in pieces:
            indices = []
            for array, first, count in terms:
                indices.append(len(inputs))
                inputs.append(array)
                at = first // count
                specs.append(pl.BlockSpec((count,) + array.shape[1:], lambda i, at=at: (at, 0, 0)))
            steps.append((offset, indices))
            offset += terms[0][2]
        plan.append(steps)
        shapes.append((offset,) + pieces[0][0][0].shape[1:])
    return pl.pallas_call(
        functools.partial(drop_last, functools.partial(sums_kernel, plan), len(after), len(inputs)),
        grid=(1,),
        in_specs=specs + [ANY] * len(after),
        out_specs=[pl.BlockSpec(dims, lambda i: (0, 0, 0)) for dims in shapes],
        out_shape=[shape(dims, bf16) for dims in shapes],
        **params(),
    )(*inputs, *after)


def drop_last(kernel, count, inputs, *refs):
    return kernel(*refs[:inputs], *refs[inputs + count :])


def gather_relative(value, axis, size):
    if size <= 8:
        return jnp.stack([value] + [xor_permute(value, axis, size, k) for k in range(1, size)])
    everyone = lax.all_gather(value, axis, axis=0)
    return jnp.take(everyone, jnp.arange(size) ^ lax.axis_index(axis), axis=0)


def absolute(stacked, own, bits):
    count = stacked.shape[0]
    for bit in range(bits):
        step = 1 << bit
        view = stacked.reshape((count // (2 * step), 2, step) + stacked.shape[1:])
        view = jnp.where((own >> bit) & 1 == 1, view[:, ::-1], view)
        stacked = view.reshape(stacked.shape)
    return stacked


def per_device(
    sizes,
    incoming_hidden_matrix,
    sequence_membership,
    matching_passages,
    softness_scale,
    combined_projection_matrix,
    mixer_projection_matrix,
    widening_matrix,
    gating_matrix,
    narrowing_matrix,
    mixer_scaling_factor,
    mixer_scaling_offset,
    perceptron_scaling_factor,
    perceptron_scaling_offset,
):
    nb, nf = sizes
    b, f = lax.axis_index("batch"), lax.axis_index("fsdp")
    x = incoming_hidden_matrix[0]
    segment = sequence_membership[0]
    T, D = x.shape
    FF = widening_matrix.shape[1]
    R = D // nf
    nblk = T // BLOCK
    y_bit = b & 1

    def tie(value, *others):
        return lax.optimization_barrier((value,) + others)[0]

    def own_half(own):
        rows = own.shape[0]
        return lax.dynamic_slice_in_dim(own, y_bit * (rows // 2), rows // 2, 0)

    def gather_rest(own, mine, before):
        mine = tie(mine, before)
        other = xor_permute(mine, "batch", nb, 1)
        return (
            own,
            xor_permute(tie(own, before), "fsdp", nf, 1),
            mine,
            other,
            xor_permute(mine, "fsdp", nf, 1),
        )

    def gather_last(pieces, during):
        return pieces + (xor_permute(tie(pieces[3], during), "fsdp", nf, 1),)

    def piece_rows(rows, share):
        half = rows // 2
        y = y_bit if share else 0 * y_bit
        two, three = (f ^ 2) * rows, (f ^ 3) * rows
        halves = [y * half, (1 - y) * half]
        starts = [f * rows, (f ^ 1) * rows, two + halves[0], two + halves[1], three + halves[0], three + halves[1]]
        down = [y * (FF // nf // 2), (1 - y) * (FF // nf // 2)]
        return jnp.stack(starts + [f] + down).astype(jnp.int32)

    marks = (segment[:, None] == jnp.arange(SEGS, dtype=jnp.int32)[None, :]).astype(jnp.int32)
    counts = jnp.sum(marks, axis=0)
    ends = jnp.cumsum(counts)
    firsts = ends - counts
    start_of = jnp.sum(marks * firsts[None, :], axis=1)
    end_of = jnp.sum(marks * ends[None, :], axis=1)
    positions = jnp.arange(T, dtype=jnp.int32) - start_of
    lane = jnp.arange(LANE)
    inverse = 1000.0 ** (-((lane % (HD // 2)).astype(f32) * 2.0) / HD)
    angles = positions.astype(f32)[:, None] * inverse[None, :]
    cosine, sine = jnp.cos(angles), jnp.where((lane % HD < HD // 2)[None, :], -1.0, 1.0) * jnp.sin(angles)
    same = segment[:, None] == jnp.arange(LANE, dtype=jnp.int32)[None, :]
    mask_q = same.astype(bf16)
    mask_k = jnp.where(same | (jnp.arange(LANE)[None, :] >= SEGS), 0.0, NEG).astype(bf16)
    mark_rows = (jnp.arange(16, dtype=jnp.int32)[:, None] == segment[None, :]).astype(bf16)
    lo = (start_of.reshape(nblk, BLOCK)[:, 0] // LANE).astype(jnp.int32)
    hi = ((end_of.reshape(nblk, BLOCK)[:, -1] + LANE - 1) // LANE).astype(jnp.int32)
    spans = hi - lo
    rows = combined_projection_matrix.shape[0]
    beyond = xor_permute(combined_projection_matrix, "fsdp", nf, 2)
    beside = xor_permute(combined_projection_matrix, "fsdp", nf, 1)
    both = jnp.concatenate([own_half(widening_matrix), own_half(mixer_projection_matrix)], axis=1)
    halves = [both, own_half(gating_matrix), own_half(narrowing_matrix)]
    vectors = jnp.stack(
        [mixer_scaling_factor, mixer_scaling_offset, perceptron_scaling_factor, perceptron_scaling_offset]
    )
    vectors = gather_relative(vectors, "fsdp", nf)
    beyond = tie(beyond, mask_q, mask_k, cosine, vectors, *halves)
    far = xor_permute(beyond, "fsdp", nf, 1)
    qkv_pieces = (combined_projection_matrix, beside, beyond, far)
    up_half, gate_half, down_half = [
        xor_permute(tie(half, cosine, mask_q, mask_k), "fsdp", nf, 2) for half in halves
    ]

    heads = (
        (jnp.arange(PAIRS * 8)[:, None] // 8 * 2 + jnp.arange(PAIRS * 8)[:, None] % 8 == jnp.arange(D)[None, :] // HD)
        & (jnp.arange(PAIRS * 8)[:, None] % 8 < 2)
    ).astype(bf16)
    count_rows = jnp.broadcast_to(counts.astype(f32)[:, None], (SEGS, LANE))

    def rowblk(width, rows=BLOCK):
        return pl.BlockSpec((rows, width), lambda i, *_: (i, 0))

    def colblk(height, cols=BLOCK):
        return pl.BlockSpec((height, cols), lambda i, *_: (0, i))

    whole_rows = jnp.stack([f * R, (f ^ 1) * R, (f ^ 2) * R, (f ^ 3) * R, f, f, f]).astype(jnp.int32)
    qkv, x_turned = pl.pallas_call(
        qkv_kernel,
        grid_spec=pltpu.PrefetchScalarGridSpec(
            num_scalar_prefetch=1,
            grid=(3,),
            in_specs=[whole((T, D)), whole((T, LANE)), whole((T, LANE))] + [ANY] * 5,
            out_specs=[pl.BlockSpec((T, D), lambda i, *_: (0, i)), whole((D, T))],
            scratch_shapes=[pltpu.VMEM((D, 3 * D), bf16), pltpu.SemaphoreType.DMA((4,))],
        ),
        out_shape=[shape((T, 3 * D), bf16), shape((D, T), bf16)],
        **params(),
    )(whole_rows, x, cosine, sine, *qkv_pieces, vectors)

    vectors = absolute(vectors, f, 2)
    vectors = vectors.transpose(1, 0, 2).reshape(4, D).astype(f32)

    def attend(h, *after):
        def keys(part):
            return pl.BlockSpec((T, PART), lambda i, *_: (0, 2 * part + h))

        return pl.pallas_call(
            functools.partial(drop_last, attend_kernel, len(after), 7),
            grid_spec=pltpu.PrefetchScalarGridSpec(
                num_scalar_prefetch=2,
                grid=(nblk,),
                in_specs=[
                    pl.BlockSpec((BLOCK, PART), lambda i, *_: (i, h)),
                    keys(1),
                    keys(2),
                    rowblk(LANE),
                    whole((T, LANE)),
                ]
                + [ANY] * len(after),
                out_specs=[rowblk(PART), pl.BlockSpec((PAIRS // 2, 8, BLOCK), lambda i, *_: (0, 0, i))],
            ),
            out_shape=[shape((T, PART), bf16), shape((PAIRS // 2, 8, T), f32)],
            **params(),
        )(lo, spans, qkv, qkv, qkv, mask_q, mask_k, *after)

    up_pieces = gather_rest(widening_matrix, up_half, qkv)
    attended0, lse0 = attend(0, up_pieces[2])
    up_pieces = gather_last(up_pieces, attended0)
    out_beside = xor_permute(tie(mixer_projection_matrix, qkv), "fsdp", nf, 1)
    out_pieces = (mixer_projection_matrix, out_beside) + up_pieces[2:]
    gate_pieces = gather_rest(gating_matrix, gate_half, attended0)
    attended1, lse1 = attend(1, gate_pieces[2], up_pieces[3])
    gate_pieces = gather_last(gate_pieces, attended1)
    down_pieces = gather_rest(narrowing_matrix, down_half, attended1)

    shared_rows = piece_rows(R, True)
    xhat1, inv1, low1, low1_turned, full_out = pl.pallas_call(
        mixer_kernel,
        grid_spec=pltpu.PrefetchScalarGridSpec(
            num_scalar_prefetch=1,
            grid=(nblk,),
            in_specs=[rowblk(PART), rowblk(PART), rowblk(D), whole((4, D))] + [ANY] * 8,
            out_specs=[rowblk(D), rowblk(LANE), rowblk(D), colblk(D), ANY],
            scratch_shapes=[pltpu.VMEM((D, D), bf16), pltpu.SemaphoreType.DMA((6,)), pltpu.SemaphoreType.DMA],
        ),
        out_shape=[shape((T, D), f32), shape((T, LANE), f32), shape((T, D), bf16), shape((D, T), bf16), shape((D, D), bf16)],
        **params(),
    )(shared_rows, attended0, attended1, x, vectors, *out_pieces, down_pieces[2], gate_pieces[3])

    W = FF // nf
    down_pieces = gather_last(down_pieces, low1)
    up_fac, gate_fac, prod, xhat2, inv2, pool, embed, full_up, full_gate, full_down = pl.pallas_call(
        ffn_kernel,
        grid_spec=pltpu.PrefetchScalarGridSpec(
            num_scalar_prefetch=1,
            grid=(nf,),
            in_specs=[whole((T, D)), whole((T, D)), whole((4, D)), whole((16, T)), whole((SEGS, LANE))] + [ANY] * 18,
            out_specs=[pl.BlockSpec((T, W), lambda i, rows: (0, rows[6] ^ i))] * 3
            + [whole((T, D)), whole((T, LANE)), whole((2 * SEGS, D)), whole((SEGS, D))]
            + [ANY] * 3,
            scratch_shapes=[
                pltpu.VMEM((nf, D, W), bf16),
                pltpu.VMEM((nf, D, W), bf16),
                pltpu.VMEM((nf, W, D), bf16),
                pltpu.SemaphoreType.DMA((nf * 12,)),
                pltpu.SemaphoreType.DMA((6,)),
                pltpu.SemaphoreType.DMA((nf * 3,)),
                pltpu.VMEM((16, D), f32),
                pltpu.VMEM((T, D), f32),
            ],
        ),
        out_shape=[shape((T, FF), bf16)] * 3
        + [shape((T, D), f32), shape((T, LANE), f32), shape((2 * SEGS, D), f32), shape((SEGS, D), bf16)]
        + [shape((D, FF), bf16), shape((D, FF), bf16), shape((FF, D), bf16)],
        **params(),
    )(shared_rows, low1, xhat1, vectors, mark_rows, count_rows, *up_pieces, *gate_pieces, *down_pieces)

    ranks = nb * nf
    total_rows = ranks * SEGS
    target = jnp.concatenate([matching_passages[0], jnp.zeros((SEGS - QSEG,), jnp.int32)])
    digits = jnp.pad(jnp.stack([target >> 5, target & 31], axis=1), ((0, 0), (0, LANE - 2))).astype(bf16)
    sent = jnp.concatenate([embed, digits], axis=1)
    if nb == 8:
        everyone = jnp.stack([sent] + [xor_permute(sent, "batch", nb, 2 * z) for z in range(1, 4)])
        everyone = jnp.stack([everyone, xor_permute(everyone, "fsdp", nf, 2)], axis=1)
        everyone = jnp.stack([everyone, xor_permute(everyone, "batch", nb, 1)], axis=1)
        everyone = jnp.stack([everyone, xor_permute(everyone, "fsdp", nf, 1)], axis=3)
    else:
        everyone = gather_relative(gather_relative(sent, "fsdp", nf), "batch", nb)
    everyone = everyone.reshape(total_rows, D + LANE)
    rank_of = ((jnp.arange(nb)[:, None] ^ b) * nf + (jnp.arange(nf)[None, :] ^ f)).reshape(ranks, 1)
    place_of = jnp.arange(SEGS)[None, :]
    doc_ids = jnp.where(place_of >= QSEG, rank_of * (SEGS - QSEG) + place_of - QSEG, -1).reshape(1, total_rows)
    doc_ids = jnp.broadcast_to(doc_ids, (8, total_rows)).astype(f32)
    loss_rows, grad_rows, small_two = pl.pallas_call(
        loss_kernel,
        grid=(total_rows // BLOCK,),
        in_specs=[
            pl.BlockSpec(memory_space=pltpu.SMEM),
            rowblk(D + LANE),
            whole((total_rows, D + LANE)),
            whole((8, total_rows)),
            whole((2 * SEGS, D)),
            whole((SEGS, LANE)),
        ],
        out_specs=[whole((SEGS, LANE)), whole((LANE, D)), whole((8, D))],
        out_shape=[shape((SEGS, LANE), f32), shape((LANE, D), f32), shape((8, D), f32)],
        scratch_shapes=[pltpu.VMEM((SEGS, D), f32)],
        **params(),
    )(softness_scale.reshape(1), everyone, everyone, doc_ids, pool, count_rows)
    query_loss = loss_rows[:QSEG, 0].reshape(1, QSEG)

    sum_two, grad_low, grad_low_turned = pl.pallas_call(
        norm_two_back_kernel,
        grid=(nblk,),
        in_specs=[rowblk(LANE), whole((LANE, D)), rowblk(D), rowblk(LANE), whole((4, D))],
        out_specs=[rowblk(D), rowblk(D), colblk(D)],
        out_shape=[shape((T, D), f32), shape((T, D), bf16), shape((D, T), bf16)],
        **params(),
    )(mask_q, grad_rows, xhat2, inv2, vectors)

    def add(*terms):
        return sum([term.astype(f32) for term in terms]).astype(bf16)

    def across(value, axis):
        if axis == "x":
            return xor_permute(value, "fsdp", nf, 2)
        return xor_permute(value, "batch", nb, 1 << BIT[axis])

    def over_batch(total):
        total = lax.psum(total.astype(f32), "batch").astype(bf16)
        return [total[:4], total[4:]]

    class Reduce:
        def __init__(self, order, keep, send):
            self.order, self.left, self.stage = order, 16, 0
            self.terms = [[[0, keep]], [[0, xor_permute(send, "fsdp", nf, 1)]]]
            self.arriving, self.pending = [], []

        def pick(self, low, high):
            found = []
            for term in self.terms:
                for start, array in term:
                    if array is not None and start <= low and high <= start + array.shape[0]:
                        found.append((array, low - start, high - low))
                        break
            return found

        def wanted(self, which):
            if which == "back":
                rest = [axis for axis in self.order if axis != "x"]
                self.pending.append((rest[6 - self.stage], None))
                self.stage += 1
                return [self.pick(0, 1)] if self.stage == 5 else [[(part, 0, part.shape[0])] for part in self.parts]
            half = self.left // 2
            middle = half + half // 2
            low, high = dict(all=(half, self.left), far=(middle, self.left), near=(half, middle))[which]
            sums = [self.pick(low, high)]
            arrival = [low - half, None]
            self.pending.append((self.order[self.stage], arrival))
            self.arriving.append(arrival)
            if which != "far":
                self.terms.append(self.arriving)
                self.arriving, self.left, self.stage = [], half, self.stage + 1
            return sums

        def go(self, out):
            axis, arrival = self.pending.pop(0)
            got = across(out, axis)
            if arrival is None:
                self.parts = [out, got]
            else:
                arrival[1] = got
            return got

    orders = [
        ("x", "z0", "y", "z1"),
        ("y", "x", "z0", "z1"),
        ("x", "y", "z0", "z1"),
        ("x", "z0", "y", "z1"),
        ("x", "y", "z0", "z1"),
    ]
    if nb != 8:
        orders = [("x", "y", "z0", "z1")] * 5

    def plain_sum(pieces, after):
        made = []
        for terms in pieces:
            arrays = [tie(array, *after) if after else array for array, _, _ in terms[-1:]]
            arrays = [array for array, _, _ in terms[:-1]] + arrays
            made.append(add(*[array[first : first + count] for array, (_, first, count) in zip(arrays, terms, strict=True)]))
        return made[0] if len(made) == 1 else jnp.concatenate(made, axis=0)

    def slot(after, *sends, apart=False):
        if nb != 8:
            sends = [
                (group, which)
                for k, (group, which) in enumerate(sends)
                if group.stage == 0 and not any(other is group and kind != "far" for other, kind in sends[:k])
            ]
        if not sends:
            return [], []
        wanted = [group.wanted(which) for group, which in sends]
        made = [plain_sum(pieces, after) for pieces in wanted] if apart else sums_of(wanted, after)
        gots = [group.go(out) for (group, _), out in zip(sends, made, strict=True)]
        for group, _ in sends:
            if nb != 8 and group.stage == 1 and not hasattr(group, "parts"):
                total = sum([array[first : first + count].astype(f32) for array, first, count in group.pick(0, 8)])
                group.parts = over_batch(total)
        return list(made), gots

    own_part = b if nb == 8 else 0
    info = jnp.stack([f, f ^ 1, f ^ 2, f ^ 3, own_part + 0 * f]).astype(jnp.int32)
    groups = W // BLOCK

    wide = nf * BLOCK

    def ffn_back(g, *after):
        parts = (16, R, PART)
        return pl.pallas_call(
            functools.partial(ffn_back_kernel, g, orders[g], groups),
            grid_spec=pltpu.PrefetchScalarGridSpec(
                num_scalar_prefetch=1,
                grid=(1,),
                in_specs=[ANY] * (7 + len(after)),
                out_specs=[ANY] * 4,
                scratch_shapes=[pltpu.VMEM((T, wide), bf16)] * 3
                + [pltpu.VMEM((T, D), bf16), pltpu.VMEM((D, T), bf16), pltpu.VMEM((D, T), bf16)]
                + [pltpu.VMEM((wide, D), bf16), pltpu.VMEM((2, T, wide), bf16)]
                + [pltpu.VMEM(parts, bf16)] * 2
                + [pltpu.SemaphoreType.DMA((20,)), pltpu.SemaphoreType.DMA((4,))],
            ),
            out_shape=[shape((T, wide), bf16)] * 2 + [shape(parts, bf16)] * 2,
            **params(),
        )(info, prod, up_fac, gate_fac, grad_low, grad_low_turned, low1_turned, full_down, *after)

    dup0, dgate0, keep, send = ffn_back(0)
    r0 = Reduce(orders[0], keep, send)
    dup1, dgate1, keep, send = ffn_back(1, send)
    r1 = Reduce(orders[1], keep, send)
    outs, gots = slot([dup1], (r0, "far"))
    dup2, dgate2, keep, send = ffn_back(2, send, *outs)
    r2 = Reduce(orders[2], keep, tie(send, *gots))
    outs, gots = slot([dup2] + gots, (r0, "near"), (r0, "all"), (r1, "far"))
    grad_hidden = pl.pallas_call(
        functools.partial(ffn_input_back_kernel, groups),
        in_specs=[ANY] * (3 + 2 * groups + len(outs)),
        out_specs=ANY,
        scratch_shapes=[
            pltpu.VMEM((2 * groups, T, wide), bf16),
            pltpu.VMEM((groups, D, wide), bf16),
            pltpu.VMEM((groups, D, wide), bf16),
            pltpu.VMEM((T, D), f32),
            pltpu.SemaphoreType.DMA((groups * 10 + 1,)),
            pltpu.SemaphoreType.DMA,
        ],
        out_shape=shape((T, D), f32),
        **params(),
    )(full_up, full_gate, sum_two, dup0, dgate0, dup1, dgate1, dup2, dgate2, *outs)
    outs, gots = slot([grad_hidden] + gots, (r1, "near"), (r2, "far"))

    sum_one, grad_branch, grad_att, delta, att_turned, small = pl.pallas_call(
        mixer_back_kernel,
        grid_spec=pltpu.PrefetchScalarGridSpec(
            num_scalar_prefetch=1,
            grid=(nblk,),
            in_specs=[
                rowblk(D),
                rowblk(D),
                rowblk(LANE),
                whole((4, D)),
                rowblk(PART),
                rowblk(PART),
                whole((D, D)),
                whole((PAIRS * 8, D)),
                whole((8, D)),
            ]
            + [ANY] * len(outs),
            out_specs=[
                rowblk(D),
                rowblk(D),
                rowblk(D),
                pl.BlockSpec((PAIRS, 8, BLOCK), lambda i, *_: (0, 0, i)),
                colblk(D),
                whole((nf, 2, SMALL, PART)),
            ],
            scratch_shapes=[pltpu.VMEM((8, D), f32)],
        ),
        out_shape=[
            shape((T, D), f32),
            shape((T, D), bf16),
            shape((T, D), bf16),
            shape((PAIRS, 8, T), f32),
            shape((D, T), bf16),
            shape((nf, 2, SMALL, PART), f32),
        ],
        **params(),
    )(info, grad_hidden, xhat1, inv1, vectors, attended0, attended1, full_out, heads, small_two, *outs)
    outs, gots = slot([grad_branch] + gots, (r0, "all"), (r1, "all"))

    def attend_back(h, *after):
        def cols(part, rows=None):
            at = 2 * part + h
            return pl.BlockSpec((rows or T, PART), (lambda i, *_: (i, at)) if rows else (lambda i, *_: (0, at)))

        kernel = functools.partial(drop_last, attend_back_kernel, len(after), 14)
        return pl.pallas_call(
            kernel,
            grid_spec=pltpu.PrefetchScalarGridSpec(
                num_scalar_prefetch=2,
                grid=(nblk,),
                in_specs=[
                    cols(0),
                    cols(1, BLOCK),
                    cols(2, BLOCK),
                    cols(0),
                    whole((PAIRS // 2, 8, T)),
                    pl.BlockSpec((PAIRS // 2, 8, T), lambda i, *_: (h, 0, 0)),
                    whole((T, LANE)),
                    rowblk(LANE),
                    whole((T, LANE)),
                    whole((T, LANE)),
                    rowblk(LANE),
                    rowblk(LANE),
                ]
                + [ANY] * len(after),
                out_specs=[whole((T, PART)), rowblk(PART), rowblk(PART)],
                scratch_shapes=[pltpu.VMEM((PART, T), f32)],
            ),
            out_shape=[shape((T, PART), bf16)] * 3,
            **params(),
        )(lo, spans, qkv, qkv, qkv, grad_att, (lse0, lse1)[h], delta, mask_q, mask_k, cosine, sine, cosine, sine, *after)

    def qkv_back(h, grads, extra, *after):
        dims = (16, R // 2 + extra, PART)
        return pl.pallas_call(
            functools.partial(qkv_back_kernel, extra, orders[3 + h]),
            grid_spec=pltpu.PrefetchScalarGridSpec(
                num_scalar_prefetch=1,
                grid=(4,),
                in_specs=[whole((D, T)), whole((D, T))]
                + [whole((T, PART))] * 3
                + [pl.BlockSpec((T, PART), lambda c, *_: (0, h)), whole((nf, 2, SMALL, PART))]
                + [ANY] * len(after),
                out_specs=[whole(dims)] * 2,
            ),
            out_shape=[shape(dims, bf16)] * 2,
            **params(),
        )(info, x_turned, att_turned, *grads, grad_branch, small, *after)

    grads0 = attend_back(0, *outs)
    outs, gots = slot([grads0[0]] + gots, (r2, "near"), (r2, "far"), (r0, "all"), (r1, "all"))
    keep, send = qkv_back(0, grads0, SMALL, *outs)
    r3 = Reduce(orders[3], keep, tie(send, *gots))
    outs, gots = slot([keep] + gots, (r0, "back"), (r1, "all"), (r2, "near"), (r2, "all"), (r3, "all"))
    grads1 = attend_back(1, *outs)
    outs, gots = slot([grads1[0]] + gots, (r0, "back"), (r1, "back"), (r2, "all"), (r3, "all"))
    keep, send = qkv_back(1, grads1, 0, *outs)
    r4 = Reduce(orders[4], keep, tie(send, *gots))
    outs, gots = slot([keep] + gots, (r0, "back"), (r1, "back"), (r2, "back"), (r3, "all"))
    more = slot([], (r4, "all"), apart=True)
    outs = outs + more[0]

    grad_input = pl.pallas_call(
        input_back_kernel,
        grid_spec=pltpu.PrefetchScalarGridSpec(
            num_scalar_prefetch=1,
            grid=(nblk,),
            in_specs=[rowblk(PART)] * 6 + [rowblk(D)] + [ANY] * (4 + len(outs)),
            out_specs=rowblk(D),
            scratch_shapes=[pltpu.VMEM((D, 3 * D), bf16), pltpu.SemaphoreType.DMA((4,))],
        ),
        out_shape=shape((T, D), f32),
        **params(),
    )(whole_rows, *grads0, *grads1, sum_one, *qkv_pieces, *outs)

    outs, _ = slot([grad_input], (r4, "all"), apart=True)
    slot(outs, (r1, "back"), (r2, "back"), (r3, "all"), apart=True)
    outs, _ = slot([], (r4, "all"), apart=True)
    slot(outs, (r2, "back"), (r3, "back"), apart=True)
    outs, _ = slot([], (r4, "all"), apart=True)
    slot(outs, (r3, "back"), apart=True)
    outs, _ = slot([], (r4, "back"), apart=True)
    slot(outs, (r3, "back"), apart=True)
    slot([], (r4, "back"), apart=True)
    slot([], (r4, "back"), apart=True)
    sum_up, sum_gate, sum_down = pl.pallas_call(
        functools.partial(ffn_out_kernel, (r0.order, r1.order, r2.order)),
        grid_spec=pltpu.PrefetchScalarGridSpec(
            num_scalar_prefetch=1,
            grid=(1,),
            in_specs=[whole((4, R, PART))] * (2 * groups),
            out_specs=[whole((R, FF)), whole((R, FF)), whole((W, D))],
        ),
        out_shape=[shape((R, FF), f32), shape((R, FF), f32), shape((W, D), f32)],
        **params(),
    )(info, *r0.parts, *r1.parts, *r2.parts)
    sum_qkv, sum_out, sum_small = pl.pallas_call(
        functools.partial(qkv_out_kernel, (r3.order, r4.order)),
        grid_spec=pltpu.PrefetchScalarGridSpec(
            num_scalar_prefetch=1,
            grid=(1,),
            in_specs=[whole((4, R // 2 + SMALL, PART))] * 2 + [whole((4, R // 2, PART))] * 2,
            out_specs=[whole((R, 3 * D)), whole((R, D)), whole((16, PART))],
        ),
        out_shape=[shape((R, 3 * D), f32), shape((R, D), f32), shape((16, PART), f32)],
        **params(),
    )(info, *r3.parts, *r4.parts)
    return (
        query_loss,
        grad_input[None],
        sum_qkv,
        sum_out,
        sum_up,
        sum_gate,
        sum_down,
        sum_small[0, :R],
        sum_small[0, R : 2 * R],
        sum_small[8, :R],
        sum_small[8, R : 2 * R],
    )


def solution(mesh):
    sizes = (mesh.shape["batch"], mesh.shape["fsdp"])
    return jax.shard_map(
        functools.partial(per_device, sizes),
        mesh=mesh,
        in_specs=(
            P(("batch", "fsdp"), None, None),
            P(("batch", "fsdp"), None),
            P(("batch", "fsdp"), None),
            P(),
            P("fsdp", None),
            P("fsdp", None),
            P("fsdp", None),
            P("fsdp", None),
            P("fsdp", None),
            P("fsdp"),
            P("fsdp"),
            P("fsdp"),
            P("fsdp"),
        ),
        out_specs=(
            P(("batch", "fsdp"), None),
            P(("batch", "fsdp"), None, None),
            P("fsdp", None),
            P("fsdp", None),
            P("fsdp", None),
            P("fsdp", None),
            P("fsdp", None),
            P("fsdp"),
            P("fsdp"),
            P("fsdp"),
            P("fsdp"),
        ),
        check_vma=False,
    )
```

```python
import functools
import math

import jax
import jax.numpy as jnp
from jax import lax
from jax.experimental import pallas as pl
from jax.experimental.pallas import tpu as pltpu
from jax.sharding import PartitionSpec as P

HEADS = 12
HD = 64
QSEG = 4
SEGS = 8
EPSILON = 1e-06
NEG = -1e30
LANE = 128
BLOCK = 256
PAIRS = HEADS // 2
PART = 384
SMALL = 16
MIB = 2**20

bf16 = jnp.bfloat16
f32 = jnp.float32


def dot(left, right, left_dim, right_dim):
    return lax.dot_general(
        left, right, (((left_dim,), (right_dim,)), ((), ())), preferred_element_type=f32
    )


def split_three(value):
    high = value.astype(bf16)
    rest = value - high.astype(f32)
    middle = rest.astype(bf16)
    low = (rest - middle.astype(f32)).astype(bf16)
    return high, middle, low


def params(limit=60):
    return dict(
        compiler_params=pltpu.CompilerParams(vmem_limit_bytes=limit * MIB),
        cost_estimate=pl.CostEstimate(flops=1, bytes_accessed=1, transcendentals=0),
    )


def shape(dims, dtype):
    return jax.ShapeDtypeStruct(dims, dtype)


ANY = pl.BlockSpec(memory_space=pl.ANY)


def whole(dims):
    return pl.BlockSpec(dims, lambda *_: (0,) * len(dims), pipeline_mode=pl.Buffered(1))


def swap_halves(tile):
    lane = lax.broadcasted_iota(jnp.int32, (1, LANE), 1)
    in_first = (lane & 63) < 32
    return jnp.where(in_first, pltpu.roll(tile, 96, 1), pltpu.roll(tile, 32, 1))


def norm_parts(value):
    center = value - jnp.mean(value, axis=1, keepdims=True)
    spread = jnp.mean(center * center, axis=1, keepdims=True)
    inv = lax.rsqrt(spread + EPSILON)
    return center * inv, inv


def norm_back(scaled, xhat, inv):
    mean_one = jnp.mean(scaled, axis=1, keepdims=True)
    mean_two = jnp.mean(scaled * xhat, axis=1, keepdims=True)
    return inv * (scaled - mean_one - xhat * mean_two)


def piece_copies(row_of, pieces, scratch, sems):
    return [
        pltpu.make_async_copy(
            piece, scratch.at[pl.ds(pl.multiple_of(row_of(k), 32), piece.shape[0])], sems.at[k]
        )
        for k, piece in enumerate(pieces)
    ]


def store_turned(ref, value, own, columns=slice(None)):
    rows = ref.shape[0] // 4
    turned = value.T
    for shard in range(4):
        at = pl.ds(pl.multiple_of((shard ^ own) * rows, 64), rows)
        ref[at, columns] = turned[shard * rows : (shard + 1) * rows]


def qkv_kernel(rows_ref, x_ref, cos_ref, sin_ref, *refs):
    pieces = refs[:4]
    out_ref, xt_ref, weight, sems = refs[-4:]
    step = pl.program_id(0)
    width = x_ref.shape[1]

    @pl.when(step == 0)
    def _():
        copies = piece_copies(lambda k: rows_ref[k], pieces, weight, sems)
        for copy in copies:
            copy.start()
        store_turned(xt_ref, x_ref[...], rows_ref[4])
        for copy in copies:
            copy.wait()

    joined = dot(x_ref[...], weight[:, pl.ds(pl.multiple_of(step * width, LANE), width)], 1, 0)

    @pl.when(step < 2)
    def _():
        scale = jnp.where(step == 0, 1.0 / math.sqrt(HD), 1.0)
        cos, sin = cos_ref[...] * scale, sin_ref[...] * scale
        for t in range(width // LANE):
            tile = joined[:, t * LANE : (t + 1) * LANE]
            out_ref[:, t * LANE : (t + 1) * LANE] = (tile * cos + swap_halves(tile) * sin).astype(bf16)

    @pl.when(step == 2)
    def _():
        out_ref[...] = joined.astype(bf16)


def key_range(first, count, total):
    blocks = (count + 1) >> 1
    first = jnp.minimum(first, total // LANE - 2 * blocks)
    return pl.multiple_of(first * LANE, LANE), blocks


def attend_kernel(lo_ref, n_ref, q_ref, k_ref, v_ref, mq_ref, mk_ref, o_ref, lse_ref):
    step = pl.program_id(0)
    lo, count = key_range(lo_ref[step], n_ref[step], k_ref.shape[0])
    first = lax.broadcasted_iota(jnp.int32, (1, LANE), 1) < HD
    zero = jnp.zeros((), bf16)
    mask_q = mq_ref[...]

    def run(width):
        keys = pl.ds(lo, width)
        mask_k = mk_ref[keys, :]

        def pair(p, _):
            cols = pl.ds(pl.multiple_of(p * LANE, LANE), LANE)
            q_pair, k_pair, v_pair = q_ref[:, cols], k_ref[keys, cols], v_ref[keys, cols]
            k_ext = jnp.concatenate([k_pair, mask_k], axis=1)
            outs, sums = [], []
            for h in range(2):
                q_one = jnp.where(first if h == 0 else ~first, q_pair, zero)
                scores = dot(jnp.concatenate([q_one, mask_q], axis=1), k_ext, 1, 1)
                peak = jnp.max(scores, axis=1, keepdims=True)
                weight = jnp.exp(scores - peak)
                total = jnp.sum(weight, axis=1, keepdims=True)
                outs.append(dot(weight.astype(bf16), v_pair, 1, 0) * (1.0 / total))
                sums.append(peak + jnp.log(total))
            o_ref[:, cols] = jnp.where(first, outs[0], outs[1]).astype(bf16)
            turned = jnp.where(first, sums[0], sums[1]).T
            lse_ref[p, 0:1, :] = turned[0:1]
            lse_ref[p, 1:2, :] = turned[HD : HD + 1]
            return 0

        lax.fori_loop(0, PAIRS // 2, pair, 0, unroll=True)

    for n in range(1, k_ref.shape[0] // BLOCK + 1):
        pl.when(count == n)(functools.partial(run, n * BLOCK))


def attend_back_kernel(
    lo_ref, n_ref, q_ref, k_ref, v_ref, do_ref, lse_ref, dl_ref, mq_ref, mk_ref, cos_ref, sin_ref, cosb_ref, sinb_ref,
    gq_ref, gk_ref, gv_ref, dq_acc,
):
    step = pl.program_id(0)

    @pl.when(step == 0)
    def _():
        dq_acc[...] = jnp.zeros_like(dq_acc)

    lo, count = key_range(lo_ref[step], n_ref[step], q_ref.shape[0])
    first = lax.broadcasted_iota(jnp.int32, (1, LANE), 1) < HD
    zero = jnp.zeros((), bf16)
    mask_k = mk_ref[...]
    cosb, sinb = cosb_ref[...], sinb_ref[...]

    def run(width):
        queries = pl.ds(lo, width)
        mask_q = mq_ref[queries, :]

        def pair(p, _):
            cols = pl.ds(pl.multiple_of(p * LANE, LANE), LANE)
            k_pair, v_pair = k_ref[:, cols], v_ref[:, cols]
            q_pair, do_pair = q_ref[queries, cols], do_ref[queries, cols]
            q_ext = jnp.concatenate([q_pair, mask_q], axis=1)
            k_turned = k_pair.T
            dk, dv = [], []
            for h in range(2):
                mine = first if h == 0 else ~first
                k_one, v_one = jnp.where(mine, k_pair, zero), jnp.where(mine, v_pair, zero)
                scores = dot(jnp.concatenate([k_one, mask_k], axis=1), q_ext, 1, 1)
                probs = jnp.exp(scores - lse_ref[p, h : h + 1, queries])
                dprobs = dot(v_one, do_pair, 1, 1)
                dscores = (probs * (dprobs - dl_ref[p, h : h + 1, queries])).astype(bf16)
                dv.append(dot(probs.astype(bf16), do_pair, 1, 0))
                dk.append(dot(dscores, q_pair, 1, 0))
                rows = pl.ds(pl.multiple_of(p * LANE + h * HD, HD), HD)
                dq_acc[rows, queries] += dot(k_turned[h * HD : (h + 1) * HD], dscores, 1, 0)
            gv_ref[:, cols] = jnp.where(first, dv[0], dv[1]).astype(bf16)
            grad = jnp.where(first, dk[0], dk[1])
            gk_ref[:, cols] = (grad * cosb - swap_halves(grad) * sinb).astype(bf16)
            return 0

        lax.fori_loop(0, PAIRS // 2, pair, 0, unroll=True)

    for n in range(1, q_ref.shape[0] // BLOCK + 1):
        pl.when(count == n)(functools.partial(run, n * BLOCK))

    @pl.when(step == pl.num_programs(0) - 1)
    def _():
        cos, sin = cos_ref[...], sin_ref[...]
        for p in range(PAIRS // 2):
            grad = dq_acc[p * LANE : (p + 1) * LANE, :].T * (1.0 / math.sqrt(HD))
            gq_ref[:, p * LANE : (p + 1) * LANE] = (grad * cos - swap_halves(grad) * sin).astype(bf16)


def mixer_kernel(rows_ref, att0_ref, att1_ref, x_ref, vec_ref, *refs):
    xhat_ref, inv_ref, low_ref, lowt_ref, full_ref, weight, sems, out_sem = refs[-8:]
    width = weight.shape[1]
    pieces = list(refs[:2]) + [piece.at[:, pl.ds(piece.shape[1] - width, width)] for piece in refs[2:4]]
    step = pl.program_id(0)
    out_copy = pltpu.make_async_copy(weight, full_ref, out_sem)

    @pl.when(step == 0)
    def _():
        copies = piece_copies(lambda k: rows_ref[k], pieces, weight, sems)
        for copy in copies:
            copy.start()
        for copy in copies:
            copy.wait()
        out_copy.start()

    branch = dot(att0_ref[...], weight[0:PART, :], 1, 0) + dot(att1_ref[...], weight[PART:, :], 1, 0)
    xhat, inv = norm_parts(x_ref[...].astype(f32) + branch)
    low = (xhat * vec_ref[0:1] + vec_ref[1:2]).astype(bf16)
    xhat_ref[...] = xhat
    inv_ref[...] = jnp.broadcast_to(inv, inv_ref.shape)
    low_ref[...] = low
    store_turned(lowt_ref, low, rows_ref[4])

    @pl.when(step == pl.num_programs(0) - 1)
    def _():
        out_copy.wait()


def ffn_kernel(rows_ref, low_ref, xhat_ref, vec_ref, mark_ref, cnt_ref, *refs):
    up_pieces, gate_pieces, down_pieces = refs[0:4], refs[4:8], refs[8:12]
    up_fac_ref, gate_fac_ref, prod_ref, xhat2_ref, inv2_ref, pool_ref, emb_ref = refs[12:19]
    full_up, full_gate, full_down = refs[19:22]
    w_up, w_gate, w_down, sems, down_sems, out_sems, pooled, total = refs[22:]
    step = pl.program_id(0)
    own = rows_ref[4]
    tokens, width = low_ref.shape
    wide = prod_ref.shape[1]
    steps = 4

    def in_copies(rel):
        cols = pl.ds(pl.multiple_of((own ^ rel) * wide, LANE), wide)
        copies = []
        for which, (pieces, scratch) in enumerate(((up_pieces, w_up), (gate_pieces, w_gate))):
            for k, piece in enumerate(pieces):
                rows = pl.ds(pl.multiple_of(rows_ref[k], 32), piece.shape[0])
                copies.append(
                    pltpu.make_async_copy(piece.at[:, cols], scratch.at[rel, rows], sems.at[rel * 8 + which * 4 + k])
                )
        copies.append(pltpu.make_async_copy(down_pieces[rel], w_down.at[rel], down_sems.at[rel]))
        return copies

    def out_copies(rel):
        cols = pl.ds(pl.multiple_of((own ^ rel) * wide, LANE), wide)
        return [
            pltpu.make_async_copy(w_up.at[rel], full_up.at[:, cols], out_sems.at[rel * 3]),
            pltpu.make_async_copy(w_gate.at[rel], full_gate.at[:, cols], out_sems.at[rel * 3 + 1]),
            pltpu.make_async_copy(w_down.at[rel], full_down.at[cols], out_sems.at[rel * 3 + 2]),
        ]

    @pl.when(step == 0)
    def _():
        for rel in range(2):
            for copy in in_copies(rel):
                copy.start()
        pooled[...] = jnp.zeros_like(pooled)

    for rel in range(steps):

        @pl.when(step == rel)
        def _(rel=rel):
            for copy in in_copies(rel):
                copy.wait()
            for copy in out_copies(rel):
                copy.start()
            if 0 < rel < steps - 1:
                for copy in in_copies(rel + 1):
                    copy.start()

    rows_at = 512

    def rows_block(i, _):
        rows = pl.ds(pl.multiple_of(i * rows_at, rows_at), rows_at)
        low = low_ref[rows, :]
        up = dot(low, w_up[step], 1, 0)
        gate = dot(low, w_gate[step], 1, 0)
        sig = 0.5 * jnp.tanh(0.5 * gate) + 0.5
        act = gate * sig
        up_fac_ref[rows, :] = act.astype(bf16)
        gate_fac_ref[rows, :] = (up * (sig + act * (1.0 - sig))).astype(bf16)
        prod = (act * up).astype(bf16)
        prod_ref[rows, :] = prod
        ffn = dot(prod, w_down[step], 1, 0)

        total[rows, :] = jnp.where(step == 0, ffn, total[rows, :] + ffn)
        return 0

    lax.fori_loop(0, tokens // rows_at, rows_block, 0, unroll=True)

    @pl.when(step == steps - 1)
    def _():
        def norm_block(i, _):
            rows = pl.ds(pl.multiple_of(i * BLOCK, BLOCK), BLOCK)
            xhat, inv = norm_parts(xhat_ref[rows, :] * vec_ref[0:1] + vec_ref[1:2] + total[rows, :])
            xhat2_ref[rows, :] = xhat
            inv2_ref[rows, :] = jnp.broadcast_to(inv, (BLOCK, LANE))
            marks = mark_ref[:, rows]
            part = jnp.zeros(pooled.shape, f32)
            for piece in split_three(xhat):
                part += dot(marks, piece, 1, 0)
            pooled[...] += part
            return 0

        lax.fori_loop(0, tokens // BLOCK, norm_block, 0)
        mean_xhat = pooled[0:SEGS] / cnt_ref[:, 0:1]
        pool = mean_xhat * vec_ref[2:3] + vec_ref[3:4]
        inv_len = lax.rsqrt(jnp.sum(pool * pool, axis=1, keepdims=True) + EPSILON)
        pool_ref[0:SEGS] = mean_xhat
        pool_ref[SEGS:] = pool
        emb_ref[...] = (pool * inv_len).astype(bf16)
        for rel in range(steps):
            for copy in out_copies(rel):
                copy.wait()


def loss_kernel(soft_ref, blk_ref, all_ref, ids_ref, pool_ref, cnt_ref, loss_ref, rows_ref, small_ref, acc):
    step = pl.program_id(0)
    soft = soft_ref[0]
    width = acc.shape[1]
    block, everyone = blk_ref[:, 0:width], all_ref[:, 0:width]
    target = blk_ref[:, width : width + LANE].astype(f32)
    target = target[:, 0:1] * 32.0 + target[:, 1:2]
    row = lax.broadcasted_iota(jnp.int32, (block.shape[0], 1), 0)
    asks = (row & (SEGS - 1)) < QSEG
    ids = ids_ref[0:1, :]
    logits = jnp.where(ids >= 0, dot(block, everyone, 1, 1) / soft, NEG)
    hit = asks & (target == ids)
    peak = jnp.max(logits, axis=1, keepdims=True)
    lse = peak + jnp.log(jnp.sum(jnp.exp(logits - peak), axis=1, keepdims=True))
    grad = (jnp.exp(logits - lse) - jnp.where(hit, 1.0, 0.0)) / soft
    grad = jnp.where(asks, grad, 0.0)
    turned = grad[:, 0:LANE].T[0:SEGS]
    part = jnp.zeros(acc.shape, f32)
    for piece in split_three(turned):
        part += dot(piece, block, 1, 0)

    @pl.when(step == 0)
    def _():
        own = part
        for piece in split_three(grad[0:SEGS]):
            own += dot(piece, everyone, 1, 0)
        acc[...] = own
        chosen = jnp.sum(jnp.where(hit, logits, 0.0), axis=1, keepdims=True)
        loss_ref[...] = jnp.broadcast_to((lse - chosen)[0:SEGS], loss_ref.shape)

    @pl.when(step > 0)
    def _():
        acc[...] += part

    @pl.when(step == pl.num_programs(0) - 1)
    def _():
        g = acc[...]
        mean_xhat, pool = pool_ref[0:SEGS], pool_ref[SEGS:]
        inv_len = lax.rsqrt(jnp.sum(pool * pool, axis=1, keepdims=True) + EPSILON)
        back = inv_len * g - inv_len * inv_len * inv_len * pool * jnp.sum(pool * g, axis=1, keepdims=True)
        rows_ref[...] = jnp.zeros_like(rows_ref)
        rows_ref[0:SEGS] = back / cnt_ref[:, 0:1]
        small_ref[...] = jnp.zeros_like(small_ref)
        small_ref[0:1] = jnp.sum(back * mean_xhat, axis=0, keepdims=True)
        small_ref[1:2] = jnp.sum(back, axis=0, keepdims=True)


def norm_two_back_kernel(mq_ref, rows_ref, xhat_ref, inv_ref, vec_ref, sum_ref, low_ref, lowt_ref):
    marks = mq_ref[...]
    scaled = jnp.zeros(xhat_ref.shape, f32)
    for piece in split_three(rows_ref[...] * vec_ref[2:3]):
        scaled += dot(marks, piece, 1, 0)
    grad = norm_back(scaled, xhat_ref[...], inv_ref[:, 0:1])
    sum_ref[...] = grad
    low = grad.astype(bf16)
    low_ref[...] = low
    lowt_ref[...] = low.T


BIT = dict(y=0, z0=1, z1=2)


def part_index(order, x, away):
    at = 0
    for axis in order:
        if axis == "z":
            at = at * 4 + (away >> 1)
        else:
            at = at * 2 + (x if axis == "x" else (away >> BIT[axis]) & 1)
    return at


def strips(source, to, sems, first, groups, g, shards, by_rows=False):
    copies = []
    for k, shard in enumerate(shards):
        at = (shard * groups + g) * BLOCK
        here = pl.ds(at if isinstance(at, int) else pl.multiple_of(at, BLOCK), BLOCK)
        there = pl.ds(k * BLOCK, BLOCK)
        if by_rows:
            copies.append(pltpu.make_async_copy(source.at[here], to.at[there], sems.at[first + k]))
        else:
            copies.append(pltpu.make_async_copy(source.at[:, here], to.at[:, there], sems.at[first + k]))
    return copies


def ffn_back_kernel(
    g, order, groups, info_ref, prod_any, up_fac_any, gate_fac_any, low_any, lowt_any, hidt_any, wd_any, *refs
):
    dup_any, dgate_any, keep_any, send_any = refs[-16:-12]
    prod, up_fac, gate_fac, low, lowt, hidt, wd, dups, keep, send, sems, out_sems = refs[-12:]
    own = info_ref[4]
    rows = keep.shape[1]
    targets = [(keep, 0), (send, 0), (keep, 1), (send, 1)]

    def one(source, to, first):
        return [pltpu.make_async_copy(source, to, sems.at[first])]

    plain = range(4)
    loads = dict(
        low=one(low_any, low, 0),
        wd=strips(wd_any, wd, sems, 4, groups, g, plain, by_rows=True),
        up_fac=strips(up_fac_any, up_fac, sems, 8, groups, g, plain),
        hidt=one(hidt_any, hidt, 1),
        gate_fac=strips(gate_fac_any, gate_fac, sems, 12, groups, g, plain),
        lowt=one(lowt_any, lowt, 2),
        prod=strips(prod_any, prod, sems, 16, groups, g, [info_ref[k] for k in range(4)]),
    )
    for copies in loads.values():
        for copy in copies:
            copy.start()

    def arrive(*names):
        for name in names:
            for copy in loads[name]:
                copy.wait()

    def store(rel, tile, value):
        ref, across = targets[rel]
        at = part_index(order, across, (tile // 3) ^ own)
        ref[at, :, tile % 3 * LANE : (tile % 3 + 1) * LANE] = value.astype(bf16)

    def store_columns(kind, value):
        for rel in range(4):
            for t in range(8):
                store(rel, kind * 8 + t, value[rel * rows : (rel + 1) * rows, t * LANE : (t + 1) * LANE])

    outs = [
        pltpu.make_async_copy(dups.at[0], dup_any, out_sems.at[0]),
        pltpu.make_async_copy(dups.at[1], dgate_any, out_sems.at[1]),
        pltpu.make_async_copy(send, send_any, out_sems.at[2]),
        pltpu.make_async_copy(keep, keep_any, out_sems.at[3]),
    ]
    arrive("low", "wd", "up_fac")
    dprod = dot(low[...], wd[...], 1, 1)
    dups[0] = (dprod * up_fac[...].astype(f32)).astype(bf16)
    arrive("gate_fac")
    dups[1] = (dprod * gate_fac[...].astype(f32)).astype(bf16)
    outs[0].start()
    outs[1].start()
    arrive("hidt")
    store_columns(0, dot(hidt[...], dups[0], 1, 0))
    store_columns(1, dot(hidt[...], dups[1], 1, 0))
    arrive("lowt", "prod")
    down = dot(lowt[...], prod[...], 1, 0)
    for rel in range(4):
        for k in range(4):
            for t in range(2):
                at = rel * BLOCK + t * LANE
                store(rel, 16 + 2 * k + t, down[k * rows : (k + 1) * rows, at : at + LANE])
    outs[2].start()
    outs[3].start()
    for copy in outs:
        copy.wait()


def ffn_input_back_kernel(groups, wu_any, wg_any, hid_any, *refs):
    dups = refs[: 2 * groups]
    out_any = refs[-7]
    dup, wu, wg, total, sems, out_sem = refs[-6:]
    plain = range(4)

    def loads(g):
        copies = [
            pltpu.make_async_copy(dups[2 * g + which], dup.at[2 * g + which], sems.at[g * 10 + which])
            for which in range(2)
        ]
        copies += strips(wu_any, wu.at[g], sems, g * 10 + 2, groups, g, plain)
        copies += strips(wg_any, wg.at[g], sems, g * 10 + 6, groups, g, plain)
        return copies

    base = pltpu.make_async_copy(hid_any, total, sems.at[groups * 10])
    for g in range(groups):
        for copy in loads(g):
            copy.start()
        if g == 0:
            base.start()

    def work(g, _):
        for k in range(groups):

            @pl.when(g == k)
            def _(k=k):
                for copy in loads(k):
                    copy.wait()
                if k == 0:
                    base.wait()

        total[...] += dot(dup[2 * g], wu[g], 1, 1) + dot(dup[2 * g + 1], wg[g], 1, 1)
        return 0

    lax.fori_loop(0, groups, work, 0)
    out = pltpu.make_async_copy(total, out_any, out_sem)
    out.start()
    out.wait()


def mixer_back_kernel(info_ref, grad_ref, xhat_ref, inv_ref, vec_ref, att0_ref, att1_ref, w_ref, heads_ref, two_ref, *refs):
    sum_ref, low_ref, datt_ref, dl_ref, attt_ref, small_ref, sums = refs[-7:]
    step = pl.program_id(0)
    grad, xhat = grad_ref[...], xhat_ref[...]
    out = norm_back(grad * vec_ref[0:1], xhat, inv_ref[:, 0:1])
    sum_ref[...] = out
    low = out.astype(bf16)
    low_ref[...] = low
    datt = dot(low, w_ref[...], 1, 1).astype(bf16)
    datt_ref[...] = datt
    att = jnp.concatenate([att0_ref[...], att1_ref[...]], axis=1)
    store_turned(attt_ref, att, info_ref[0])
    inner = datt.astype(f32) * att.astype(f32)
    heads = heads_ref[...]
    rows = jnp.zeros((heads.shape[0], inner.shape[0]), f32)
    for piece in split_three(inner)[:2]:
        rows += dot(heads, piece, 1, 1)
    for p in range(PAIRS):
        dl_ref[p] = rows[p * 8 : (p + 1) * 8]

    @pl.when(step == 0)
    def _():
        small_ref[...] = jnp.zeros_like(small_ref)
        sums[...] = jnp.zeros_like(sums)

    sums[0:1] += jnp.sum(grad * xhat, axis=0, keepdims=True)
    sums[1:2] += jnp.sum(grad, axis=0, keepdims=True)

    @pl.when(step == pl.num_programs(0) - 1)
    def _():
        width = sums.shape[1] // 4
        for y, ref in enumerate((sums, two_ref)):
            for shard in range(4):
                cols = slice(shard * width, (shard + 1) * width)
                small_ref[shard, y, 0:1, 0:width] = ref[0:1, cols]
                small_ref[shard, y, 0:1, width : 2 * width] = ref[1:2, cols]


def qkv_back_kernel(extra, order, info_ref, xt_ref, attt_ref, gq_ref, gk_ref, gv_ref, gb_ref, small_ref, *refs):
    keep_ref, send_ref = refs[-2:]
    step = pl.program_id(0)
    half = keep_ref.shape[1] - extra
    own = info_ref[4]
    targets = [(keep_ref, 0), (send_ref, 0), (keep_ref, 1), (send_ref, 1)]

    def run(left_ref, right_ref):
        value = dot(left_ref[...], right_ref[...], 1, 0).astype(bf16)
        for rel, (ref, across) in enumerate(targets):
            for y in range(2):
                at = (2 * rel + y) * half
                to = part_index(order, across, (2 * step + y) ^ own)
                ref[to, 0:half, :] = value[at : at + half]
                if extra:
                    ref[to, half:, :] = small_ref[info_ref[rel], y].astype(bf16)

    for which, right_ref in enumerate((gq_ref, gk_ref, gv_ref, gb_ref)):
        pl.when(step == which)(functools.partial(run, xt_ref if which < 3 else attt_ref, right_ref))


def copy_part(order, own, part, pair, write):
    away = part ^ own
    one, *rest = [axis for axis in order if axis != "x"]
    at = part_index(rest, 0, away)
    for which in range(2):

        @pl.when((away >> BIT[one]) & 1 == which)
        def _(which=which):
            write(pair[which][at].astype(f32))


def ffn_out_kernel(orders, info_ref, *refs):
    groups = (len(refs) - 3) // 2
    up_ref, gate_ref, down_ref = refs[-3:]
    own = info_ref[4]
    rows = up_ref.shape[0]
    for g in range(groups):
        for part in range(8):

            def write(value, g=g, part=part):
                for t in range(3):
                    tile = part * 3 + t
                    block = value[:, t * LANE : (t + 1) * LANE]
                    kind, within = tile // 8, tile % 8
                    if kind < 2:
                        at = ((within // 2) * groups + g) * BLOCK + (within % 2) * LANE
                        (up_ref, gate_ref)[kind][:, at : at + LANE] = block
                    else:
                        at = g * BLOCK + (within % 2) * LANE
                        col = (within // 2) * rows
                        down_ref[at : at + LANE, col : col + rows] = block.T

            copy_part(orders[g], own, part, refs[2 * g : 2 * g + 2], write)


def qkv_out_kernel(orders, info_ref, *refs):
    qkv_ref, out_ref, small_ref = refs[-3:]
    own = info_ref[4]
    half = qkv_ref.shape[0] // 2
    width = out_ref.shape[1]
    for h in range(2):
        for part in range(8):

            def write(value, h=h, part=part):
                y, c = part & 1, part >> 1
                rows = slice(y * half, (y + 1) * half)
                if c < 3:
                    at = c * width + h * PART
                    qkv_ref[rows, at : at + PART] = value[0:half]
                else:
                    out_ref[rows, h * PART : (h + 1) * PART] = value[0:half]
                if h == 0 and c == 0:
                    small_ref[y * 8 : y * 8 + 8] = value[half : half + 8]

            copy_part(orders[h], own, part, refs[2 * h : 2 * h + 2], write)


def input_back_kernel(rows_ref, gq0, gk0, gv0, gq1, gk1, gv1, sum_ref, *refs):
    pieces = refs[:4]
    out_ref, weight, sems = refs[-3:]
    width = sum_ref.shape[1]

    @pl.when(pl.program_id(0) == 0)
    def _():
        copies = piece_copies(lambda k: rows_ref[k], pieces, weight, sems)
        for copy in copies:
            copy.start()
        for copy in copies:
            copy.wait()

    total = sum_ref[...]
    for half, parts in enumerate(((gq0, gk0, gv0), (gq1, gk1, gv1))):
        for part, ref in enumerate(parts):
            at = part * width + half * PART
            total += dot(ref[...], weight[:, at : at + PART], 1, 1)
    out_ref[...] = total


def xor_permute(value, axis, size, bits):
    return lax.ppermute(value, axis, [(i, i ^ bits) for i in range(size)])


def join_kernel(first_ref, one_ref, two_ref, *refs):
    out_ref = refs[-1]
    rows = one_ref.shape[0]
    for ref, at in ((one_ref, first_ref[0]), (two_ref, 1 - first_ref[0])):
        out_ref[pl.ds(pl.multiple_of(at * rows, 32), rows), :] = ref[...]


def join(first, one, two, *after):
    dims = (2 * one.shape[0], one.shape[1])
    return pl.pallas_call(
        join_kernel,
        grid_spec=pltpu.PrefetchScalarGridSpec(
            num_scalar_prefetch=1,
            grid=(1,),
            in_specs=[whole(one.shape), whole(two.shape)] + [ANY] * len(after),
            out_specs=whole(dims),
        ),
        out_shape=shape(dims, one.dtype),
        **params(8),
    )(first, one, two, *after)


def sums_kernel(plan, *refs):
    outs = refs[len(refs) - len(plan) :]
    for out_ref, pieces in zip(outs, plan, strict=True):
        for offset, terms in pieces:
            total = refs[terms[0]][...].astype(f32)
            for term in terms[1:]:
                total += refs[term][...].astype(f32)
            out_ref[offset : offset + total.shape[0]] = total.astype(bf16)


def sums_of(wanted, after):
    inputs, specs, plan, shapes = [], [], [], []
    for pieces in wanted:
        offset, steps = 0, []
        for terms in pieces:
            indices = []
            for array, first, count in terms:
                indices.append(len(inputs))
                inputs.append(array)
                at = first // count
                specs.append(pl.BlockSpec((count,) + array.shape[1:], lambda i, at=at: (at, 0, 0)))
            steps.append((offset, indices))
            offset += terms[0][2]
        plan.append(steps)
        shapes.append((offset,) + pieces[0][0][0].shape[1:])
    return pl.pallas_call(
        functools.partial(drop_last, functools.partial(sums_kernel, plan), len(after), len(inputs)),
        grid=(1,),
        in_specs=specs + [ANY] * len(after),
        out_specs=[pl.BlockSpec(dims, lambda i: (0, 0, 0)) for dims in shapes],
        out_shape=[shape(dims, bf16) for dims in shapes],
        **params(16),
    )(*inputs, *after)


def drop_last(kernel, count, inputs, *refs):
    return kernel(*refs[:inputs], *refs[inputs + count :])


def gather_relative(value, axis, size):
    if size <= 8:
        return jnp.stack([value] + [xor_permute(value, axis, size, k) for k in range(1, size)])
    everyone = lax.all_gather(value, axis, axis=0)
    return jnp.take(everyone, jnp.arange(size) ^ lax.axis_index(axis), axis=0)


def absolute(stacked, own, bits):
    count = stacked.shape[0]
    for bit in range(bits):
        step = 1 << bit
        view = stacked.reshape((count // (2 * step), 2, step) + stacked.shape[1:])
        view = jnp.where((own >> bit) & 1 == 1, view[:, ::-1], view)
        stacked = view.reshape(stacked.shape)
    return stacked


def per_device(
    sizes,
    incoming_hidden_matrix,
    sequence_membership,
    matching_passages,
    softness_scale,
    combined_projection_matrix,
    mixer_projection_matrix,
    widening_matrix,
    gating_matrix,
    narrowing_matrix,
    mixer_scaling_factor,
    mixer_scaling_offset,
    perceptron_scaling_factor,
    perceptron_scaling_offset,
):
    nb, nf = sizes
    b, f = lax.axis_index("batch"), lax.axis_index("fsdp")
    x = incoming_hidden_matrix[0]
    segment = sequence_membership[0]
    T, D = x.shape
    FF = widening_matrix.shape[1]
    R = D // nf
    nblk = T // BLOCK
    y_bit = b & 1

    def tie(value, *others):
        return lax.optimization_barrier((value,) + others)[0]

    def own_half(own):
        rows = own.shape[0]
        return lax.dynamic_slice_in_dim(own, y_bit * (rows // 2), rows // 2, 0)

    def gather_far(own, beside, mine, other, *after):
        pair = join(y_bit.reshape(1), mine, other, *after)
        return (own, beside, pair, xor_permute(pair, "fsdp", nf, 1))

    marks = (segment[:, None] == jnp.arange(SEGS, dtype=jnp.int32)[None, :]).astype(jnp.int32)
    counts = jnp.sum(marks, axis=0)
    ends = jnp.cumsum(counts)
    firsts = ends - counts
    start_of = jnp.sum(marks * firsts[None, :], axis=1)
    end_of = jnp.sum(marks * ends[None, :], axis=1)
    positions = jnp.arange(T, dtype=jnp.int32) - start_of
    lane = jnp.arange(LANE)
    inverse = 1000.0 ** (-((lane % (HD // 2)).astype(f32) * 2.0) / HD)
    angles = positions.astype(f32)[:, None] * inverse[None, :]
    cosine, sine = jnp.cos(angles), jnp.where((lane % HD < HD // 2)[None, :], -1.0, 1.0) * jnp.sin(angles)
    same = segment[:, None] == jnp.arange(LANE, dtype=jnp.int32)[None, :]
    mask_q = same.astype(bf16)
    mask_k = jnp.where(same | (jnp.arange(LANE)[None, :] >= SEGS), 0.0, NEG).astype(bf16)
    mark_rows = (jnp.arange(16, dtype=jnp.int32)[:, None] == segment[None, :]).astype(bf16)
    lo = (start_of.reshape(nblk, BLOCK)[:, 0] // LANE).astype(jnp.int32)
    hi = ((end_of.reshape(nblk, BLOCK)[:, -1] + LANE - 1) // LANE).astype(jnp.int32)
    spans = hi - lo
    rows = combined_projection_matrix.shape[0]
    beyond = xor_permute(combined_projection_matrix, "fsdp", nf, 2)
    beside = xor_permute(combined_projection_matrix, "fsdp", nf, 1)
    both = jnp.concatenate([own_half(widening_matrix), own_half(mixer_projection_matrix)], axis=1)
    halves = [both, own_half(gating_matrix), own_half(narrowing_matrix)]
    vectors = jnp.stack(
        [mixer_scaling_factor, mixer_scaling_offset, perceptron_scaling_factor, perceptron_scaling_offset]
    )
    vectors = gather_relative(vectors, "fsdp", nf)
    beyond = tie(beyond, mask_q, mask_k, cosine, vectors, *halves)
    far = xor_permute(beyond, "fsdp", nf, 1)
    qkv_pieces = (combined_projection_matrix, beside, beyond, far)
    beside_all = [
        xor_permute(weight, "fsdp", nf, 1)
        for weight in (mixer_projection_matrix, widening_matrix, gating_matrix, narrowing_matrix)
    ]
    up_half = xor_permute(tie(halves[0], cosine, mask_q, mask_k), "fsdp", nf, 2)

    heads = (
        (jnp.arange(PAIRS * 8)[:, None] // 8 * 2 + jnp.arange(PAIRS * 8)[:, None] % 8 == jnp.arange(D)[None, :] // HD)
        & (jnp.arange(PAIRS * 8)[:, None] % 8 < 2)
    ).astype(bf16)
    count_rows = jnp.broadcast_to(counts.astype(f32)[:, None], (SEGS, LANE))

    def rowblk(width, rows=BLOCK):
        return pl.BlockSpec((rows, width), lambda i, *_: (i, 0))

    def colblk(height, cols=BLOCK):
        return pl.BlockSpec((height, cols), lambda i, *_: (0, i))

    whole_rows = jnp.stack([f * R, (f ^ 1) * R, (f ^ 2) * R, (f ^ 3) * R, f]).astype(jnp.int32)
    qkv, x_turned = pl.pallas_call(
        qkv_kernel,
        grid_spec=pltpu.PrefetchScalarGridSpec(
            num_scalar_prefetch=1,
            grid=(3,),
            in_specs=[whole((T, D)), whole((T, LANE)), whole((T, LANE))] + [ANY] * 9,
            out_specs=[pl.BlockSpec((T, D), lambda i, *_: (0, i)), whole((D, T))],
            scratch_shapes=[pltpu.VMEM((D, 3 * D), bf16), pltpu.SemaphoreType.DMA((4,))],
        ),
        out_shape=[shape((T, 3 * D), bf16), shape((D, T), bf16)],
        **params(22),
    )(whole_rows, x, cosine, sine, *qkv_pieces, vectors, *beside_all)

    vectors = absolute(vectors, f, 2)
    vectors = vectors.transpose(1, 0, 2).reshape(4, D).astype(f32)

    def attend(h, *after):
        def keys(part):
            return pl.BlockSpec((T, PART), lambda i, *_: (0, 2 * part + h))

        return pl.pallas_call(
            functools.partial(drop_last, attend_kernel, len(after), 7),
            grid_spec=pltpu.PrefetchScalarGridSpec(
                num_scalar_prefetch=2,
                grid=(nblk,),
                in_specs=[
                    pl.BlockSpec((BLOCK, PART), lambda i, *_: (i, h)),
                    keys(1),
                    keys(2),
                    rowblk(LANE),
                    whole((T, LANE)),
                ]
                + [ANY] * len(after),
                out_specs=[rowblk(PART), pl.BlockSpec((PAIRS // 2, 8, BLOCK), lambda i, *_: (0, 0, i))],
            ),
            out_shape=[shape((T, PART), bf16), shape((PAIRS // 2, 8, T), f32)],
            **params(14),
        )(lo, spans, qkv, qkv, qkv, mask_q, mask_k, *after)

    def onward(half, *before):
        half = tie(half, *before)
        return half, xor_permute(half, "batch", nb, 1)

    gate_half = xor_permute(tie(halves[1], qkv, up_half), "fsdp", nf, 2)
    up_half, up_other = onward(up_half, qkv)
    attended0, lse0 = attend(0, up_half)
    down_half = xor_permute(tie(halves[2], attended0, gate_half, up_other), "fsdp", nf, 2)
    gate_half, gate_other = onward(gate_half, attended0, up_other)
    up_pieces = gather_far(widening_matrix, beside_all[1], up_half, up_other, attended0, gate_half)
    attended1, lse1 = attend(1, gate_half, up_pieces[2])
    down_half, down_other = onward(down_half, attended1, gate_other)
    gate_pieces = gather_far(gating_matrix, beside_all[2], gate_half, gate_other, attended1, down_half)
    out_pieces = (mixer_projection_matrix, beside_all[0]) + up_pieces[2:]

    xhat1, inv1, low1, low1_turned, full_out = pl.pallas_call(
        mixer_kernel,
        grid_spec=pltpu.PrefetchScalarGridSpec(
            num_scalar_prefetch=1,
            grid=(nblk,),
            in_specs=[rowblk(PART), rowblk(PART), rowblk(D), whole((4, D))] + [ANY] * 6,
            out_specs=[rowblk(D), rowblk(LANE), rowblk(D), colblk(D), ANY],
            scratch_shapes=[pltpu.VMEM((D, D), bf16), pltpu.SemaphoreType.DMA((4,)), pltpu.SemaphoreType.DMA],
        ),
        out_shape=[shape((T, D), f32), shape((T, LANE), f32), shape((T, D), bf16), shape((D, T), bf16), shape((D, D), bf16)],
        **params(14),
    )(whole_rows, attended0, attended1, x, vectors, *out_pieces, down_half, gate_pieces[2])

    W = FF // nf
    down_pieces = gather_far(narrowing_matrix, beside_all[3], down_half, down_other, low1)
    up_fac, gate_fac, prod, xhat2, inv2, pool, embed, full_up, full_gate, full_down = pl.pallas_call(
        ffn_kernel,
        grid_spec=pltpu.PrefetchScalarGridSpec(
            num_scalar_prefetch=1,
            grid=(nf,),
            in_specs=[whole((T, D)), whole((T, D)), whole((4, D)), whole((16, T)), whole((SEGS, LANE))] + [ANY] * 12,
            out_specs=[pl.BlockSpec((T, W), lambda i, rows: (0, rows[4] ^ i))] * 3
            + [whole((T, D)), whole((T, LANE)), whole((2 * SEGS, D)), whole((SEGS, D))]
            + [ANY] * 3,
            scratch_shapes=[
                pltpu.VMEM((nf, D, W), bf16),
                pltpu.VMEM((nf, D, W), bf16),
                pltpu.VMEM((nf, W, D), bf16),
                pltpu.SemaphoreType.DMA((nf * 8,)),
                pltpu.SemaphoreType.DMA((nf,)),
                pltpu.SemaphoreType.DMA((nf * 3,)),
                pltpu.VMEM((16, D), f32),
                pltpu.VMEM((T, D), f32),
            ],
        ),
        out_shape=[shape((T, FF), bf16)] * 3
        + [shape((T, D), f32), shape((T, LANE), f32), shape((2 * SEGS, D), f32), shape((SEGS, D), bf16)]
        + [shape((D, FF), bf16), shape((D, FF), bf16), shape((FF, D), bf16)],
        **params(46),
    )(whole_rows, low1, xhat1, vectors, mark_rows, count_rows, *up_pieces, *gate_pieces, *down_pieces)

    ranks = nb * nf
    total_rows = ranks * SEGS
    target = jnp.concatenate([matching_passages[0], jnp.zeros((SEGS - QSEG,), jnp.int32)])
    digits = jnp.pad(jnp.stack([target >> 5, target & 31], axis=1), ((0, 0), (0, LANE - 2))).astype(bf16)
    sent = jnp.concatenate([embed, digits], axis=1)
    if nb == 8:
        everyone = jnp.stack([sent] + [xor_permute(sent, "batch", nb, 2 * z) for z in range(1, 4)])
        everyone = jnp.stack([everyone, xor_permute(everyone, "fsdp", nf, 2)], axis=1)
        everyone = jnp.stack([everyone, xor_permute(everyone, "batch", nb, 1)], axis=1)
        everyone = jnp.stack([everyone, xor_permute(everyone, "fsdp", nf, 1)], axis=3)
    else:
        everyone = gather_relative(gather_relative(sent, "fsdp", nf), "batch", nb)
    everyone = everyone.reshape(total_rows, D + LANE)
    rank_of = ((jnp.arange(nb)[:, None] ^ b) * nf + (jnp.arange(nf)[None, :] ^ f)).reshape(ranks, 1)
    place_of = jnp.arange(SEGS)[None, :]
    doc_ids = jnp.where(place_of >= QSEG, rank_of * (SEGS - QSEG) + place_of - QSEG, -1).reshape(1, total_rows)
    doc_ids = jnp.broadcast_to(doc_ids, (8, total_rows)).astype(f32)
    loss_rows, grad_rows, small_two = pl.pallas_call(
        loss_kernel,
        grid=(total_rows // BLOCK,),
        in_specs=[
            pl.BlockSpec(memory_space=pltpu.SMEM),
            rowblk(D + LANE),
            whole((total_rows, D + LANE)),
            whole((8, total_rows)),
            whole((2 * SEGS, D)),
            whole((SEGS, LANE)),
        ],
        out_specs=[whole((SEGS, LANE)), whole((LANE, D)), whole((8, D))],
        out_shape=[shape((SEGS, LANE), f32), shape((LANE, D), f32), shape((8, D), f32)],
        scratch_shapes=[pltpu.VMEM((SEGS, D), f32)],
        **params(8),
    )(softness_scale.reshape(1), everyone, everyone, doc_ids, pool, count_rows)
    query_loss = loss_rows[:QSEG, 0].reshape(1, QSEG)

    sum_two, grad_low, grad_low_turned = pl.pallas_call(
        norm_two_back_kernel,
        grid=(nblk,),
        in_specs=[rowblk(LANE), whole((LANE, D)), rowblk(D), rowblk(LANE), whole((4, D))],
        out_specs=[rowblk(D), rowblk(D), colblk(D)],
        out_shape=[shape((T, D), f32), shape((T, D), bf16), shape((D, T), bf16)],
        **params(12),
    )(mask_q, grad_rows, xhat2, inv2, vectors)

    def add(*terms):
        return sum([term.astype(f32) for term in terms]).astype(bf16)

    def across(value, axis):
        if axis == "x":
            return xor_permute(value, "fsdp", nf, 2)
        return xor_permute(value, "batch", nb, 1 << BIT[axis])

    def over_batch(total):
        total = lax.psum(total.astype(f32), "batch").astype(bf16)
        return [total[:4], total[4:]]

    class Reduce:
        def __init__(self, order, keep, send):
            self.order, self.left, self.stage = order, 16, 0
            self.terms = [[[0, keep]], [[0, xor_permute(send, "fsdp", nf, 1)]]]
            self.arriving, self.pending = [], []

        def pick(self, low, high):
            found = []
            for term in self.terms:
                for start, array in term:
                    if array is not None and start <= low and high <= start + array.shape[0]:
                        found.append((array, low - start, high - low))
                        break
            return found

        def wanted(self, which):
            if which == "back":
                rest = [axis for axis in self.order if axis != "x"]
                self.pending.append((rest[6 - self.stage], None))
                self.stage += 1
                return [self.pick(0, 1)] if self.stage == 5 else [[(part, 0, part.shape[0])] for part in self.parts]
            half = self.left // 2
            middle = half + half // 2
            low, high = dict(all=(half, self.left), far=(middle, self.left), near=(half, middle))[which]
            sums = [self.pick(low, high)]
            arrival = [low - half, None]
            self.pending.append((self.order[self.stage], arrival))
            self.arriving.append(arrival)
            if which != "far":
                self.terms.append(self.arriving)
                self.arriving, self.left, self.stage = [], half, self.stage + 1
            return sums

        def go(self, out):
            axis, arrival = self.pending.pop(0)
            got = across(out, axis)
            if arrival is None:
                self.parts = [out, got]
            else:
                arrival[1] = got
            return got

    orders = [
        ("x", "z0", "y", "z1"),
        ("y", "x", "z0", "z1"),
        ("x", "y", "z0", "z1"),
        ("x", "z0", "y", "z1"),
        ("x", "y", "z0", "z1"),
    ]
    if nb != 8:
        orders = [("x", "y", "z0", "z1")] * 5

    def plain_sum(pieces, after):
        made = []
        for terms in pieces:
            arrays = [tie(array, *after) if after else array for array, _, _ in terms[-1:]]
            arrays = [array for array, _, _ in terms[:-1]] + arrays
            made.append(add(*[array[first : first + count] for array, (_, first, count) in zip(arrays, terms, strict=True)]))
        return made[0] if len(made) == 1 else jnp.concatenate(made, axis=0)

    def slot(after, *sends, apart=False):
        if nb != 8:
            sends = [
                (group, which)
                for k, (group, which) in enumerate(sends)
                if group.stage == 0 and not any(other is group and kind != "far" for other, kind in sends[:k])
            ]
        if not sends:
            return [], []
        wanted = [group.wanted(which) for group, which in sends]
        made = [plain_sum(pieces, after) for pieces in wanted] if apart else sums_of(wanted, after)
        gots = [group.go(out) for (group, _), out in zip(sends, made, strict=True)]
        for group, _ in sends:
            if nb != 8 and group.stage == 1 and not hasattr(group, "parts"):
                total = sum([array[first : first + count].astype(f32) for array, first, count in group.pick(0, 8)])
                group.parts = over_batch(total)
        return list(made), gots

    own_part = b if nb == 8 else 0
    info = jnp.stack([f, f ^ 1, f ^ 2, f ^ 3, own_part + 0 * f]).astype(jnp.int32)
    groups = W // BLOCK

    wide = nf * BLOCK

    def ffn_back(g, *after):
        parts = (16, R, PART)
        return pl.pallas_call(
            functools.partial(ffn_back_kernel, g, orders[g], groups),
            grid_spec=pltpu.PrefetchScalarGridSpec(
                num_scalar_prefetch=1,
                grid=(1,),
                in_specs=[ANY] * (7 + len(after)),
                out_specs=[ANY] * 4,
                scratch_shapes=[pltpu.VMEM((T, wide), bf16)] * 3
                + [pltpu.VMEM((T, D), bf16), pltpu.VMEM((D, T), bf16), pltpu.VMEM((D, T), bf16)]
                + [pltpu.VMEM((wide, D), bf16), pltpu.VMEM((2, T, wide), bf16)]
                + [pltpu.VMEM(parts, bf16)] * 2
                + [pltpu.SemaphoreType.DMA((20,)), pltpu.SemaphoreType.DMA((4,))],
            ),
            out_shape=[shape((T, wide), bf16)] * 2 + [shape(parts, bf16)] * 2,
            **params(38),
        )(info, prod, up_fac, gate_fac, grad_low, grad_low_turned, low1_turned, full_down, *after)

    dup0, dgate0, keep, send = ffn_back(0)
    r0 = Reduce(orders[0], keep, send)
    dup1, dgate1, keep, send = ffn_back(1, send)
    r1 = Reduce(orders[1], keep, send)
    outs, gots = slot([dup1], (r0, "far"))
    dup2, dgate2, keep, send = ffn_back(2, send, *outs)
    r2 = Reduce(orders[2], keep, tie(send, *gots))
    outs, gots = slot([dup2] + gots, (r0, "near"), (r0, "all"), (r1, "far"))
    grad_hidden = pl.pallas_call(
        functools.partial(ffn_input_back_kernel, groups),
        in_specs=[ANY] * (3 + 2 * groups + len(outs)),
        out_specs=ANY,
        scratch_shapes=[
            pltpu.VMEM((2 * groups, T, wide), bf16),
            pltpu.VMEM((groups, D, wide), bf16),
            pltpu.VMEM((groups, D, wide), bf16),
            pltpu.VMEM((T, D), f32),
            pltpu.SemaphoreType.DMA((groups * 10 + 1,)),
            pltpu.SemaphoreType.DMA,
        ],
        out_shape=shape((T, D), f32),
        **params(36),
    )(full_up, full_gate, sum_two, dup0, dgate0, dup1, dgate1, dup2, dgate2, *outs)
    outs, gots = slot([grad_hidden] + gots, (r1, "near"), (r2, "far"))

    sum_one, grad_branch, grad_att, delta, att_turned, small = pl.pallas_call(
        mixer_back_kernel,
        grid_spec=pltpu.PrefetchScalarGridSpec(
            num_scalar_prefetch=1,
            grid=(nblk,),
            in_specs=[
                rowblk(D),
                rowblk(D),
                rowblk(LANE),
                whole((4, D)),
                rowblk(PART),
                rowblk(PART),
                whole((D, D)),
                whole((PAIRS * 8, D)),
                whole((8, D)),
            ]
            + [ANY] * len(outs),
            out_specs=[
                rowblk(D),
                rowblk(D),
                rowblk(D),
                pl.BlockSpec((PAIRS, 8, BLOCK), lambda i, *_: (0, 0, i)),
                colblk(D),
                whole((nf, 2, SMALL, PART)),
            ],
            scratch_shapes=[pltpu.VMEM((8, D), f32)],
        ),
        out_shape=[
            shape((T, D), f32),
            shape((T, D), bf16),
            shape((T, D), bf16),
            shape((PAIRS, 8, T), f32),
            shape((D, T), bf16),
            shape((nf, 2, SMALL, PART), f32),
        ],
        **params(16),
    )(info, grad_hidden, xhat1, inv1, vectors, attended0, attended1, full_out, heads, small_two, *outs)
    outs, gots = slot([grad_branch] + gots, (r0, "all"), (r1, "all"))

    def attend_back(h, *after):
        def cols(part, rows=None):
            at = 2 * part + h
            return pl.BlockSpec((rows or T, PART), (lambda i, *_: (i, at)) if rows else (lambda i, *_: (0, at)))

        kernel = functools.partial(drop_last, attend_back_kernel, len(after), 14)
        return pl.pallas_call(
            kernel,
            grid_spec=pltpu.PrefetchScalarGridSpec(
                num_scalar_prefetch=2,
                grid=(nblk,),
                in_specs=[
                    cols(0),
                    cols(1, BLOCK),
                    cols(2, BLOCK),
                    cols(0),
                    whole((PAIRS // 2, 8, T)),
                    pl.BlockSpec((PAIRS // 2, 8, T), lambda i, *_: (h, 0, 0)),
                    whole((T, LANE)),
                    rowblk(LANE),
                    whole((T, LANE)),
                    whole((T, LANE)),
                    rowblk(LANE),
                    rowblk(LANE),
                ]
                + [ANY] * len(after),
                out_specs=[whole((T, PART)), rowblk(PART), rowblk(PART)],
                scratch_shapes=[pltpu.VMEM((PART, T), f32)],
            ),
            out_shape=[shape((T, PART), bf16)] * 3,
            **params(16),
        )(lo, spans, qkv, qkv, qkv, grad_att, (lse0, lse1)[h], delta, mask_q, mask_k, cosine, sine, cosine, sine, *after)

    def qkv_back(h, grads, extra, *after):
        dims = (16, R // 2 + extra, PART)
        return pl.pallas_call(
            functools.partial(qkv_back_kernel, extra, orders[3 + h]),
            grid_spec=pltpu.PrefetchScalarGridSpec(
                num_scalar_prefetch=1,
                grid=(4,),
                in_specs=[whole((D, T)), whole((D, T))]
                + [whole((T, PART))] * 3
                + [pl.BlockSpec((T, PART), lambda c, *_: (0, h)), whole((nf, 2, SMALL, PART))]
                + [ANY] * len(after),
                out_specs=[whole(dims)] * 2,
            ),
            out_shape=[shape(dims, bf16)] * 2,
            **params(18),
        )(info, x_turned, att_turned, *grads, grad_branch, small, *after)

    grads0 = attend_back(0, *outs)
    outs, gots = slot([grads0[0]] + gots, (r2, "near"), (r2, "far"), (r0, "all"), (r1, "all"))
    keep, send = qkv_back(0, grads0, SMALL, *outs)
    r3 = Reduce(orders[3], keep, tie(send, *gots))
    outs, gots = slot([keep] + gots, (r0, "back"), (r1, "all"), (r2, "near"), (r2, "all"), (r3, "all"))
    grads1 = attend_back(1, *outs)
    outs, gots = slot([grads1[0]] + gots, (r0, "back"), (r1, "back"), (r2, "all"), (r3, "all"))
    keep, send = qkv_back(1, grads1, 0, *outs)
    r4 = Reduce(orders[4], keep, tie(send, *gots))
    outs, gots = slot([keep] + gots, (r0, "back"), (r1, "back"), (r2, "back"), (r3, "all"))
    more = slot([], (r4, "all"), apart=True)
    outs = outs + more[0]

    grad_input = pl.pallas_call(
        input_back_kernel,
        grid_spec=pltpu.PrefetchScalarGridSpec(
            num_scalar_prefetch=1,
            grid=(nblk,),
            in_specs=[rowblk(PART)] * 6 + [rowblk(D)] + [ANY] * (4 + len(outs)),
            out_specs=rowblk(D),
            scratch_shapes=[pltpu.VMEM((D, 3 * D), bf16), pltpu.SemaphoreType.DMA((4,))],
        ),
        out_shape=shape((T, D), f32),
        **params(16),
    )(whole_rows, *grads0, *grads1, sum_one, *qkv_pieces, *outs)

    outs, _ = slot([grad_input], (r4, "all"), apart=True)
    slot(outs, (r1, "back"), (r2, "back"), (r3, "all"), apart=True)
    outs, _ = slot([], (r4, "all"), apart=True)
    slot(outs, (r2, "back"), (r3, "back"), apart=True)
    outs, _ = slot([], (r4, "all"), apart=True)
    slot(outs, (r3, "back"), apart=True)
    outs, _ = slot([], (r4, "back"), apart=True)
    slot(outs, (r3, "back"), apart=True)
    slot([], (r4, "back"), apart=True)
    slot([], (r4, "back"), apart=True)
    sum_up, sum_gate, sum_down = pl.pallas_call(
        functools.partial(ffn_out_kernel, (r0.order, r1.order, r2.order)),
        grid_spec=pltpu.PrefetchScalarGridSpec(
            num_scalar_prefetch=1,
            grid=(1,),
            in_specs=[whole((4, R, PART))] * (2 * groups),
            out_specs=[whole((R, FF)), whole((R, FF)), whole((W, D))],
        ),
        out_shape=[shape((R, FF), f32), shape((R, FF), f32), shape((W, D), f32)],
        **params(26),
    )(info, *r0.parts, *r1.parts, *r2.parts)
    sum_qkv, sum_out, sum_small = pl.pallas_call(
        functools.partial(qkv_out_kernel, (r3.order, r4.order)),
        grid_spec=pltpu.PrefetchScalarGridSpec(
            num_scalar_prefetch=1,
            grid=(1,),
            in_specs=[whole((4, R // 2 + SMALL, PART))] * 2 + [whole((4, R // 2, PART))] * 2,
            out_specs=[whole((R, 3 * D)), whole((R, D)), whole((16, PART))],
        ),
        out_shape=[shape((R, 3 * D), f32), shape((R, D), f32), shape((16, PART), f32)],
        **params(16),
    )(info, *r3.parts, *r4.parts)
    return (
        query_loss,
        grad_input[None],
        sum_qkv,
        sum_out,
        sum_up,
        sum_gate,
        sum_down,
        sum_small[0, :R],
        sum_small[0, R : 2 * R],
        sum_small[8, :R],
        sum_small[8, R : 2 * R],
    )


def solution(mesh):
    sizes = (mesh.shape["batch"], mesh.shape["fsdp"])
    return jax.shard_map(
        functools.partial(per_device, sizes),
        mesh=mesh,
        in_specs=(
            P(("batch", "fsdp"), None, None),
            P(("batch", "fsdp"), None),
            P(("batch", "fsdp"), None),
            P(),
            P("fsdp", None),
            P("fsdp", None),
            P("fsdp", None),
            P("fsdp", None),
            P("fsdp", None),
            P("fsdp"),
            P("fsdp"),
            P("fsdp"),
            P("fsdp"),
        ),
        out_specs=(
            P(("batch", "fsdp"), None),
            P(("batch", "fsdp"), None, None),
            P("fsdp", None),
            P("fsdp", None),
            P("fsdp", None),
            P("fsdp", None),
            P("fsdp", None),
            P("fsdp"),
            P("fsdp"),
            P("fsdp"),
            P("fsdp"),
        ),
        check_vma=False,
    )
```

```python
import functools
import math

import jax
import jax.numpy as jnp
from jax import lax
from jax.experimental import pallas as pl
from jax.experimental.pallas import tpu as pltpu
from jax.sharding import PartitionSpec as P

HEADS = 12
HD = 64
QSEG = 4
SEGS = 8
EPSILON = 1e-06
NEG = -1e30
LANE = 128
BLOCK = 256
PAIRS = HEADS // 2
PART = 384
SMALL = 16
MIB = 2**20

bf16 = jnp.bfloat16
f32 = jnp.float32


def dot(left, right, left_dim, right_dim):
    return lax.dot_general(
        left, right, (((left_dim,), (right_dim,)), ((), ())), preferred_element_type=f32
    )


def split_three(value):
    high = value.astype(bf16)
    rest = value - high.astype(f32)
    middle = rest.astype(bf16)
    low = (rest - middle.astype(f32)).astype(bf16)
    return high, middle, low


def params(limit=60):
    return dict(
        compiler_params=pltpu.CompilerParams(vmem_limit_bytes=limit * MIB),
        cost_estimate=pl.CostEstimate(flops=1, bytes_accessed=1, transcendentals=0),
    )


def shape(dims, dtype):
    return jax.ShapeDtypeStruct(dims, dtype)


ANY = pl.BlockSpec(memory_space=pl.ANY)


def whole(dims):
    return pl.BlockSpec(dims, lambda *_: (0,) * len(dims), pipeline_mode=pl.Buffered(1))


def swap_halves(tile):
    lane = lax.broadcasted_iota(jnp.int32, (1, LANE), 1)
    in_first = (lane & 63) < 32
    return jnp.where(in_first, pltpu.roll(tile, 96, 1), pltpu.roll(tile, 32, 1))


def norm_parts(value):
    center = value - jnp.mean(value, axis=1, keepdims=True)
    spread = jnp.mean(center * center, axis=1, keepdims=True)
    inv = lax.rsqrt(spread + EPSILON)
    return center * inv, inv


def norm_back(scaled, xhat, inv):
    mean_one = jnp.mean(scaled, axis=1, keepdims=True)
    mean_two = jnp.mean(scaled * xhat, axis=1, keepdims=True)
    return inv * (scaled - mean_one - xhat * mean_two)


def piece_copies(row_of, pieces, scratch, sems):
    return [
        pltpu.make_async_copy(
            piece, scratch.at[pl.ds(pl.multiple_of(row_of(k), 32), piece.shape[0])], sems.at[k]
        )
        for k, piece in enumerate(pieces)
    ]


def store_turned(ref, value, own, columns=slice(None)):
    rows = ref.shape[0] // 4
    turned = value.T
    for shard in range(4):
        at = pl.ds(pl.multiple_of((shard ^ own) * rows, 64), rows)
        ref[at, columns] = turned[shard * rows : (shard + 1) * rows]


def qkv_kernel(rows_ref, x_ref, cos_ref, sin_ref, *refs):
    pieces = refs[:4]
    out_ref, xt_ref, weight, sems = refs[-4:]
    step = pl.program_id(0)
    width = x_ref.shape[1]

    @pl.when(step == 0)
    def _():
        copies = piece_copies(lambda k: rows_ref[k], pieces, weight, sems)
        for copy in copies:
            copy.start()
        store_turned(xt_ref, x_ref[...], rows_ref[4])
        for copy in copies:
            copy.wait()

    joined = dot(x_ref[...], weight[:, pl.ds(pl.multiple_of(step * width, LANE), width)], 1, 0)

    @pl.when(step < 2)
    def _():
        scale = jnp.where(step == 0, 1.0 / math.sqrt(HD), 1.0)
        cos, sin = cos_ref[...] * scale, sin_ref[...] * scale
        for t in range(width // LANE):
            tile = joined[:, t * LANE : (t + 1) * LANE]
            out_ref[:, t * LANE : (t + 1) * LANE] = (tile * cos + swap_halves(tile) * sin).astype(bf16)

    @pl.when(step == 2)
    def _():
        out_ref[...] = joined.astype(bf16)


def key_range(first, count, total):
    blocks = (count + 1) >> 1
    first = jnp.minimum(first, total // LANE - 2 * blocks)
    return pl.multiple_of(first * LANE, LANE), blocks


def attend_kernel(lo_ref, n_ref, q_ref, k_ref, v_ref, mq_ref, mk_ref, o_ref, lse_ref):
    step = pl.program_id(0)
    lo, count = key_range(lo_ref[step], n_ref[step], k_ref.shape[0])
    first = lax.broadcasted_iota(jnp.int32, (1, LANE), 1) < HD
    zero = jnp.zeros((), bf16)
    mask_q = mq_ref[...]

    def run(width):
        keys = pl.ds(lo, width)
        mask_k = mk_ref[keys, :]

        def pair(p, _):
            cols = pl.ds(pl.multiple_of(p * LANE, LANE), LANE)
            q_pair, k_pair, v_pair = q_ref[:, cols], k_ref[keys, cols], v_ref[keys, cols]
            k_ext = jnp.concatenate([k_pair, mask_k], axis=1)
            outs, sums = [], []
            for h in range(2):
                q_one = jnp.where(first if h == 0 else ~first, q_pair, zero)
                scores = dot(jnp.concatenate([q_one, mask_q], axis=1), k_ext, 1, 1)
                peak = jnp.max(scores, axis=1, keepdims=True)
                weight = jnp.exp(scores - peak)
                total = jnp.sum(weight, axis=1, keepdims=True)
                outs.append(dot(weight.astype(bf16), v_pair, 1, 0) * (1.0 / total))
                sums.append(peak + jnp.log(total))
            o_ref[:, cols] = jnp.where(first, outs[0], outs[1]).astype(bf16)
            turned = jnp.where(first, sums[0], sums[1]).T
            lse_ref[p, 0:1, :] = turned[0:1]
            lse_ref[p, 1:2, :] = turned[HD : HD + 1]
            return 0

        lax.fori_loop(0, PAIRS // 2, pair, 0, unroll=True)

    for n in range(1, k_ref.shape[0] // BLOCK + 1):
        pl.when(count == n)(functools.partial(run, n * BLOCK))


def attend_back_kernel(
    lo_ref, n_ref, q_ref, k_ref, v_ref, do_ref, lse_ref, dl_ref, mq_ref, mk_ref, cos_ref, sin_ref, cosb_ref, sinb_ref,
    gq_ref, gk_ref, gv_ref, dq_acc,
):
    step = pl.program_id(0)

    @pl.when(step == 0)
    def _():
        dq_acc[...] = jnp.zeros_like(dq_acc)

    lo, count = key_range(lo_ref[step], n_ref[step], q_ref.shape[0])
    first = lax.broadcasted_iota(jnp.int32, (1, LANE), 1) < HD
    zero = jnp.zeros((), bf16)
    mask_k = mk_ref[...]
    cosb, sinb = cosb_ref[...], sinb_ref[...]

    def run(width):
        queries = pl.ds(lo, width)
        mask_q = mq_ref[queries, :]

        def pair(p, _):
            cols = pl.ds(pl.multiple_of(p * LANE, LANE), LANE)
            k_pair, v_pair = k_ref[:, cols], v_ref[:, cols]
            q_pair, do_pair = q_ref[queries, cols], do_ref[queries, cols]
            q_ext = jnp.concatenate([q_pair, mask_q], axis=1)
            k_turned = k_pair.T
            dk, dv = [], []
            for h in range(2):
                mine = first if h == 0 else ~first
                k_one, v_one = jnp.where(mine, k_pair, zero), jnp.where(mine, v_pair, zero)
                scores = dot(jnp.concatenate([k_one, mask_k], axis=1), q_ext, 1, 1)
                probs = jnp.exp(scores - lse_ref[p, h : h + 1, queries])
                dprobs = dot(v_one, do_pair, 1, 1)
                dscores = (probs * (dprobs - dl_ref[p, h : h + 1, queries])).astype(bf16)
                dv.append(dot(probs.astype(bf16), do_pair, 1, 0))
                dk.append(dot(dscores, q_pair, 1, 0))
                rows = pl.ds(pl.multiple_of(p * LANE + h * HD, HD), HD)
                dq_acc[rows, queries] += dot(k_turned[h * HD : (h + 1) * HD], dscores, 1, 0)
            gv_ref[:, cols] = jnp.where(first, dv[0], dv[1]).astype(bf16)
            grad = jnp.where(first, dk[0], dk[1])
            gk_ref[:, cols] = (grad * cosb - swap_halves(grad) * sinb).astype(bf16)
            return 0

        lax.fori_loop(0, PAIRS // 2, pair, 0, unroll=True)

    for n in range(1, q_ref.shape[0] // BLOCK + 1):
        pl.when(count == n)(functools.partial(run, n * BLOCK))

    @pl.when(step == pl.num_programs(0) - 1)
    def _():
        cos, sin = cos_ref[...], sin_ref[...]
        for p in range(PAIRS // 2):
            grad = dq_acc[p * LANE : (p + 1) * LANE, :].T * (1.0 / math.sqrt(HD))
            gq_ref[:, p * LANE : (p + 1) * LANE] = (grad * cos - swap_halves(grad) * sin).astype(bf16)


def mixer_kernel(rows_ref, att0_ref, att1_ref, x_ref, vec_ref, *refs):
    xhat_ref, inv_ref, low_ref, lowt_ref, full_ref, weight, sems, out_sem = refs[-8:]
    width = weight.shape[1]
    pieces = list(refs[:2]) + [piece.at[:, pl.ds(piece.shape[1] - width, width)] for piece in refs[2:4]]
    step = pl.program_id(0)
    out_copy = pltpu.make_async_copy(weight, full_ref, out_sem)

    @pl.when(step == 0)
    def _():
        copies = piece_copies(lambda k: rows_ref[k], pieces, weight, sems)
        for copy in copies:
            copy.start()
        for copy in copies:
            copy.wait()
        out_copy.start()

    branch = dot(att0_ref[...], weight[0:PART, :], 1, 0) + dot(att1_ref[...], weight[PART:, :], 1, 0)
    xhat, inv = norm_parts(x_ref[...].astype(f32) + branch)
    low = (xhat * vec_ref[0:1] + vec_ref[1:2]).astype(bf16)
    xhat_ref[...] = xhat
    inv_ref[...] = jnp.broadcast_to(inv, inv_ref.shape)
    low_ref[...] = low
    store_turned(lowt_ref, low, rows_ref[4])

    @pl.when(step == pl.num_programs(0) - 1)
    def _():
        out_copy.wait()


def ffn_kernel(rows_ref, low_ref, xhat_ref, vec_ref, mark_ref, cnt_ref, *refs):
    up_pieces, gate_pieces, down_pieces = refs[0:4], refs[4:8], refs[8:12]
    up_fac_ref, gate_fac_ref, prod_ref, xhat2_ref, inv2_ref, pool_ref, emb_ref = refs[12:19]
    full_up, full_gate, full_down = refs[19:22]
    w_up, w_gate, w_down, sems, down_sems, out_sems, pooled, total = refs[22:]
    step = pl.program_id(0)
    own = rows_ref[4]
    tokens, width = low_ref.shape
    wide = prod_ref.shape[1]
    steps = 4

    def in_copies(rel):
        cols = pl.ds(pl.multiple_of((own ^ rel) * wide, LANE), wide)
        copies = []
        for which, (pieces, scratch) in enumerate(((up_pieces, w_up), (gate_pieces, w_gate))):
            for k, piece in enumerate(pieces):
                rows = pl.ds(pl.multiple_of(rows_ref[k], 32), piece.shape[0])
                copies.append(
                    pltpu.make_async_copy(piece.at[:, cols], scratch.at[rel, rows], sems.at[rel * 8 + which * 4 + k])
                )
        copies.append(pltpu.make_async_copy(down_pieces[rel], w_down.at[rel], down_sems.at[rel]))
        return copies

    def out_copies(rel):
        cols = pl.ds(pl.multiple_of((own ^ rel) * wide, LANE), wide)
        return [
            pltpu.make_async_copy(w_up.at[rel], full_up.at[:, cols], out_sems.at[rel * 3]),
            pltpu.make_async_copy(w_gate.at[rel], full_gate.at[:, cols], out_sems.at[rel * 3 + 1]),
            pltpu.make_async_copy(w_down.at[rel], full_down.at[cols], out_sems.at[rel * 3 + 2]),
        ]

    @pl.when(step == 0)
    def _():
        for rel in range(2):
            for copy in in_copies(rel):
                copy.start()
        pooled[...] = jnp.zeros_like(pooled)

    for rel in range(steps):

        @pl.when(step == rel)
        def _(rel=rel):
            for copy in in_copies(rel):
                copy.wait()
            for copy in out_copies(rel):
                copy.start()
            if 0 < rel < steps - 1:
                for copy in in_copies(rel + 1):
                    copy.start()

    rows_at = 512

    def rows_block(i, _):
        rows = pl.ds(pl.multiple_of(i * rows_at, rows_at), rows_at)
        low = low_ref[rows, :]
        up = dot(low, w_up[step], 1, 0)
        gate = dot(low, w_gate[step], 1, 0)
        sig = 0.5 * jnp.tanh(0.5 * gate) + 0.5
        act = gate * sig
        up_fac_ref[rows, :] = act.astype(bf16)
        gate_fac_ref[rows, :] = (up * (sig + act * (1.0 - sig))).astype(bf16)
        prod = (act * up).astype(bf16)
        prod_ref[rows, :] = prod
        ffn = dot(prod, w_down[step], 1, 0)

        total[rows, :] = jnp.where(step == 0, ffn, total[rows, :] + ffn)
        return 0

    lax.fori_loop(0, tokens // rows_at, rows_block, 0, unroll=True)

    @pl.when(step == steps - 1)
    def _():
        def norm_block(i, _):
            rows = pl.ds(pl.multiple_of(i * BLOCK, BLOCK), BLOCK)
            xhat, inv = norm_parts(xhat_ref[rows, :] * vec_ref[0:1] + vec_ref[1:2] + total[rows, :])
            xhat2_ref[rows, :] = xhat
            inv2_ref[rows, :] = jnp.broadcast_to(inv, (BLOCK, LANE))
            marks = mark_ref[:, rows]
            part = jnp.zeros(pooled.shape, f32)
            for piece in split_three(xhat):
                part += dot(marks, piece, 1, 0)
            pooled[...] += part
            return 0

        lax.fori_loop(0, tokens // BLOCK, norm_block, 0)
        mean_xhat = pooled[0:SEGS] / cnt_ref[:, 0:1]
        pool = mean_xhat * vec_ref[2:3] + vec_ref[3:4]
        inv_len = lax.rsqrt(jnp.sum(pool * pool, axis=1, keepdims=True) + EPSILON)
        pool_ref[0:SEGS] = mean_xhat
        pool_ref[SEGS:] = pool
        emb_ref[...] = (pool * inv_len).astype(bf16)
        for rel in range(steps):
            for copy in out_copies(rel):
                copy.wait()


def loss_kernel(soft_ref, blk_ref, all_ref, ids_ref, pool_ref, cnt_ref, loss_ref, rows_ref, small_ref, acc):
    step = pl.program_id(0)
    soft = soft_ref[0]
    width = acc.shape[1]
    block, everyone = blk_ref[:, 0:width], all_ref[:, 0:width]
    target = blk_ref[:, width : width + LANE].astype(f32)
    target = target[:, 0:1] * 32.0 + target[:, 1:2]
    row = lax.broadcasted_iota(jnp.int32, (block.shape[0], 1), 0)
    asks = (row & (SEGS - 1)) < QSEG
    ids = ids_ref[0:1, :]
    logits = jnp.where(ids >= 0, dot(block, everyone, 1, 1) / soft, NEG)
    hit = asks & (target == ids)
    peak = jnp.max(logits, axis=1, keepdims=True)
    lse = peak + jnp.log(jnp.sum(jnp.exp(logits - peak), axis=1, keepdims=True))
    grad = (jnp.exp(logits - lse) - jnp.where(hit, 1.0, 0.0)) / soft
    grad = jnp.where(asks, grad, 0.0)
    turned = grad[:, 0:LANE].T[0:SEGS]
    part = jnp.zeros(acc.shape, f32)
    for piece in split_three(turned):
        part += dot(piece, block, 1, 0)

    @pl.when(step == 0)
    def _():
        own = part
        for piece in split_three(grad[0:SEGS]):
            own += dot(piece, everyone, 1, 0)
        acc[...] = own
        chosen = jnp.sum(jnp.where(hit, logits, 0.0), axis=1, keepdims=True)
        loss_ref[...] = jnp.broadcast_to((lse - chosen)[0:SEGS], loss_ref.shape)

    @pl.when(step > 0)
    def _():
        acc[...] += part

    @pl.when(step == pl.num_programs(0) - 1)
    def _():
        g = acc[...]
        mean_xhat, pool = pool_ref[0:SEGS], pool_ref[SEGS:]
        inv_len = lax.rsqrt(jnp.sum(pool * pool, axis=1, keepdims=True) + EPSILON)
        back = inv_len * g - inv_len * inv_len * inv_len * pool * jnp.sum(pool * g, axis=1, keepdims=True)
        rows_ref[...] = jnp.zeros_like(rows_ref)
        rows_ref[0:SEGS] = back / cnt_ref[:, 0:1]
        small_ref[...] = jnp.zeros_like(small_ref)
        small_ref[0:1] = jnp.sum(back * mean_xhat, axis=0, keepdims=True)
        small_ref[1:2] = jnp.sum(back, axis=0, keepdims=True)


def norm_two_back_kernel(mq_ref, rows_ref, xhat_ref, inv_ref, vec_ref, sum_ref, low_ref, lowt_ref):
    marks = mq_ref[...]
    scaled = jnp.zeros(xhat_ref.shape, f32)
    for piece in split_three(rows_ref[...] * vec_ref[2:3]):
        scaled += dot(marks, piece, 1, 0)
    grad = norm_back(scaled, xhat_ref[...], inv_ref[:, 0:1])
    sum_ref[...] = grad
    low = grad.astype(bf16)
    low_ref[...] = low
    lowt_ref[...] = low.T


BIT = dict(y=0, z0=1, z1=2)


def part_index(order, x, away):
    at = 0
    for axis in order:
        if axis == "z":
            at = at * 4 + (away >> 1)
        else:
            at = at * 2 + (x if axis == "x" else (away >> BIT[axis]) & 1)
    return at


def strips(source, to, sems, first, groups, g, shards, by_rows=False):
    copies = []
    for k, shard in enumerate(shards):
        at = (shard * groups + g) * BLOCK
        here = pl.ds(at if isinstance(at, int) else pl.multiple_of(at, BLOCK), BLOCK)
        there = pl.ds(k * BLOCK, BLOCK)
        if by_rows:
            copies.append(pltpu.make_async_copy(source.at[here], to.at[there], sems.at[first + k]))
        else:
            copies.append(pltpu.make_async_copy(source.at[:, here], to.at[:, there], sems.at[first + k]))
    return copies


def ffn_back_kernel(
    g, order, groups, info_ref, prod_any, up_fac_any, gate_fac_any, low_any, lowt_any, hidt_any, wd_any, *refs
):
    dup_any, dgate_any, keep_any, send_any = refs[-16:-12]
    prod, up_fac, gate_fac, low, lowt, hidt, wd, dups, keep, send, sems, out_sems = refs[-12:]
    own = info_ref[4]
    rows = keep.shape[1]
    targets = [(keep, 0), (send, 0), (keep, 1), (send, 1)]

    def one(source, to, first):
        return [pltpu.make_async_copy(source, to, sems.at[first])]

    plain = range(4)
    loads = dict(
        low=one(low_any, low, 0),
        wd=strips(wd_any, wd, sems, 4, groups, g, plain, by_rows=True),
        up_fac=strips(up_fac_any, up_fac, sems, 8, groups, g, plain),
        hidt=one(hidt_any, hidt, 1),
        gate_fac=strips(gate_fac_any, gate_fac, sems, 12, groups, g, plain),
        lowt=one(lowt_any, lowt, 2),
        prod=strips(prod_any, prod, sems, 16, groups, g, [info_ref[k] for k in range(4)]),
    )
    for copies in loads.values():
        for copy in copies:
            copy.start()

    def arrive(*names):
        for name in names:
            for copy in loads[name]:
                copy.wait()

    def store(rel, tile, value):
        ref, across = targets[rel]
        at = part_index(order, across, (tile // 3) ^ own)
        ref[at, :, tile % 3 * LANE : (tile % 3 + 1) * LANE] = value.astype(bf16)

    def store_columns(kind, value):
        for rel in range(4):
            for t in range(8):
                store(rel, kind * 8 + t, value[rel * rows : (rel + 1) * rows, t * LANE : (t + 1) * LANE])

    outs = [
        pltpu.make_async_copy(dups.at[0], dup_any, out_sems.at[0]),
        pltpu.make_async_copy(dups.at[1], dgate_any, out_sems.at[1]),
        pltpu.make_async_copy(send, send_any, out_sems.at[2]),
        pltpu.make_async_copy(keep, keep_any, out_sems.at[3]),
    ]
    arrive("low", "wd", "up_fac")
    dprod = dot(low[...], wd[...], 1, 1)
    dups[0] = (dprod * up_fac[...].astype(f32)).astype(bf16)
    arrive("gate_fac")
    dups[1] = (dprod * gate_fac[...].astype(f32)).astype(bf16)
    outs[0].start()
    outs[1].start()
    arrive("hidt")
    store_columns(0, dot(hidt[...], dups[0], 1, 0))
    store_columns(1, dot(hidt[...], dups[1], 1, 0))
    arrive("lowt", "prod")
    down = dot(lowt[...], prod[...], 1, 0)
    for rel in range(4):
        for k in range(4):
            for t in range(2):
                at = rel * BLOCK + t * LANE
                store(rel, 16 + 2 * k + t, down[k * rows : (k + 1) * rows, at : at + LANE])
    outs[2].start()
    outs[3].start()
    for copy in outs:
        copy.wait()


def ffn_input_back_kernel(groups, wu_any, wg_any, hid_any, *refs):
    dups = refs[: 2 * groups]
    out_any = refs[-7]
    dup, wu, wg, total, sems, out_sem = refs[-6:]
    plain = range(4)

    def loads(g):
        copies = [
            pltpu.make_async_copy(dups[2 * g + which], dup.at[2 * g + which], sems.at[g * 10 + which])
            for which in range(2)
        ]
        copies += strips(wu_any, wu.at[g], sems, g * 10 + 2, groups, g, plain)
        copies += strips(wg_any, wg.at[g], sems, g * 10 + 6, groups, g, plain)
        return copies

    base = pltpu.make_async_copy(hid_any, total, sems.at[groups * 10])
    for g in range(groups):
        for copy in loads(g):
            copy.start()
        if g == 0:
            base.start()

    def work(g, _):
        for k in range(groups):

            @pl.when(g == k)
            def _(k=k):
                for copy in loads(k):
                    copy.wait()
                if k == 0:
                    base.wait()

        total[...] += dot(dup[2 * g], wu[g], 1, 1) + dot(dup[2 * g + 1], wg[g], 1, 1)
        return 0

    lax.fori_loop(0, groups, work, 0)
    out = pltpu.make_async_copy(total, out_any, out_sem)
    out.start()
    out.wait()


def mixer_back_kernel(info_ref, grad_ref, xhat_ref, inv_ref, vec_ref, att0_ref, att1_ref, w_ref, heads_ref, two_ref, *refs):
    sum_ref, low_ref, datt_ref, dl_ref, attt_ref, small_ref, sums = refs[-7:]
    step = pl.program_id(0)
    grad, xhat = grad_ref[...], xhat_ref[...]
    out = norm_back(grad * vec_ref[0:1], xhat, inv_ref[:, 0:1])
    sum_ref[...] = out
    low = out.astype(bf16)
    low_ref[...] = low
    datt = dot(low, w_ref[...], 1, 1).astype(bf16)
    datt_ref[...] = datt
    att = jnp.concatenate([att0_ref[...], att1_ref[...]], axis=1)
    store_turned(attt_ref, att, info_ref[0])
    inner = datt.astype(f32) * att.astype(f32)
    heads = heads_ref[...]
    rows = jnp.zeros((heads.shape[0], inner.shape[0]), f32)
    for piece in split_three(inner)[:2]:
        rows += dot(heads, piece, 1, 1)
    for p in range(PAIRS):
        dl_ref[p] = rows[p * 8 : (p + 1) * 8]

    @pl.when(step == 0)
    def _():
        small_ref[...] = jnp.zeros_like(small_ref)
        sums[...] = jnp.zeros_like(sums)

    sums[0:1] += jnp.sum(grad * xhat, axis=0, keepdims=True)
    sums[1:2] += jnp.sum(grad, axis=0, keepdims=True)

    @pl.when(step == pl.num_programs(0) - 1)
    def _():
        width = sums.shape[1] // 4
        for y, ref in enumerate((sums, two_ref)):
            for shard in range(4):
                cols = slice(shard * width, (shard + 1) * width)
                small_ref[shard, y, 0:1, 0:width] = ref[0:1, cols]
                small_ref[shard, y, 0:1, width : 2 * width] = ref[1:2, cols]


def qkv_back_kernel(extra, order, info_ref, xt_ref, attt_ref, gq_ref, gk_ref, gv_ref, gb_ref, small_ref, *refs):
    keep_ref, send_ref = refs[-2:]
    step = pl.program_id(0)
    half = keep_ref.shape[1] - extra
    own = info_ref[4]
    targets = [(keep_ref, 0), (send_ref, 0), (keep_ref, 1), (send_ref, 1)]

    def run(left_ref, right_ref):
        value = dot(left_ref[...], right_ref[...], 1, 0).astype(bf16)
        for rel, (ref, across) in enumerate(targets):
            for y in range(2):
                at = (2 * rel + y) * half
                to = part_index(order, across, (2 * step + y) ^ own)
                ref[to, 0:half, :] = value[at : at + half]
                if extra:
                    ref[to, half:, :] = small_ref[info_ref[rel], y].astype(bf16)

    for which, right_ref in enumerate((gq_ref, gk_ref, gv_ref, gb_ref)):
        pl.when(step == which)(functools.partial(run, xt_ref if which < 3 else attt_ref, right_ref))


def copy_part(order, own, part, pair, write):
    away = part ^ own
    one, *rest = [axis for axis in order if axis != "x"]
    at = part_index(rest, 0, away)
    for which in range(2):

        @pl.when((away >> BIT[one]) & 1 == which)
        def _(which=which):
            write(pair[which][at].astype(f32))


def ffn_out_kernel(orders, info_ref, *refs):
    groups = (len(refs) - 3) // 2
    up_ref, gate_ref, down_ref = refs[-3:]
    own = info_ref[4]
    rows = up_ref.shape[0]
    for g in range(groups):
        for part in range(8):

            def write(value, g=g, part=part):
                for t in range(3):
                    tile = part * 3 + t
                    block = value[:, t * LANE : (t + 1) * LANE]
                    kind, within = tile // 8, tile % 8
                    if kind < 2:
                        at = ((within // 2) * groups + g) * BLOCK + (within % 2) * LANE
                        (up_ref, gate_ref)[kind][:, at : at + LANE] = block
                    else:
                        at = g * BLOCK + (within % 2) * LANE
                        col = (within // 2) * rows
                        down_ref[at : at + LANE, col : col + rows] = block.T

            copy_part(orders[g], own, part, refs[2 * g : 2 * g + 2], write)


def qkv_out_kernel(orders, info_ref, *refs):
    qkv_ref, out_ref, small_ref = refs[-3:]
    own = info_ref[4]
    half = qkv_ref.shape[0] // 2
    width = out_ref.shape[1]
    for h in range(2):
        for part in range(8):

            def write(value, h=h, part=part):
                y, c = part & 1, part >> 1
                rows = slice(y * half, (y + 1) * half)
                if c < 3:
                    at = c * width + h * PART
                    qkv_ref[rows, at : at + PART] = value[0:half]
                else:
                    out_ref[rows, h * PART : (h + 1) * PART] = value[0:half]
                if h == 0 and c == 0:
                    small_ref[y * 8 : y * 8 + 8] = value[half : half + 8]

            copy_part(orders[h], own, part, refs[2 * h : 2 * h + 2], write)


def input_back_kernel(rows_ref, gq0, gk0, gv0, gq1, gk1, gv1, sum_ref, *refs):
    pieces = refs[:4]
    out_ref, weight, sems = refs[-3:]
    width = sum_ref.shape[1]

    @pl.when(pl.program_id(0) == 0)
    def _():
        copies = piece_copies(lambda k: rows_ref[k], pieces, weight, sems)
        for copy in copies:
            copy.start()
        for copy in copies:
            copy.wait()

    total = sum_ref[...]
    for half, parts in enumerate(((gq0, gk0, gv0), (gq1, gk1, gv1))):
        for part, ref in enumerate(parts):
            at = part * width + half * PART
            total += dot(ref[...], weight[:, at : at + PART], 1, 1)
    out_ref[...] = total


def xor_permute(value, axis, size, bits):
    return lax.ppermute(value, axis, [(i, i ^ bits) for i in range(size)])


def join_kernel(first_ref, one_ref, two_ref, *refs):
    out_ref = refs[-1]
    rows = one_ref.shape[0]
    for ref, at in ((one_ref, first_ref[0]), (two_ref, 1 - first_ref[0])):
        out_ref[pl.ds(pl.multiple_of(at * rows, 32), rows), :] = ref[...]


def join(first, one, two, *after):
    dims = (2 * one.shape[0], one.shape[1])
    return pl.pallas_call(
        join_kernel,
        grid_spec=pltpu.PrefetchScalarGridSpec(
            num_scalar_prefetch=1,
            grid=(1,),
            in_specs=[whole(one.shape), whole(two.shape)] + [ANY] * len(after),
            out_specs=whole(dims),
        ),
        out_shape=shape(dims, one.dtype),
        **params(8),
    )(first, one, two, *after)


def sums_kernel(plan, *refs):
    outs = refs[len(refs) - len(plan) :]
    for out_ref, pieces in zip(outs, plan, strict=True):
        for offset, terms in pieces:
            total = refs[terms[0]][...].astype(f32)
            for term in terms[1:]:
                total += refs[term][...].astype(f32)
            out_ref[offset : offset + total.shape[0]] = total.astype(bf16)


def sums_of(wanted, after):
    inputs, specs, plan, shapes = [], [], [], []
    for pieces in wanted:
        offset, steps = 0, []
        for terms in pieces:
            indices = []
            for array, first, count in terms:
                indices.append(len(inputs))
                inputs.append(array)
                at = first // count
                specs.append(pl.BlockSpec((count,) + array.shape[1:], lambda i, at=at: (at, 0, 0)))
            steps.append((offset, indices))
            offset += terms[0][2]
        plan.append(steps)
        shapes.append((offset,) + pieces[0][0][0].shape[1:])
    return pl.pallas_call(
        functools.partial(drop_last, functools.partial(sums_kernel, plan), len(after), len(inputs)),
        grid=(1,),
        in_specs=specs + [ANY] * len(after),
        out_specs=[pl.BlockSpec(dims, lambda i: (0, 0, 0)) for dims in shapes],
        out_shape=[shape(dims, bf16) for dims in shapes],
        **params(16),
    )(*inputs, *after)


def drop_last(kernel, count, inputs, *refs):
    return kernel(*refs[:inputs], *refs[inputs + count :])


def gather_relative(value, axis, size):
    if size <= 8:
        return jnp.stack([value] + [xor_permute(value, axis, size, k) for k in range(1, size)])
    everyone = lax.all_gather(value, axis, axis=0)
    return jnp.take(everyone, jnp.arange(size) ^ lax.axis_index(axis), axis=0)


def absolute(stacked, own, bits):
    count = stacked.shape[0]
    for bit in range(bits):
        step = 1 << bit
        view = stacked.reshape((count // (2 * step), 2, step) + stacked.shape[1:])
        view = jnp.where((own >> bit) & 1 == 1, view[:, ::-1], view)
        stacked = view.reshape(stacked.shape)
    return stacked


def per_device(
    sizes,
    incoming_hidden_matrix,
    sequence_membership,
    matching_passages,
    softness_scale,
    combined_projection_matrix,
    mixer_projection_matrix,
    widening_matrix,
    gating_matrix,
    narrowing_matrix,
    mixer_scaling_factor,
    mixer_scaling_offset,
    perceptron_scaling_factor,
    perceptron_scaling_offset,
):
    nb, nf = sizes
    b, f = lax.axis_index("batch"), lax.axis_index("fsdp")
    x = incoming_hidden_matrix[0]
    segment = sequence_membership[0]
    T, D = x.shape
    FF = widening_matrix.shape[1]
    R = D // nf
    nblk = T // BLOCK
    y_bit = b & 1

    def tie(value, *others):
        return lax.optimization_barrier((value,) + others)[0]

    def own_half(own):
        rows = own.shape[0]
        return lax.dynamic_slice_in_dim(own, y_bit * (rows // 2), rows // 2, 0)

    def gather_far(own, beside, mine, other, *after):
        pair = join(y_bit.reshape(1), mine, other, *after)
        return (own, beside, pair, xor_permute(pair, "fsdp", nf, 1))

    marks = (segment[:, None] == jnp.arange(SEGS, dtype=jnp.int32)[None, :]).astype(jnp.int32)
    counts = jnp.sum(marks, axis=0)
    ends = jnp.cumsum(counts)
    firsts = ends - counts
    start_of = jnp.sum(marks * firsts[None, :], axis=1)
    end_of = jnp.sum(marks * ends[None, :], axis=1)
    positions = jnp.arange(T, dtype=jnp.int32) - start_of
    lane = jnp.arange(LANE)
    inverse = 1000.0 ** (-((lane % (HD // 2)).astype(f32) * 2.0) / HD)
    angles = positions.astype(f32)[:, None] * inverse[None, :]
    cosine, sine = jnp.cos(angles), jnp.where((lane % HD < HD // 2)[None, :], -1.0, 1.0) * jnp.sin(angles)
    same = segment[:, None] == jnp.arange(LANE, dtype=jnp.int32)[None, :]
    mask_q = same.astype(bf16)
    mask_k = jnp.where(same | (jnp.arange(LANE)[None, :] >= SEGS), 0.0, NEG).astype(bf16)
    mark_rows = (jnp.arange(16, dtype=jnp.int32)[:, None] == segment[None, :]).astype(bf16)
    lo = (start_of.reshape(nblk, BLOCK)[:, 0] // LANE).astype(jnp.int32)
    hi = ((end_of.reshape(nblk, BLOCK)[:, -1] + LANE - 1) // LANE).astype(jnp.int32)
    spans = hi - lo
    rows = combined_projection_matrix.shape[0]
    beyond = xor_permute(combined_projection_matrix, "fsdp", nf, 2)
    beside = xor_permute(combined_projection_matrix, "fsdp", nf, 1)
    both = jnp.concatenate([own_half(widening_matrix), own_half(mixer_projection_matrix)], axis=1)
    halves = [both, own_half(gating_matrix), own_half(narrowing_matrix)]
    vectors = jnp.stack(
        [mixer_scaling_factor, mixer_scaling_offset, perceptron_scaling_factor, perceptron_scaling_offset]
    )
    vectors = gather_relative(vectors, "fsdp", nf)
    beyond = tie(beyond, mask_q, mask_k, cosine, vectors, *halves)
    far = xor_permute(beyond, "fsdp", nf, 1)
    qkv_pieces = (combined_projection_matrix, beside, beyond, far)
    beside_all = [
        xor_permute(weight, "fsdp", nf, 1)
        for weight in (mixer_projection_matrix, widening_matrix, gating_matrix, narrowing_matrix)
    ]
    up_half = xor_permute(tie(halves[0], cosine, mask_q, mask_k), "fsdp", nf, 2)

    heads = (
        (jnp.arange(PAIRS * 8)[:, None] // 8 * 2 + jnp.arange(PAIRS * 8)[:, None] % 8 == jnp.arange(D)[None, :] // HD)
        & (jnp.arange(PAIRS * 8)[:, None] % 8 < 2)
    ).astype(bf16)
    count_rows = jnp.broadcast_to(counts.astype(f32)[:, None], (SEGS, LANE))

    def rowblk(width, rows=BLOCK):
        return pl.BlockSpec((rows, width), lambda i, *_: (i, 0))

    def colblk(height, cols=BLOCK):
        return pl.BlockSpec((height, cols), lambda i, *_: (0, i))

    whole_rows = jnp.stack([f * R, (f ^ 1) * R, (f ^ 2) * R, (f ^ 3) * R, f]).astype(jnp.int32)
    qkv, x_turned = pl.pallas_call(
        qkv_kernel,
        grid_spec=pltpu.PrefetchScalarGridSpec(
            num_scalar_prefetch=1,
            grid=(3,),
            in_specs=[whole((T, D)), whole((T, LANE)), whole((T, LANE))] + [ANY] * 5,
            out_specs=[pl.BlockSpec((T, D), lambda i, *_: (0, i)), whole((D, T))],
            scratch_shapes=[pltpu.VMEM((D, 3 * D), bf16), pltpu.SemaphoreType.DMA((4,))],
        ),
        out_shape=[shape((T, 3 * D), bf16), shape((D, T), bf16)],
        **params(60),
    )(whole_rows, x, cosine, sine, *qkv_pieces, vectors)

    vectors = absolute(vectors, f, 2)
    vectors = vectors.transpose(1, 0, 2).reshape(4, D).astype(f32)

    def attend(h, *after):
        def keys(part):
            return pl.BlockSpec((T, PART), lambda i, *_: (0, 2 * part + h))

        return pl.pallas_call(
            functools.partial(drop_last, attend_kernel, len(after), 7),
            grid_spec=pltpu.PrefetchScalarGridSpec(
                num_scalar_prefetch=2,
                grid=(nblk,),
                in_specs=[
                    pl.BlockSpec((BLOCK, PART), lambda i, *_: (i, h)),
                    keys(1),
                    keys(2),
                    rowblk(LANE),
                    whole((T, LANE)),
                ]
                + [ANY] * len(after),
                out_specs=[rowblk(PART), pl.BlockSpec((PAIRS // 2, 8, BLOCK), lambda i, *_: (0, 0, i))],
            ),
            out_shape=[shape((T, PART), bf16), shape((PAIRS // 2, 8, T), f32)],
            **params(14),
        )(lo, spans, qkv, qkv, qkv, mask_q, mask_k, *after)

    def onward(half, *before):
        half = tie(half, *before)
        return half, xor_permute(half, "batch", nb, 1)

    gate_half = xor_permute(tie(halves[1], qkv, up_half), "fsdp", nf, 2)
    up_half, up_other = onward(up_half, qkv)
    attended0, lse0 = attend(0, up_half)
    down_half = xor_permute(tie(halves[2], attended0, gate_half, up_other), "fsdp", nf, 2)
    gate_half, gate_other = onward(gate_half, attended0, up_other)
    up_pieces = gather_far(widening_matrix, beside_all[1], up_half, up_other, attended0, gate_half)
    attended1, lse1 = attend(1, gate_half, up_pieces[2])
    down_half, down_other = onward(down_half, attended1, gate_other)
    gate_pieces = gather_far(gating_matrix, beside_all[2], gate_half, gate_other, attended1, down_half)
    out_pieces = (mixer_projection_matrix, beside_all[0]) + up_pieces[2:]

    xhat1, inv1, low1, low1_turned, full_out = pl.pallas_call(
        mixer_kernel,
        grid_spec=pltpu.PrefetchScalarGridSpec(
            num_scalar_prefetch=1,
            grid=(nblk,),
            in_specs=[rowblk(PART), rowblk(PART), rowblk(D), whole((4, D))] + [ANY] * 6,
            out_specs=[rowblk(D), rowblk(LANE), rowblk(D), colblk(D), ANY],
            scratch_shapes=[pltpu.VMEM((D, D), bf16), pltpu.SemaphoreType.DMA((4,)), pltpu.SemaphoreType.DMA],
        ),
        out_shape=[shape((T, D), f32), shape((T, LANE), f32), shape((T, D), bf16), shape((D, T), bf16), shape((D, D), bf16)],
        **params(14),
    )(whole_rows, attended0, attended1, x, vectors, *out_pieces, down_half, gate_pieces[2])

    W = FF // nf
    down_pieces = gather_far(narrowing_matrix, beside_all[3], down_half, down_other, low1)
    up_fac, gate_fac, prod, xhat2, inv2, pool, embed, full_up, full_gate, full_down = pl.pallas_call(
        ffn_kernel,
        grid_spec=pltpu.PrefetchScalarGridSpec(
            num_scalar_prefetch=1,
            grid=(nf,),
            in_specs=[whole((T, D)), whole((T, D)), whole((4, D)), whole((16, T)), whole((SEGS, LANE))] + [ANY] * 12,
            out_specs=[pl.BlockSpec((T, W), lambda i, rows: (0, rows[4] ^ i))] * 3
            + [whole((T, D)), whole((T, LANE)), whole((2 * SEGS, D)), whole((SEGS, D))]
            + [ANY] * 3,
            scratch_shapes=[
                pltpu.VMEM((nf, D, W), bf16),
                pltpu.VMEM((nf, D, W), bf16),
                pltpu.VMEM((nf, W, D), bf16),
                pltpu.SemaphoreType.DMA((nf * 8,)),
                pltpu.SemaphoreType.DMA((nf,)),
                pltpu.SemaphoreType.DMA((nf * 3,)),
                pltpu.VMEM((16, D), f32),
                pltpu.VMEM((T, D), f32),
            ],
        ),
        out_shape=[shape((T, FF), bf16)] * 3
        + [shape((T, D), f32), shape((T, LANE), f32), shape((2 * SEGS, D), f32), shape((SEGS, D), bf16)]
        + [shape((D, FF), bf16), shape((D, FF), bf16), shape((FF, D), bf16)],
        **params(46),
    )(whole_rows, low1, xhat1, vectors, mark_rows, count_rows, *up_pieces, *gate_pieces, *down_pieces)

    ranks = nb * nf
    total_rows = ranks * SEGS
    target = jnp.concatenate([matching_passages[0], jnp.zeros((SEGS - QSEG,), jnp.int32)])
    digits = jnp.pad(jnp.stack([target >> 5, target & 31], axis=1), ((0, 0), (0, LANE - 2))).astype(bf16)
    sent = jnp.concatenate([embed, digits], axis=1)
    if nb == 8:
        everyone = jnp.stack([sent] + [xor_permute(sent, "batch", nb, 2 * z) for z in range(1, 4)])
        everyone = jnp.stack([everyone, xor_permute(everyone, "fsdp", nf, 2)], axis=1)
        everyone = jnp.stack([everyone, xor_permute(everyone, "batch", nb, 1)], axis=1)
        everyone = jnp.stack([everyone, xor_permute(everyone, "fsdp", nf, 1)], axis=3)
    else:
        everyone = gather_relative(gather_relative(sent, "fsdp", nf), "batch", nb)
    everyone = everyone.reshape(total_rows, D + LANE)
    rank_of = ((jnp.arange(nb)[:, None] ^ b) * nf + (jnp.arange(nf)[None, :] ^ f)).reshape(ranks, 1)
    place_of = jnp.arange(SEGS)[None, :]
    doc_ids = jnp.where(place_of >= QSEG, rank_of * (SEGS - QSEG) + place_of - QSEG, -1).reshape(1, total_rows)
    doc_ids = jnp.broadcast_to(doc_ids, (8, total_rows)).astype(f32)
    loss_rows, grad_rows, small_two = pl.pallas_call(
        loss_kernel,
        grid=(total_rows // BLOCK,),
        in_specs=[
            pl.BlockSpec(memory_space=pltpu.SMEM),
            rowblk(D + LANE),
            whole((total_rows, D + LANE)),
            whole((8, total_rows)),
            whole((2 * SEGS, D)),
            whole((SEGS, LANE)),
        ],
        out_specs=[whole((SEGS, LANE)), whole((LANE, D)), whole((8, D))],
        out_shape=[shape((SEGS, LANE), f32), shape((LANE, D), f32), shape((8, D), f32)],
        scratch_shapes=[pltpu.VMEM((SEGS, D), f32)],
        **params(8),
    )(softness_scale.reshape(1), everyone, everyone, doc_ids, pool, count_rows)
    query_loss = loss_rows[:QSEG, 0].reshape(1, QSEG)

    sum_two, grad_low, grad_low_turned = pl.pallas_call(
        norm_two_back_kernel,
        grid=(nblk,),
        in_specs=[rowblk(LANE), whole((LANE, D)), rowblk(D), rowblk(LANE), whole((4, D))],
        out_specs=[rowblk(D), rowblk(D), colblk(D)],
        out_shape=[shape((T, D), f32), shape((T, D), bf16), shape((D, T), bf16)],
        **params(12),
    )(mask_q, grad_rows, xhat2, inv2, vectors)

    def add(*terms):
        return sum([term.astype(f32) for term in terms]).astype(bf16)

    def across(value, axis):
        if axis == "x":
            return xor_permute(value, "fsdp", nf, 2)
        return xor_permute(value, "batch", nb, 1 << BIT[axis])

    def over_batch(total):
        total = lax.psum(total.astype(f32), "batch").astype(bf16)
        return [total[:4], total[4:]]

    class Reduce:
        def __init__(self, order, keep, send):
            self.order, self.left, self.stage = order, 16, 0
            self.terms = [[[0, keep]], [[0, xor_permute(send, "fsdp", nf, 1)]]]
            self.arriving, self.pending = [], []

        def pick(self, low, high):
            found = []
            for term in self.terms:
                for start, array in term:
                    if array is not None and start <= low and high <= start + array.shape[0]:
                        found.append((array, low - start, high - low))
                        break
            return found

        def wanted(self, which):
            if which == "back":
                rest = [axis for axis in self.order if axis != "x"]
                self.pending.append((rest[6 - self.stage], None))
                self.stage += 1
                return [self.pick(0, 1)] if self.stage == 5 else [[(part, 0, part.shape[0])] for part in self.parts]
            half = self.left // 2
            middle = half + half // 2
            low, high = dict(all=(half, self.left), far=(middle, self.left), near=(half, middle))[which]
            sums = [self.pick(low, high)]
            arrival = [low - half, None]
            self.pending.append((self.order[self.stage], arrival))
            self.arriving.append(arrival)
            if which != "far":
                self.terms.append(self.arriving)
                self.arriving, self.left, self.stage = [], half, self.stage + 1
            return sums

        def go(self, out):
            axis, arrival = self.pending.pop(0)
            got = across(out, axis)
            if arrival is None:
                self.parts = [out, got]
            else:
                arrival[1] = got
            return got

    orders = [
        ("x", "z0", "y", "z1"),
        ("y", "x", "z0", "z1"),
        ("x", "y", "z0", "z1"),
        ("x", "z0", "y", "z1"),
        ("x", "y", "z0", "z1"),
    ]
    if nb != 8:
        orders = [("x", "y", "z0", "z1")] * 5

    def plain_sum(pieces, after):
        made = []
        for terms in pieces:
            arrays = [tie(array, *after) if after else array for array, _, _ in terms[-1:]]
            arrays = [array for array, _, _ in terms[:-1]] + arrays
            made.append(add(*[array[first : first + count] for array, (_, first, count) in zip(arrays, terms, strict=True)]))
        return made[0] if len(made) == 1 else jnp.concatenate(made, axis=0)

    def slot(after, *sends, apart=False):
        if nb != 8:
            sends = [
                (group, which)
                for k, (group, which) in enumerate(sends)
                if group.stage == 0 and not any(other is group and kind != "far" for other, kind in sends[:k])
            ]
        if not sends:
            return [], []
        wanted = [group.wanted(which) for group, which in sends]
        made = [plain_sum(pieces, after) for pieces in wanted] if apart else sums_of(wanted, after)
        gots = [group.go(out) for (group, _), out in zip(sends, made, strict=True)]
        for group, _ in sends:
            if nb != 8 and group.stage == 1 and not hasattr(group, "parts"):
                total = sum([array[first : first + count].astype(f32) for array, first, count in group.pick(0, 8)])
                group.parts = over_batch(total)
        return list(made), gots

    own_part = b if nb == 8 else 0
    info = jnp.stack([f, f ^ 1, f ^ 2, f ^ 3, own_part + 0 * f]).astype(jnp.int32)
    groups = W // BLOCK

    wide = nf * BLOCK

    def ffn_back(g, *after):
        parts = (16, R, PART)
        return pl.pallas_call(
            functools.partial(ffn_back_kernel, g, orders[g], groups),
            grid_spec=pltpu.PrefetchScalarGridSpec(
                num_scalar_prefetch=1,
                grid=(1,),
                in_specs=[ANY] * (7 + len(after)),
                out_specs=[ANY] * 4,
                scratch_shapes=[pltpu.VMEM((T, wide), bf16)] * 3
                + [pltpu.VMEM((T, D), bf16), pltpu.VMEM((D, T), bf16), pltpu.VMEM((D, T), bf16)]
                + [pltpu.VMEM((wide, D), bf16), pltpu.VMEM((2, T, wide), bf16)]
                + [pltpu.VMEM(parts, bf16)] * 2
                + [pltpu.SemaphoreType.DMA((20,)), pltpu.SemaphoreType.DMA((4,))],
            ),
            out_shape=[shape((T, wide), bf16)] * 2 + [shape(parts, bf16)] * 2,
            **params(38),
        )(info, prod, up_fac, gate_fac, grad_low, grad_low_turned, low1_turned, full_down, *after)

    dup0, dgate0, keep, send = ffn_back(0)
    r0 = Reduce(orders[0], keep, send)
    dup1, dgate1, keep, send = ffn_back(1, send)
    r1 = Reduce(orders[1], keep, send)
    outs, gots = slot([dup1], (r0, "far"))
    dup2, dgate2, keep, send = ffn_back(2, send, *outs)
    r2 = Reduce(orders[2], keep, tie(send, *gots))
    outs, gots = slot([dup2] + gots, (r0, "near"), (r0, "all"), (r1, "far"))
    grad_hidden = pl.pallas_call(
        functools.partial(ffn_input_back_kernel, groups),
        in_specs=[ANY] * (3 + 2 * groups + len(outs)),
        out_specs=ANY,
        scratch_shapes=[
            pltpu.VMEM((2 * groups, T, wide), bf16),
            pltpu.VMEM((groups, D, wide), bf16),
            pltpu.VMEM((groups, D, wide), bf16),
            pltpu.VMEM((T, D), f32),
            pltpu.SemaphoreType.DMA((groups * 10 + 1,)),
            pltpu.SemaphoreType.DMA,
        ],
        out_shape=shape((T, D), f32),
        **params(36),
    )(full_up, full_gate, sum_two, dup0, dgate0, dup1, dgate1, dup2, dgate2, *outs)
    outs, gots = slot([grad_hidden] + gots, (r0, "all"), (r1, "near"), (r1, "all"), (r2, "far"))

    sum_one, grad_branch, grad_att, delta, att_turned, small = pl.pallas_call(
        mixer_back_kernel,
        grid_spec=pltpu.PrefetchScalarGridSpec(
            num_scalar_prefetch=1,
            grid=(nblk,),
            in_specs=[
                rowblk(D),
                rowblk(D),
                rowblk(LANE),
                whole((4, D)),
                rowblk(PART),
                rowblk(PART),
                whole((D, D)),
                whole((PAIRS * 8, D)),
                whole((8, D)),
            ]
            + [ANY] * len(outs),
            out_specs=[
                rowblk(D),
                rowblk(D),
                rowblk(D),
                pl.BlockSpec((PAIRS, 8, BLOCK), lambda i, *_: (0, 0, i)),
                colblk(D),
                whole((nf, 2, SMALL, PART)),
            ],
            scratch_shapes=[pltpu.VMEM((8, D), f32)],
        ),
        out_shape=[
            shape((T, D), f32),
            shape((T, D), bf16),
            shape((T, D), bf16),
            shape((PAIRS, 8, T), f32),
            shape((D, T), bf16),
            shape((nf, 2, SMALL, PART), f32),
        ],
        **params(16),
    )(info, grad_hidden, xhat1, inv1, vectors, attended0, attended1, full_out, heads, small_two, *outs)
    def attend_back(h, *after):
        def cols(part, rows=None):
            at = 2 * part + h
            return pl.BlockSpec((rows or T, PART), (lambda i, *_: (i, at)) if rows else (lambda i, *_: (0, at)))

        kernel = functools.partial(drop_last, attend_back_kernel, len(after), 14)
        return pl.pallas_call(
            kernel,
            grid_spec=pltpu.PrefetchScalarGridSpec(
                num_scalar_prefetch=2,
                grid=(nblk,),
                in_specs=[
                    cols(0),
                    cols(1, BLOCK),
                    cols(2, BLOCK),
                    cols(0),
                    whole((PAIRS // 2, 8, T)),
                    pl.BlockSpec((PAIRS // 2, 8, T), lambda i, *_: (h, 0, 0)),
                    whole((T, LANE)),
                    rowblk(LANE),
                    whole((T, LANE)),
                    whole((T, LANE)),
                    rowblk(LANE),
                    rowblk(LANE),
                ]
                + [ANY] * len(after),
                out_specs=[whole((T, PART)), rowblk(PART), rowblk(PART)],
                scratch_shapes=[pltpu.VMEM((PART, T), f32)],
            ),
            out_shape=[shape((T, PART), bf16)] * 3,
            **params(16),
        )(lo, spans, qkv, qkv, qkv, grad_att, (lse0, lse1)[h], delta, mask_q, mask_k, cosine, sine, cosine, sine, *after)

    def qkv_back(h, grads, extra, *after):
        dims = (16, R // 2 + extra, PART)
        return pl.pallas_call(
            functools.partial(qkv_back_kernel, extra, orders[3 + h]),
            grid_spec=pltpu.PrefetchScalarGridSpec(
                num_scalar_prefetch=1,
                grid=(4,),
                in_specs=[whole((D, T)), whole((D, T))]
                + [whole((T, PART))] * 3
                + [pl.BlockSpec((T, PART), lambda c, *_: (0, h)), whole((nf, 2, SMALL, PART))]
                + [ANY] * len(after),
                out_specs=[whole(dims)] * 2,
            ),
            out_shape=[shape(dims, bf16)] * 2,
            **params(18),
        )(info, x_turned, att_turned, *grads, grad_branch, small, *after)

    grads0 = attend_back(0)
    outs, gots = slot([grads0[0]] + gots, (r2, "near"), (r2, "far"), (r0, "all"), (r1, "all"))
    keep, send = qkv_back(0, grads0, SMALL, *outs)
    r3 = Reduce(orders[3], keep, tie(send, *gots))
    outs, gots = slot([keep] + gots, (r0, "back"), (r1, "all"), (r2, "near"), (r2, "all"), (r3, "all"))
    grads1 = attend_back(1, *outs)
    outs, gots = slot([grads1[0]] + gots, (r0, "back"), (r1, "back"), (r2, "all"), (r3, "all"))
    keep, send = qkv_back(1, grads1, 0, *outs)
    r4 = Reduce(orders[4], keep, tie(send, *gots))
    outs, gots = slot([keep] + gots, (r0, "back"), (r1, "back"), (r2, "back"), (r3, "all"))
    more = slot([], (r4, "all"), apart=True)
    outs = outs + more[0]

    grad_input = pl.pallas_call(
        input_back_kernel,
        grid_spec=pltpu.PrefetchScalarGridSpec(
            num_scalar_prefetch=1,
            grid=(nblk,),
            in_specs=[rowblk(PART)] * 6 + [rowblk(D)] + [ANY] * (4 + len(outs)),
            out_specs=rowblk(D),
            scratch_shapes=[pltpu.VMEM((D, 3 * D), bf16), pltpu.SemaphoreType.DMA((4,))],
        ),
        out_shape=shape((T, D), f32),
        **params(16),
    )(whole_rows, *grads0, *grads1, sum_one, *qkv_pieces, *outs)

    outs, _ = slot([grad_input], (r4, "all"), apart=True)
    slot(outs, (r1, "back"), (r2, "back"), (r3, "all"), apart=True)
    outs, _ = slot([], (r4, "all"), apart=True)
    slot(outs, (r2, "back"), (r3, "back"), apart=True)
    outs, _ = slot([], (r4, "all"), apart=True)
    slot(outs, (r3, "back"), apart=True)
    outs, _ = slot([], (r4, "back"), apart=True)
    slot(outs, (r3, "back"), apart=True)
    slot([], (r4, "back"), apart=True)
    slot([], (r4, "back"), apart=True)
    sum_up, sum_gate, sum_down = pl.pallas_call(
        functools.partial(ffn_out_kernel, (r0.order, r1.order, r2.order)),
        grid_spec=pltpu.PrefetchScalarGridSpec(
            num_scalar_prefetch=1,
            grid=(1,),
            in_specs=[whole((4, R, PART))] * (2 * groups),
            out_specs=[whole((R, FF)), whole((R, FF)), whole((W, D))],
        ),
        out_shape=[shape((R, FF), f32), shape((R, FF), f32), shape((W, D), f32)],
        **params(26),
    )(info, *r0.parts, *r1.parts, *r2.parts)
    sum_qkv, sum_out, sum_small = pl.pallas_call(
        functools.partial(qkv_out_kernel, (r3.order, r4.order)),
        grid_spec=pltpu.PrefetchScalarGridSpec(
            num_scalar_prefetch=1,
            grid=(1,),
            in_specs=[whole((4, R // 2 + SMALL, PART))] * 2 + [whole((4, R // 2, PART))] * 2,
            out_specs=[whole((R, 3 * D)), whole((R, D)), whole((16, PART))],
        ),
        out_shape=[shape((R, 3 * D), f32), shape((R, D), f32), shape((16, PART), f32)],
        **params(16),
    )(info, *r3.parts, *r4.parts)
    return (
        query_loss,
        grad_input[None],
        sum_qkv,
        sum_out,
        sum_up,
        sum_gate,
        sum_down,
        sum_small[0, :R],
        sum_small[0, R : 2 * R],
        sum_small[8, :R],
        sum_small[8, R : 2 * R],
    )


def solution(mesh):
    sizes = (mesh.shape["batch"], mesh.shape["fsdp"])
    return jax.shard_map(
        functools.partial(per_device, sizes),
        mesh=mesh,
        in_specs=(
            P(("batch", "fsdp"), None, None),
            P(("batch", "fsdp"), None),
            P(("batch", "fsdp"), None),
            P(),
            P("fsdp", None),
            P("fsdp", None),
            P("fsdp", None),
            P("fsdp", None),
            P("fsdp", None),
            P("fsdp"),
            P("fsdp"),
            P("fsdp"),
            P("fsdp"),
        ),
        out_specs=(
            P(("batch", "fsdp"), None),
            P(("batch", "fsdp"), None, None),
            P("fsdp", None),
            P("fsdp", None),
            P("fsdp", None),
            P("fsdp", None),
            P("fsdp", None),
            P("fsdp"),
            P("fsdp"),
            P("fsdp"),
            P("fsdp"),
        ),
        check_vma=False,
    )
```

```python
import functools
import math

import jax
import jax.numpy as jnp
from jax import lax
from jax.experimental import pallas as pl
from jax.experimental.pallas import tpu as pltpu
from jax.sharding import PartitionSpec as P

HEADS = 12
HD = 64
QSEG = 4
SEGS = 8
EPSILON = 1e-06
NEG = -1e30
LANE = 128
BLOCK = 256
PAIRS = HEADS // 2
PART = 384
SMALL = 16
MIB = 2**20

bf16 = jnp.bfloat16
f32 = jnp.float32


def dot(left, right, left_dim, right_dim):
    return lax.dot_general(
        left, right, (((left_dim,), (right_dim,)), ((), ())), preferred_element_type=f32
    )


def split_three(value):
    high = value.astype(bf16)
    rest = value - high.astype(f32)
    middle = rest.astype(bf16)
    low = (rest - middle.astype(f32)).astype(bf16)
    return high, middle, low


def params(limit=60):
    return dict(
        compiler_params=pltpu.CompilerParams(vmem_limit_bytes=limit * MIB),
        cost_estimate=pl.CostEstimate(flops=1, bytes_accessed=1, transcendentals=0),
    )


def shape(dims, dtype):
    return jax.ShapeDtypeStruct(dims, dtype)


ANY = pl.BlockSpec(memory_space=pl.ANY)


def whole(dims):
    return pl.BlockSpec(dims, lambda *_: (0,) * len(dims), pipeline_mode=pl.Buffered(1))


def swap_halves(tile):
    lane = lax.broadcasted_iota(jnp.int32, (1, LANE), 1)
    in_first = (lane & 63) < 32
    return jnp.where(in_first, pltpu.roll(tile, 96, 1), pltpu.roll(tile, 32, 1))


def norm_parts(value):
    center = value - jnp.mean(value, axis=1, keepdims=True)
    spread = jnp.mean(center * center, axis=1, keepdims=True)
    inv = lax.rsqrt(spread + EPSILON)
    return center * inv, inv


def norm_back(scaled, xhat, inv):
    mean_one = jnp.mean(scaled, axis=1, keepdims=True)
    mean_two = jnp.mean(scaled * xhat, axis=1, keepdims=True)
    return inv * (scaled - mean_one - xhat * mean_two)


def piece_copies(row_of, pieces, scratch, sems):
    return [
        pltpu.make_async_copy(
            piece, scratch.at[pl.ds(pl.multiple_of(row_of(k), 32), piece.shape[0])], sems.at[k]
        )
        for k, piece in enumerate(pieces)
    ]


def store_turned(ref, value, own, columns=slice(None)):
    rows = ref.shape[0] // 4
    turned = value.T
    for shard in range(4):
        at = pl.ds(pl.multiple_of((shard ^ own) * rows, 64), rows)
        ref[at, columns] = turned[shard * rows : (shard + 1) * rows]


def qkv_kernel(rows_ref, x_ref, cos_ref, sin_ref, *refs):
    pieces = refs[:4]
    out_ref, xt_ref, weight, sems = refs[-4:]
    step = pl.program_id(0)
    width = x_ref.shape[1]

    @pl.when(step == 0)
    def _():
        copies = piece_copies(lambda k: rows_ref[k], pieces, weight, sems)
        for copy in copies:
            copy.start()
        store_turned(xt_ref, x_ref[...], rows_ref[4])
        for copy in copies:
            copy.wait()

    joined = dot(x_ref[...], weight[:, pl.ds(pl.multiple_of(step * width, LANE), width)], 1, 0)

    @pl.when(step < 2)
    def _():
        scale = jnp.where(step == 0, 1.0 / math.sqrt(HD), 1.0)
        cos, sin = cos_ref[...] * scale, sin_ref[...] * scale
        for t in range(width // LANE):
            tile = joined[:, t * LANE : (t + 1) * LANE]
            out_ref[:, t * LANE : (t + 1) * LANE] = (tile * cos + swap_halves(tile) * sin).astype(bf16)

    @pl.when(step == 2)
    def _():
        out_ref[...] = joined.astype(bf16)


def key_range(first, count, total):
    blocks = (count + 1) >> 1
    first = jnp.minimum(first, total // LANE - 2 * blocks)
    return pl.multiple_of(first * LANE, LANE), blocks


def attend_kernel(lo_ref, n_ref, q_ref, k_ref, v_ref, mq_ref, mk_ref, o_ref, lse_ref):
    step = pl.program_id(0)
    lo, count = key_range(lo_ref[step], n_ref[step], k_ref.shape[0])
    first = lax.broadcasted_iota(jnp.int32, (1, LANE), 1) < HD
    zero = jnp.zeros((), bf16)
    mask_q = mq_ref[...]

    def run(width):
        keys = pl.ds(lo, width)
        mask_k = mk_ref[keys, :]

        def pair(p, _):
            cols = pl.ds(pl.multiple_of(p * LANE, LANE), LANE)
            q_pair, k_pair, v_pair = q_ref[:, cols], k_ref[keys, cols], v_ref[keys, cols]
            k_ext = jnp.concatenate([k_pair, mask_k], axis=1)
            outs, sums = [], []
            for h in range(2):
                q_one = jnp.where(first if h == 0 else ~first, q_pair, zero)
                scores = dot(jnp.concatenate([q_one, mask_q], axis=1), k_ext, 1, 1)
                peak = jnp.max(scores, axis=1, keepdims=True)
                weight = jnp.exp(scores - peak)
                total = jnp.sum(weight, axis=1, keepdims=True)
                outs.append(dot(weight.astype(bf16), v_pair, 1, 0) * (1.0 / total))
                sums.append(peak + jnp.log(total))
            o_ref[:, cols] = jnp.where(first, outs[0], outs[1]).astype(bf16)
            turned = jnp.where(first, sums[0], sums[1]).T
            lse_ref[p, 0:1, :] = turned[0:1]
            lse_ref[p, 1:2, :] = turned[HD : HD + 1]
            return 0

        lax.fori_loop(0, PAIRS // 2, pair, 0, unroll=True)

    for n in range(1, k_ref.shape[0] // BLOCK + 1):
        pl.when(count == n)(functools.partial(run, n * BLOCK))


def attend_back_kernel(
    lo_ref, n_ref, q_ref, k_ref, v_ref, do_ref, lse_ref, dl_ref, mq_ref, mk_ref, cos_ref, sin_ref, cosb_ref, sinb_ref,
    gq_ref, gk_ref, gv_ref, dq_acc,
):
    step = pl.program_id(0)

    @pl.when(step == 0)
    def _():
        dq_acc[...] = jnp.zeros_like(dq_acc)

    lo, count = key_range(lo_ref[step], n_ref[step], q_ref.shape[0])
    first = lax.broadcasted_iota(jnp.int32, (1, LANE), 1) < HD
    zero = jnp.zeros((), bf16)
    mask_k = mk_ref[...]
    cosb, sinb = cosb_ref[...], sinb_ref[...]

    def run(width):
        queries = pl.ds(lo, width)
        mask_q = mq_ref[queries, :]

        def pair(p, _):
            cols = pl.ds(pl.multiple_of(p * LANE, LANE), LANE)
            k_pair, v_pair = k_ref[:, cols], v_ref[:, cols]
            q_pair, do_pair = q_ref[queries, cols], do_ref[queries, cols]
            q_ext = jnp.concatenate([q_pair, mask_q], axis=1)
            k_turned = k_pair.T
            dk, dv = [], []
            for h in range(2):
                mine = first if h == 0 else ~first
                k_one, v_one = jnp.where(mine, k_pair, zero), jnp.where(mine, v_pair, zero)
                scores = dot(jnp.concatenate([k_one, mask_k], axis=1), q_ext, 1, 1)
                probs = jnp.exp(scores - lse_ref[p, h : h + 1, queries])
                dprobs = dot(v_one, do_pair, 1, 1)
                dscores = (probs * (dprobs - dl_ref[p, h : h + 1, queries])).astype(bf16)
                dv.append(dot(probs.astype(bf16), do_pair, 1, 0))
                dk.append(dot(dscores, q_pair, 1, 0))
                rows = pl.ds(pl.multiple_of(p * LANE + h * HD, HD), HD)
                dq_acc[rows, queries] += dot(k_turned[h * HD : (h + 1) * HD], dscores, 1, 0)
            gv_ref[:, cols] = jnp.where(first, dv[0], dv[1]).astype(bf16)
            grad = jnp.where(first, dk[0], dk[1])
            gk_ref[:, cols] = (grad * cosb - swap_halves(grad) * sinb).astype(bf16)
            return 0

        lax.fori_loop(0, PAIRS // 2, pair, 0, unroll=True)

    for n in range(1, q_ref.shape[0] // BLOCK + 1):
        pl.when(count == n)(functools.partial(run, n * BLOCK))

    @pl.when(step == pl.num_programs(0) - 1)
    def _():
        cos, sin = cos_ref[...], sin_ref[...]
        for p in range(PAIRS // 2):
            grad = dq_acc[p * LANE : (p + 1) * LANE, :].T * (1.0 / math.sqrt(HD))
            gq_ref[:, p * LANE : (p + 1) * LANE] = (grad * cos - swap_halves(grad) * sin).astype(bf16)


def mixer_kernel(rows_ref, att0_ref, att1_ref, x_ref, vec_ref, *refs):
    xhat_ref, inv_ref, low_ref, lowt_ref, full_ref, weight, sems, out_sem = refs[-8:]
    width = weight.shape[1]
    pieces = list(refs[:2]) + [piece.at[:, pl.ds(piece.shape[1] - width, width)] for piece in refs[2:4]]
    step = pl.program_id(0)
    out_copy = pltpu.make_async_copy(weight, full_ref, out_sem)

    @pl.when(step == 0)
    def _():
        copies = piece_copies(lambda k: rows_ref[k], pieces, weight, sems)
        for copy in copies:
            copy.start()
        for copy in copies:
            copy.wait()
        out_copy.start()

    branch = dot(att0_ref[...], weight[0:PART, :], 1, 0) + dot(att1_ref[...], weight[PART:, :], 1, 0)
    xhat, inv = norm_parts(x_ref[...].astype(f32) + branch)
    low = (xhat * vec_ref[0:1] + vec_ref[1:2]).astype(bf16)
    xhat_ref[...] = xhat
    inv_ref[...] = jnp.broadcast_to(inv, inv_ref.shape)
    low_ref[...] = low
    store_turned(lowt_ref, low, rows_ref[4])

    @pl.when(step == pl.num_programs(0) - 1)
    def _():
        out_copy.wait()


def ffn_kernel(rows_ref, low_ref, xhat_ref, vec_ref, mark_ref, cnt_ref, *refs):
    up_pieces, gate_pieces, down_pieces = refs[0:4], refs[4:8], refs[8:12]
    up_fac_ref, gate_fac_ref, prod_ref, xhat2_ref, inv2_ref, pool_ref, emb_ref = refs[12:19]
    full_up, full_gate, full_down = refs[19:22]
    w_up, w_gate, w_down, sems, down_sems, out_sems, pooled, total = refs[22:]
    step = pl.program_id(0)
    own = rows_ref[4]
    tokens, width = low_ref.shape
    wide = prod_ref.shape[1]
    steps = 4

    def in_copies(rel):
        cols = pl.ds(pl.multiple_of((own ^ rel) * wide, LANE), wide)
        copies = []
        for which, (pieces, scratch) in enumerate(((up_pieces, w_up), (gate_pieces, w_gate))):
            for k, piece in enumerate(pieces):
                rows = pl.ds(pl.multiple_of(rows_ref[k], 32), piece.shape[0])
                copies.append(
                    pltpu.make_async_copy(piece.at[:, cols], scratch.at[rel, rows], sems.at[rel * 8 + which * 4 + k])
                )
        copies.append(pltpu.make_async_copy(down_pieces[rel], w_down.at[rel], down_sems.at[rel]))
        return copies

    def out_copies(rel):
        cols = pl.ds(pl.multiple_of((own ^ rel) * wide, LANE), wide)
        return [
            pltpu.make_async_copy(w_up.at[rel], full_up.at[:, cols], out_sems.at[rel * 3]),
            pltpu.make_async_copy(w_gate.at[rel], full_gate.at[:, cols], out_sems.at[rel * 3 + 1]),
            pltpu.make_async_copy(w_down.at[rel], full_down.at[cols], out_sems.at[rel * 3 + 2]),
        ]

    @pl.when(step == 0)
    def _():
        for rel in range(2):
            for copy in in_copies(rel):
                copy.start()
        pooled[...] = jnp.zeros_like(pooled)

    for rel in range(steps):

        @pl.when(step == rel)
        def _(rel=rel):
            for copy in in_copies(rel):
                copy.wait()
            for copy in out_copies(rel):
                copy.start()
            if 0 < rel < steps - 1:
                for copy in in_copies(rel + 1):
                    copy.start()

    rows_at = 512

    def rows_block(i, _):
        rows = pl.ds(pl.multiple_of(i * rows_at, rows_at), rows_at)
        low = low_ref[rows, :]
        up = dot(low, w_up[step], 1, 0)
        gate = dot(low, w_gate[step], 1, 0)
        sig = 0.5 * jnp.tanh(0.5 * gate) + 0.5
        act = gate * sig
        up_fac_ref[rows, :] = act.astype(bf16)
        gate_fac_ref[rows, :] = (up * (sig + act * (1.0 - sig))).astype(bf16)
        prod = (act * up).astype(bf16)
        prod_ref[rows, :] = prod
        ffn = dot(prod, w_down[step], 1, 0)

        total[rows, :] = jnp.where(step == 0, ffn, total[rows, :] + ffn)
        return 0

    lax.fori_loop(0, tokens // rows_at, rows_block, 0, unroll=True)

    @pl.when(step == steps - 1)
    def _():
        def norm_block(i, _):
            rows = pl.ds(pl.multiple_of(i * BLOCK, BLOCK), BLOCK)
            xhat, inv = norm_parts(xhat_ref[rows, :] * vec_ref[0:1] + vec_ref[1:2] + total[rows, :])
            xhat2_ref[rows, :] = xhat
            inv2_ref[rows, :] = jnp.broadcast_to(inv, (BLOCK, LANE))
            marks = mark_ref[:, rows]
            part = jnp.zeros(pooled.shape, f32)
            for piece in split_three(xhat):
                part += dot(marks, piece, 1, 0)
            pooled[...] += part
            return 0

        lax.fori_loop(0, tokens // BLOCK, norm_block, 0)
        mean_xhat = pooled[0:SEGS] / cnt_ref[:, 0:1]
        pool = mean_xhat * vec_ref[2:3] + vec_ref[3:4]
        inv_len = lax.rsqrt(jnp.sum(pool * pool, axis=1, keepdims=True) + EPSILON)
        pool_ref[0:SEGS] = mean_xhat
        pool_ref[SEGS:] = pool
        emb_ref[...] = (pool * inv_len).astype(bf16)
        for rel in range(steps):
            for copy in out_copies(rel):
                copy.wait()


def loss_kernel(soft_ref, blk_ref, all_ref, ids_ref, pool_ref, cnt_ref, loss_ref, rows_ref, small_ref, acc):
    step = pl.program_id(0)
    soft = soft_ref[0]
    width = acc.shape[1]
    block, everyone = blk_ref[:, 0:width], all_ref[:, 0:width]
    target = blk_ref[:, width : width + LANE].astype(f32)
    target = target[:, 0:1] * 32.0 + target[:, 1:2]
    row = lax.broadcasted_iota(jnp.int32, (block.shape[0], 1), 0)
    asks = (row & (SEGS - 1)) < QSEG
    ids = ids_ref[0:1, :]
    logits = jnp.where(ids >= 0, dot(block, everyone, 1, 1) / soft, NEG)
    hit = asks & (target == ids)
    peak = jnp.max(logits, axis=1, keepdims=True)
    lse = peak + jnp.log(jnp.sum(jnp.exp(logits - peak), axis=1, keepdims=True))
    grad = (jnp.exp(logits - lse) - jnp.where(hit, 1.0, 0.0)) / soft
    grad = jnp.where(asks, grad, 0.0)
    turned = grad[:, 0:LANE].T[0:SEGS]
    part = jnp.zeros(acc.shape, f32)
    for piece in split_three(turned):
        part += dot(piece, block, 1, 0)

    @pl.when(step == 0)
    def _():
        own = part
        for piece in split_three(grad[0:SEGS]):
            own += dot(piece, everyone, 1, 0)
        acc[...] = own
        chosen = jnp.sum(jnp.where(hit, logits, 0.0), axis=1, keepdims=True)
        loss_ref[...] = jnp.broadcast_to((lse - chosen)[0:SEGS], loss_ref.shape)

    @pl.when(step > 0)
    def _():
        acc[...] += part

    @pl.when(step == pl.num_programs(0) - 1)
    def _():
        g = acc[...]
        mean_xhat, pool = pool_ref[0:SEGS], pool_ref[SEGS:]
        inv_len = lax.rsqrt(jnp.sum(pool * pool, axis=1, keepdims=True) + EPSILON)
        back = inv_len * g - inv_len * inv_len * inv_len * pool * jnp.sum(pool * g, axis=1, keepdims=True)
        rows_ref[...] = jnp.zeros_like(rows_ref)
        rows_ref[0:SEGS] = back / cnt_ref[:, 0:1]
        small_ref[...] = jnp.zeros_like(small_ref)
        small_ref[0:1] = jnp.sum(back * mean_xhat, axis=0, keepdims=True)
        small_ref[1:2] = jnp.sum(back, axis=0, keepdims=True)


def norm_two_back_kernel(mq_ref, rows_ref, xhat_ref, inv_ref, vec_ref, sum_ref, low_ref, lowt_ref):
    marks = mq_ref[...]
    scaled = jnp.zeros(xhat_ref.shape, f32)
    for piece in split_three(rows_ref[...] * vec_ref[2:3]):
        scaled += dot(marks, piece, 1, 0)
    grad = norm_back(scaled, xhat_ref[...], inv_ref[:, 0:1])
    sum_ref[...] = grad
    low = grad.astype(bf16)
    low_ref[...] = low
    lowt_ref[...] = low.T


BIT = dict(y=0, z0=1, z1=2)


def part_index(order, x, away):
    at = 0
    for axis in order:
        if axis == "z":
            at = at * 4 + (away >> 1)
        else:
            at = at * 2 + (x if axis == "x" else (away >> BIT[axis]) & 1)
    return at


def strips(source, to, sems, first, groups, g, shards, by_rows=False):
    copies = []
    for k, shard in enumerate(shards):
        at = (shard * groups + g) * BLOCK
        here = pl.ds(at if isinstance(at, int) else pl.multiple_of(at, BLOCK), BLOCK)
        there = pl.ds(k * BLOCK, BLOCK)
        if by_rows:
            copies.append(pltpu.make_async_copy(source.at[here], to.at[there], sems.at[first + k]))
        else:
            copies.append(pltpu.make_async_copy(source.at[:, here], to.at[:, there], sems.at[first + k]))
    return copies


def ffn_back_kernel(
    g, order, groups, info_ref, prod_any, up_fac_any, gate_fac_any, low_any, lowt_any, hidt_any, wd_any, *refs
):
    dup_any, dgate_any, keep_any, send_any = refs[-16:-12]
    prod, up_fac, gate_fac, low, lowt, hidt, wd, dups, keep, send, sems, out_sems = refs[-12:]
    own = info_ref[4]
    rows = keep.shape[1]
    targets = [(keep, 0), (send, 0), (keep, 1), (send, 1)]

    def one(source, to, first):
        return [pltpu.make_async_copy(source, to, sems.at[first])]

    plain = range(4)
    loads = dict(
        low=one(low_any, low, 0),
        wd=strips(wd_any, wd, sems, 4, groups, g, plain, by_rows=True),
        up_fac=strips(up_fac_any, up_fac, sems, 8, groups, g, plain),
        hidt=one(hidt_any, hidt, 1),
        gate_fac=strips(gate_fac_any, gate_fac, sems, 12, groups, g, plain),
        lowt=one(lowt_any, lowt, 2),
        prod=strips(prod_any, prod, sems, 16, groups, g, [info_ref[k] for k in range(4)]),
    )
    for copies in loads.values():
        for copy in copies:
            copy.start()

    def arrive(*names):
        for name in names:
            for copy in loads[name]:
                copy.wait()

    def store(rel, tile, value):
        ref, across = targets[rel]
        at = part_index(order, across, (tile // 3) ^ own)
        ref[at, :, tile % 3 * LANE : (tile % 3 + 1) * LANE] = value.astype(bf16)

    def store_columns(kind, value):
        for rel in range(4):
            for t in range(8):
                store(rel, kind * 8 + t, value[rel * rows : (rel + 1) * rows, t * LANE : (t + 1) * LANE])

    outs = [
        pltpu.make_async_copy(dups.at[0], dup_any, out_sems.at[0]),
        pltpu.make_async_copy(dups.at[1], dgate_any, out_sems.at[1]),
        pltpu.make_async_copy(send, send_any, out_sems.at[2]),
        pltpu.make_async_copy(keep, keep_any, out_sems.at[3]),
    ]
    arrive("low", "wd", "up_fac")
    dprod = dot(low[...], wd[...], 1, 1)
    dups[0] = (dprod * up_fac[...].astype(f32)).astype(bf16)
    arrive("gate_fac")
    dups[1] = (dprod * gate_fac[...].astype(f32)).astype(bf16)
    outs[0].start()
    outs[1].start()
    arrive("hidt")
    store_columns(0, dot(hidt[...], dups[0], 1, 0))
    store_columns(1, dot(hidt[...], dups[1], 1, 0))
    arrive("lowt", "prod")
    down = dot(lowt[...], prod[...], 1, 0)
    for rel in range(4):
        for k in range(4):
            for t in range(2):
                at = rel * BLOCK + t * LANE
                store(rel, 16 + 2 * k + t, down[k * rows : (k + 1) * rows, at : at + LANE])
    outs[2].start()
    outs[3].start()
    for copy in outs:
        copy.wait()


def ffn_input_back_kernel(groups, wu_any, wg_any, hid_any, *refs):
    dups = refs[: 2 * groups]
    out_any = refs[-7]
    dup, wu, wg, total, sems, out_sem = refs[-6:]
    plain = range(4)

    def loads(g):
        copies = [
            pltpu.make_async_copy(dups[2 * g + which], dup.at[2 * g + which], sems.at[g * 10 + which])
            for which in range(2)
        ]
        copies += strips(wu_any, wu.at[g], sems, g * 10 + 2, groups, g, plain)
        copies += strips(wg_any, wg.at[g], sems, g * 10 + 6, groups, g, plain)
        return copies

    base = pltpu.make_async_copy(hid_any, total, sems.at[groups * 10])
    for g in range(groups):
        for copy in loads(g):
            copy.start()
        if g == 0:
            base.start()

    def work(g, _):
        for k in range(groups):

            @pl.when(g == k)
            def _(k=k):
                for copy in loads(k):
                    copy.wait()
                if k == 0:
                    base.wait()

        total[...] += dot(dup[2 * g], wu[g], 1, 1) + dot(dup[2 * g + 1], wg[g], 1, 1)
        return 0

    lax.fori_loop(0, groups, work, 0)
    out = pltpu.make_async_copy(total, out_any, out_sem)
    out.start()
    out.wait()


def mixer_back_kernel(info_ref, grad_ref, xhat_ref, inv_ref, vec_ref, att0_ref, att1_ref, w_ref, heads_ref, two_ref, *refs):
    sum_ref, low_ref, datt_ref, dl_ref, attt_ref, small_ref, sums = refs[-7:]
    step = pl.program_id(0)
    grad, xhat = grad_ref[...], xhat_ref[...]
    out = norm_back(grad * vec_ref[0:1], xhat, inv_ref[:, 0:1])
    sum_ref[...] = out
    low = out.astype(bf16)
    low_ref[...] = low
    datt = dot(low, w_ref[...], 1, 1).astype(bf16)
    datt_ref[...] = datt
    att = jnp.concatenate([att0_ref[...], att1_ref[...]], axis=1)
    store_turned(attt_ref, att, info_ref[0])
    inner = datt.astype(f32) * att.astype(f32)
    heads = heads_ref[...]
    rows = jnp.zeros((heads.shape[0], inner.shape[0]), f32)
    for piece in split_three(inner)[:2]:
        rows += dot(heads, piece, 1, 1)
    for p in range(PAIRS):
        dl_ref[p] = rows[p * 8 : (p + 1) * 8]

    @pl.when(step == 0)
    def _():
        small_ref[...] = jnp.zeros_like(small_ref)
        sums[...] = jnp.zeros_like(sums)

    sums[0:1] += jnp.sum(grad * xhat, axis=0, keepdims=True)
    sums[1:2] += jnp.sum(grad, axis=0, keepdims=True)

    @pl.when(step == pl.num_programs(0) - 1)
    def _():
        width = sums.shape[1] // 4
        for y, ref in enumerate((sums, two_ref)):
            for shard in range(4):
                cols = slice(shard * width, (shard + 1) * width)
                small_ref[shard, y, 0:1, 0:width] = ref[0:1, cols]
                small_ref[shard, y, 0:1, width : 2 * width] = ref[1:2, cols]


def qkv_back_kernel(extra, order, info_ref, xt_ref, attt_ref, gq_ref, gk_ref, gv_ref, gb_ref, small_ref, *refs):
    keep_ref, send_ref = refs[-2:]
    step = pl.program_id(0)
    half = keep_ref.shape[1] - extra
    own = info_ref[4]
    targets = [(keep_ref, 0), (send_ref, 0), (keep_ref, 1), (send_ref, 1)]

    def run(left_ref, right_ref):
        value = dot(left_ref[...], right_ref[...], 1, 0).astype(bf16)
        for rel, (ref, across) in enumerate(targets):
            for y in range(2):
                at = (2 * rel + y) * half
                to = part_index(order, across, (2 * step + y) ^ own)
                ref[to, 0:half, :] = value[at : at + half]
                if extra:
                    ref[to, half:, :] = small_ref[info_ref[rel], y].astype(bf16)

    for which, right_ref in enumerate((gq_ref, gk_ref, gv_ref, gb_ref)):
        pl.when(step == which)(functools.partial(run, xt_ref if which < 3 else attt_ref, right_ref))


def copy_part(order, own, part, pair, write):
    away = part ^ own
    one, *rest = [axis for axis in order if axis != "x"]
    at = part_index(rest, 0, away)
    for which in range(2):

        @pl.when((away >> BIT[one]) & 1 == which)
        def _(which=which):
            write(pair[which][at].astype(f32))


def ffn_out_kernel(orders, info_ref, *refs):
    groups = (len(refs) - 3) // 2
    up_ref, gate_ref, down_ref = refs[-3:]
    own = info_ref[4]
    rows = up_ref.shape[0]
    for g in range(groups):
        for part in range(8):

            def write(value, g=g, part=part):
                for t in range(3):
                    tile = part * 3 + t
                    block = value[:, t * LANE : (t + 1) * LANE]
                    kind, within = tile // 8, tile % 8
                    if kind < 2:
                        at = ((within // 2) * groups + g) * BLOCK + (within % 2) * LANE
                        (up_ref, gate_ref)[kind][:, at : at + LANE] = block
                    else:
                        at = g * BLOCK + (within % 2) * LANE
                        col = (within // 2) * rows
                        down_ref[at : at + LANE, col : col + rows] = block.T

            copy_part(orders[g], own, part, refs[2 * g : 2 * g + 2], write)


def qkv_out_kernel(orders, info_ref, *refs):
    qkv_ref, out_ref, small_ref = refs[-3:]
    own = info_ref[4]
    half = qkv_ref.shape[0] // 2
    width = out_ref.shape[1]
    for h in range(2):
        for part in range(8):

            def write(value, h=h, part=part):
                y, c = part & 1, part >> 1
                rows = slice(y * half, (y + 1) * half)
                if c < 3:
                    at = c * width + h * PART
                    qkv_ref[rows, at : at + PART] = value[0:half]
                else:
                    out_ref[rows, h * PART : (h + 1) * PART] = value[0:half]
                if h == 0 and c == 0:
                    small_ref[y * 8 : y * 8 + 8] = value[half : half + 8]

            copy_part(orders[h], own, part, refs[2 * h : 2 * h + 2], write)


def input_back_kernel(rows_ref, gq0, gk0, gv0, gq1, gk1, gv1, sum_ref, *refs):
    pieces = refs[:4]
    out_ref, weight, sems = refs[-3:]
    width = sum_ref.shape[1]

    @pl.when(pl.program_id(0) == 0)
    def _():
        copies = piece_copies(lambda k: rows_ref[k], pieces, weight, sems)
        for copy in copies:
            copy.start()
        for copy in copies:
            copy.wait()

    total = sum_ref[...]
    for half, parts in enumerate(((gq0, gk0, gv0), (gq1, gk1, gv1))):
        for part, ref in enumerate(parts):
            at = part * width + half * PART
            total += dot(ref[...], weight[:, at : at + PART], 1, 1)
    out_ref[...] = total


def xor_permute(value, axis, size, bits):
    return lax.ppermute(value, axis, [(i, i ^ bits) for i in range(size)])


def join_kernel(first_ref, one_ref, two_ref, *refs):
    out_ref = refs[-1]
    rows = one_ref.shape[0]
    for ref, at in ((one_ref, first_ref[0]), (two_ref, 1 - first_ref[0])):
        out_ref[pl.ds(pl.multiple_of(at * rows, 32), rows), :] = ref[...]


def join(first, one, two, *after):
    dims = (2 * one.shape[0], one.shape[1])
    return pl.pallas_call(
        join_kernel,
        grid_spec=pltpu.PrefetchScalarGridSpec(
            num_scalar_prefetch=1,
            grid=(1,),
            in_specs=[whole(one.shape), whole(two.shape)] + [ANY] * len(after),
            out_specs=whole(dims),
        ),
        out_shape=shape(dims, one.dtype),
        **params(8),
    )(first, one, two, *after)


def sums_kernel(plan, *refs):
    outs = refs[len(refs) - len(plan) :]
    for out_ref, pieces in zip(outs, plan, strict=True):
        for offset, terms in pieces:
            total = refs[terms[0]][...].astype(f32)
            for term in terms[1:]:
                total += refs[term][...].astype(f32)
            out_ref[offset : offset + total.shape[0]] = total.astype(bf16)


def sums_of(wanted, after):
    inputs, specs, plan, shapes = [], [], [], []
    for pieces in wanted:
        offset, steps = 0, []
        for terms in pieces:
            indices = []
            for array, first, count in terms:
                indices.append(len(inputs))
                inputs.append(array)
                at = first // count
                specs.append(pl.BlockSpec((count,) + array.shape[1:], lambda i, at=at: (at, 0, 0)))
            steps.append((offset, indices))
            offset += terms[0][2]
        plan.append(steps)
        shapes.append((offset,) + pieces[0][0][0].shape[1:])
    return pl.pallas_call(
        functools.partial(drop_last, functools.partial(sums_kernel, plan), len(after), len(inputs)),
        grid=(1,),
        in_specs=specs + [ANY] * len(after),
        out_specs=[pl.BlockSpec(dims, lambda i: (0, 0, 0)) for dims in shapes],
        out_shape=[shape(dims, bf16) for dims in shapes],
        **params(16),
    )(*inputs, *after)


def drop_last(kernel, count, inputs, *refs):
    return kernel(*refs[:inputs], *refs[inputs + count :])


def gather_relative(value, axis, size):
    if size <= 8:
        return jnp.stack([value] + [xor_permute(value, axis, size, k) for k in range(1, size)])
    everyone = lax.all_gather(value, axis, axis=0)
    return jnp.take(everyone, jnp.arange(size) ^ lax.axis_index(axis), axis=0)


def absolute(stacked, own, bits):
    count = stacked.shape[0]
    for bit in range(bits):
        step = 1 << bit
        view = stacked.reshape((count // (2 * step), 2, step) + stacked.shape[1:])
        view = jnp.where((own >> bit) & 1 == 1, view[:, ::-1], view)
        stacked = view.reshape(stacked.shape)
    return stacked


def per_device(
    sizes,
    incoming_hidden_matrix,
    sequence_membership,
    matching_passages,
    softness_scale,
    combined_projection_matrix,
    mixer_projection_matrix,
    widening_matrix,
    gating_matrix,
    narrowing_matrix,
    mixer_scaling_factor,
    mixer_scaling_offset,
    perceptron_scaling_factor,
    perceptron_scaling_offset,
):
    nb, nf = sizes
    b, f = lax.axis_index("batch"), lax.axis_index("fsdp")
    x = incoming_hidden_matrix[0]
    segment = sequence_membership[0]
    T, D = x.shape
    FF = widening_matrix.shape[1]
    R = D // nf
    nblk = T // BLOCK
    y_bit = b & 1

    def tie(value, *others):
        return lax.optimization_barrier((value,) + others)[0]

    def own_half(own):
        rows = own.shape[0]
        return lax.dynamic_slice_in_dim(own, y_bit * (rows // 2), rows // 2, 0)

    def gather_far(own, beside, mine, other, *after):
        pair = join(y_bit.reshape(1), mine, other, *after)
        return (own, beside, pair, xor_permute(pair, "fsdp", nf, 1))

    marks = (segment[:, None] == jnp.arange(SEGS, dtype=jnp.int32)[None, :]).astype(jnp.int32)
    counts = jnp.sum(marks, axis=0)
    ends = jnp.cumsum(counts)
    firsts = ends - counts
    start_of = jnp.sum(marks * firsts[None, :], axis=1)
    end_of = jnp.sum(marks * ends[None, :], axis=1)
    positions = jnp.arange(T, dtype=jnp.int32) - start_of
    lane = jnp.arange(LANE)
    inverse = 1000.0 ** (-((lane % (HD // 2)).astype(f32) * 2.0) / HD)
    angles = positions.astype(f32)[:, None] * inverse[None, :]
    cosine, sine = jnp.cos(angles), jnp.where((lane % HD < HD // 2)[None, :], -1.0, 1.0) * jnp.sin(angles)
    same = segment[:, None] == jnp.arange(LANE, dtype=jnp.int32)[None, :]
    mask_q = same.astype(bf16)
    mask_k = jnp.where(same | (jnp.arange(LANE)[None, :] >= SEGS), 0.0, NEG).astype(bf16)
    mark_rows = (jnp.arange(16, dtype=jnp.int32)[:, None] == segment[None, :]).astype(bf16)
    lo = (start_of.reshape(nblk, BLOCK)[:, 0] // LANE).astype(jnp.int32)
    hi = ((end_of.reshape(nblk, BLOCK)[:, -1] + LANE - 1) // LANE).astype(jnp.int32)
    spans = hi - lo
    rows = combined_projection_matrix.shape[0]
    beyond = xor_permute(combined_projection_matrix, "fsdp", nf, 2)
    beside = xor_permute(combined_projection_matrix, "fsdp", nf, 1)
    both = jnp.concatenate([own_half(widening_matrix), own_half(mixer_projection_matrix)], axis=1)
    halves = [both, own_half(gating_matrix), own_half(narrowing_matrix)]
    vectors = jnp.stack(
        [mixer_scaling_factor, mixer_scaling_offset, perceptron_scaling_factor, perceptron_scaling_offset]
    )
    vectors = gather_relative(vectors, "fsdp", nf)
    beyond = tie(beyond, mask_q, mask_k, cosine, vectors, *halves)
    far = xor_permute(beyond, "fsdp", nf, 1)
    qkv_pieces = (combined_projection_matrix, beside, beyond, far)
    beside_all = [
        xor_permute(weight, "fsdp", nf, 1)
        for weight in (mixer_projection_matrix, widening_matrix, gating_matrix, narrowing_matrix)
    ]
    up_half = xor_permute(tie(halves[0], cosine, mask_q, mask_k), "fsdp", nf, 2)

    heads = (
        (jnp.arange(PAIRS * 8)[:, None] // 8 * 2 + jnp.arange(PAIRS * 8)[:, None] % 8 == jnp.arange(D)[None, :] // HD)
        & (jnp.arange(PAIRS * 8)[:, None] % 8 < 2)
    ).astype(bf16)
    count_rows = jnp.broadcast_to(counts.astype(f32)[:, None], (SEGS, LANE))

    def rowblk(width, rows=BLOCK):
        return pl.BlockSpec((rows, width), lambda i, *_: (i, 0))

    def colblk(height, cols=BLOCK):
        return pl.BlockSpec((height, cols), lambda i, *_: (0, i))

    whole_rows = jnp.stack([f * R, (f ^ 1) * R, (f ^ 2) * R, (f ^ 3) * R, f]).astype(jnp.int32)
    qkv, x_turned = pl.pallas_call(
        qkv_kernel,
        grid_spec=pltpu.PrefetchScalarGridSpec(
            num_scalar_prefetch=1,
            grid=(3,),
            in_specs=[whole((T, D)), whole((T, LANE)), whole((T, LANE))] + [ANY] * 5,
            out_specs=[pl.BlockSpec((T, D), lambda i, *_: (0, i)), whole((D, T))],
            scratch_shapes=[pltpu.VMEM((D, 3 * D), bf16), pltpu.SemaphoreType.DMA((4,))],
        ),
        out_shape=[shape((T, 3 * D), bf16), shape((D, T), bf16)],
        **params(60),
    )(whole_rows, x, cosine, sine, *qkv_pieces, vectors)

    vectors = absolute(vectors, f, 2)
    vectors = vectors.transpose(1, 0, 2).reshape(4, D).astype(f32)

    def attend(h, *after):
        def keys(part):
            return pl.BlockSpec((T, PART), lambda i, *_: (0, 2 * part + h))

        return pl.pallas_call(
            functools.partial(drop_last, attend_kernel, len(after), 7),
            grid_spec=pltpu.PrefetchScalarGridSpec(
                num_scalar_prefetch=2,
                grid=(nblk,),
                in_specs=[
                    pl.BlockSpec((BLOCK, PART), lambda i, *_: (i, h)),
                    keys(1),
                    keys(2),
                    rowblk(LANE),
                    whole((T, LANE)),
                ]
                + [ANY] * len(after),
                out_specs=[rowblk(PART), pl.BlockSpec((PAIRS // 2, 8, BLOCK), lambda i, *_: (0, 0, i))],
            ),
            out_shape=[shape((T, PART), bf16), shape((PAIRS // 2, 8, T), f32)],
            **params(14),
        )(lo, spans, qkv, qkv, qkv, mask_q, mask_k, *after)

    def onward(half, *before):
        half = tie(half, *before)
        return half, xor_permute(half, "batch", nb, 1)

    gate_half = xor_permute(tie(halves[1], qkv, up_half), "fsdp", nf, 2)
    up_half, up_other = onward(up_half, qkv)
    attended0, lse0 = attend(0, up_half)
    down_half = xor_permute(tie(halves[2], attended0, gate_half, up_other), "fsdp", nf, 2)
    gate_half, gate_other = onward(gate_half, attended0, up_other)
    up_pieces = gather_far(widening_matrix, beside_all[1], up_half, up_other, attended0, gate_half)
    attended1, lse1 = attend(1, gate_half, up_pieces[2])
    down_half, down_other = onward(down_half, attended1, gate_other)
    gate_pieces = gather_far(gating_matrix, beside_all[2], gate_half, gate_other, attended1, down_half)
    out_pieces = (mixer_projection_matrix, beside_all[0]) + up_pieces[2:]

    xhat1, inv1, low1, low1_turned, full_out = pl.pallas_call(
        mixer_kernel,
        grid_spec=pltpu.PrefetchScalarGridSpec(
            num_scalar_prefetch=1,
            grid=(nblk,),
            in_specs=[rowblk(PART), rowblk(PART), rowblk(D), whole((4, D))] + [ANY] * 6,
            out_specs=[rowblk(D), rowblk(LANE), rowblk(D), colblk(D), ANY],
            scratch_shapes=[pltpu.VMEM((D, D), bf16), pltpu.SemaphoreType.DMA((4,)), pltpu.SemaphoreType.DMA],
        ),
        out_shape=[shape((T, D), f32), shape((T, LANE), f32), shape((T, D), bf16), shape((D, T), bf16), shape((D, D), bf16)],
        **params(14),
    )(whole_rows, attended0, attended1, x, vectors, *out_pieces, down_half, gate_pieces[2])

    W = FF // nf
    down_pieces = gather_far(narrowing_matrix, beside_all[3], down_half, down_other, low1)
    up_fac, gate_fac, prod, xhat2, inv2, pool, embed, full_up, full_gate, full_down = pl.pallas_call(
        ffn_kernel,
        grid_spec=pltpu.PrefetchScalarGridSpec(
            num_scalar_prefetch=1,
            grid=(nf,),
            in_specs=[whole((T, D)), whole((T, D)), whole((4, D)), whole((16, T)), whole((SEGS, LANE))] + [ANY] * 12,
            out_specs=[pl.BlockSpec((T, W), lambda i, rows: (0, rows[4] ^ i))] * 3
            + [whole((T, D)), whole((T, LANE)), whole((2 * SEGS, D)), whole((SEGS, D))]
            + [ANY] * 3,
            scratch_shapes=[
                pltpu.VMEM((nf, D, W), bf16),
                pltpu.VMEM((nf, D, W), bf16),
                pltpu.VMEM((nf, W, D), bf16),
                pltpu.SemaphoreType.DMA((nf * 8,)),
                pltpu.SemaphoreType.DMA((nf,)),
                pltpu.SemaphoreType.DMA((nf * 3,)),
                pltpu.VMEM((16, D), f32),
                pltpu.VMEM((T, D), f32),
            ],
        ),
        out_shape=[shape((T, FF), bf16)] * 3
        + [shape((T, D), f32), shape((T, LANE), f32), shape((2 * SEGS, D), f32), shape((SEGS, D), bf16)]
        + [shape((D, FF), bf16), shape((D, FF), bf16), shape((FF, D), bf16)],
        **params(46),
    )(whole_rows, low1, xhat1, vectors, mark_rows, count_rows, *up_pieces, *gate_pieces, *down_pieces)

    ranks = nb * nf
    total_rows = ranks * SEGS
    target = jnp.concatenate([matching_passages[0], jnp.zeros((SEGS - QSEG,), jnp.int32)])
    digits = jnp.pad(jnp.stack([target >> 5, target & 31], axis=1), ((0, 0), (0, LANE - 2))).astype(bf16)
    sent = jnp.concatenate([embed, digits], axis=1)
    if nb == 8:
        everyone = jnp.stack([sent] + [xor_permute(sent, "batch", nb, 2 * z) for z in range(1, 4)])
        everyone = jnp.stack([everyone, xor_permute(everyone, "fsdp", nf, 2)], axis=1)
        everyone = jnp.stack([everyone, xor_permute(everyone, "batch", nb, 1)], axis=1)
        everyone = jnp.stack([everyone, xor_permute(everyone, "fsdp", nf, 1)], axis=3)
    else:
        everyone = gather_relative(gather_relative(sent, "fsdp", nf), "batch", nb)
    everyone = everyone.reshape(total_rows, D + LANE)
    rank_of = ((jnp.arange(nb)[:, None] ^ b) * nf + (jnp.arange(nf)[None, :] ^ f)).reshape(ranks, 1)
    place_of = jnp.arange(SEGS)[None, :]
    doc_ids = jnp.where(place_of >= QSEG, rank_of * (SEGS - QSEG) + place_of - QSEG, -1).reshape(1, total_rows)
    doc_ids = jnp.broadcast_to(doc_ids, (8, total_rows)).astype(f32)
    loss_rows, grad_rows, small_two = pl.pallas_call(
        loss_kernel,
        grid=(total_rows // BLOCK,),
        in_specs=[
            pl.BlockSpec(memory_space=pltpu.SMEM),
            rowblk(D + LANE),
            whole((total_rows, D + LANE)),
            whole((8, total_rows)),
            whole((2 * SEGS, D)),
            whole((SEGS, LANE)),
        ],
        out_specs=[whole((SEGS, LANE)), whole((LANE, D)), whole((8, D))],
        out_shape=[shape((SEGS, LANE), f32), shape((LANE, D), f32), shape((8, D), f32)],
        scratch_shapes=[pltpu.VMEM((SEGS, D), f32)],
        **params(8),
    )(softness_scale.reshape(1), everyone, everyone, doc_ids, pool, count_rows)
    query_loss = loss_rows[:QSEG, 0].reshape(1, QSEG)

    sum_two, grad_low, grad_low_turned = pl.pallas_call(
        norm_two_back_kernel,
        grid=(nblk,),
        in_specs=[rowblk(LANE), whole((LANE, D)), rowblk(D), rowblk(LANE), whole((4, D))],
        out_specs=[rowblk(D), rowblk(D), colblk(D)],
        out_shape=[shape((T, D), f32), shape((T, D), bf16), shape((D, T), bf16)],
        **params(12),
    )(mask_q, grad_rows, xhat2, inv2, vectors)

    def add(*terms):
        return sum([term.astype(f32) for term in terms]).astype(bf16)

    def across(value, axis):
        if axis == "x":
            return xor_permute(value, "fsdp", nf, 2)
        return xor_permute(value, "batch", nb, 1 << BIT[axis])

    def over_batch(total):
        total = lax.psum(total.astype(f32), "batch").astype(bf16)
        return [total[:4], total[4:]]

    class Reduce:
        def __init__(self, order, keep, send):
            self.order, self.left, self.stage = order, 16, 0
            self.terms = [[[0, keep]], [[0, xor_permute(send, "fsdp", nf, 1)]]]
            self.arriving, self.pending = [], []

        def pick(self, low, high):
            found = []
            for term in self.terms:
                for start, array in term:
                    if array is not None and start <= low and high <= start + array.shape[0]:
                        found.append((array, low - start, high - low))
                        break
            return found

        def wanted(self, which):
            if which == "back":
                rest = [axis for axis in self.order if axis != "x"]
                self.pending.append((rest[6 - self.stage], None))
                self.stage += 1
                return [self.pick(0, 1)] if self.stage == 5 else [[(part, 0, part.shape[0])] for part in self.parts]
            half = self.left // 2
            middle = half + half // 2
            low, high = dict(all=(half, self.left), far=(middle, self.left), near=(half, middle))[which]
            sums = [self.pick(low, high)]
            arrival = [low - half, None]
            self.pending.append((self.order[self.stage], arrival))
            self.arriving.append(arrival)
            if which != "far":
                self.terms.append(self.arriving)
                self.arriving, self.left, self.stage = [], half, self.stage + 1
            return sums

        def go(self, out):
            axis, arrival = self.pending.pop(0)
            got = across(out, axis)
            if arrival is None:
                self.parts = [out, got]
            else:
                arrival[1] = got
            return got

    orders = [
        ("x", "z0", "y", "z1"),
        ("y", "x", "z0", "z1"),
        ("x", "y", "z0", "z1"),
        ("x", "z0", "y", "z1"),
        ("x", "y", "z0", "z1"),
    ]
    if nb != 8:
        orders = [("x", "y", "z0", "z1")] * 5

    def plain_sum(pieces, after):
        made = []
        for terms in pieces:
            arrays = [tie(array, *after) if after else array for array, _, _ in terms[-1:]]
            arrays = [array for array, _, _ in terms[:-1]] + arrays
            made.append(add(*[array[first : first + count] for array, (_, first, count) in zip(arrays, terms, strict=True)]))
        return made[0] if len(made) == 1 else jnp.concatenate(made, axis=0)

    def slot(after, *sends, apart=False):
        if nb != 8:
            sends = [
                (group, which)
                for k, (group, which) in enumerate(sends)
                if group.stage == 0 and not any(other is group and kind != "far" for other, kind in sends[:k])
            ]
        if not sends:
            return [], []
        wanted = [group.wanted(which) for group, which in sends]
        made = [plain_sum(pieces, after) for pieces in wanted] if apart else sums_of(wanted, after)
        gots = [group.go(out) for (group, _), out in zip(sends, made, strict=True)]
        for group, _ in sends:
            if nb != 8 and group.stage == 1 and not hasattr(group, "parts"):
                total = sum([array[first : first + count].astype(f32) for array, first, count in group.pick(0, 8)])
                group.parts = over_batch(total)
        return list(made), gots

    own_part = b if nb == 8 else 0
    info = jnp.stack([f, f ^ 1, f ^ 2, f ^ 3, own_part + 0 * f]).astype(jnp.int32)
    groups = W // BLOCK

    wide = nf * BLOCK

    def ffn_back(g, *after):
        parts = (16, R, PART)
        return pl.pallas_call(
            functools.partial(ffn_back_kernel, g, orders[g], groups),
            grid_spec=pltpu.PrefetchScalarGridSpec(
                num_scalar_prefetch=1,
                grid=(1,),
                in_specs=[ANY] * (7 + len(after)),
                out_specs=[ANY] * 4,
                scratch_shapes=[pltpu.VMEM((T, wide), bf16)] * 3
                + [pltpu.VMEM((T, D), bf16), pltpu.VMEM((D, T), bf16), pltpu.VMEM((D, T), bf16)]
                + [pltpu.VMEM((wide, D), bf16), pltpu.VMEM((2, T, wide), bf16)]
                + [pltpu.VMEM(parts, bf16)] * 2
                + [pltpu.SemaphoreType.DMA((20,)), pltpu.SemaphoreType.DMA((4,))],
            ),
            out_shape=[shape((T, wide), bf16)] * 2 + [shape(parts, bf16)] * 2,
            **params(38),
        )(info, prod, up_fac, gate_fac, grad_low, grad_low_turned, low1_turned, full_down, *after)

    dup0, dgate0, keep, send = ffn_back(0)
    r0 = Reduce(orders[0], keep, send)
    dup1, dgate1, keep, send = ffn_back(1, send)
    r1 = Reduce(orders[1], keep, send)
    outs, gots = slot([dup1], (r0, "far"))
    dup2, dgate2, keep, send = ffn_back(2, send, *outs)
    r2 = Reduce(orders[2], keep, tie(send, *gots))
    outs, gots = slot([dup2] + gots, (r0, "near"), (r0, "all"), (r1, "far"))
    grad_hidden = pl.pallas_call(
        functools.partial(ffn_input_back_kernel, groups),
        in_specs=[ANY] * (3 + 2 * groups + len(outs)),
        out_specs=ANY,
        scratch_shapes=[
            pltpu.VMEM((2 * groups, T, wide), bf16),
            pltpu.VMEM((groups, D, wide), bf16),
            pltpu.VMEM((groups, D, wide), bf16),
            pltpu.VMEM((T, D), f32),
            pltpu.SemaphoreType.DMA((groups * 10 + 1,)),
            pltpu.SemaphoreType.DMA,
        ],
        out_shape=shape((T, D), f32),
        **params(36),
    )(full_up, full_gate, sum_two, dup0, dgate0, dup1, dgate1, dup2, dgate2, *outs)
    outs, gots = slot([grad_hidden] + gots, (r0, "all"), (r1, "near"), (r1, "all"), (r2, "far"))

    sum_one, grad_branch, grad_att, delta, att_turned, small = pl.pallas_call(
        mixer_back_kernel,
        grid_spec=pltpu.PrefetchScalarGridSpec(
            num_scalar_prefetch=1,
            grid=(nblk,),
            in_specs=[
                rowblk(D),
                rowblk(D),
                rowblk(LANE),
                whole((4, D)),
                rowblk(PART),
                rowblk(PART),
                whole((D, D)),
                whole((PAIRS * 8, D)),
                whole((8, D)),
            ]
            + [ANY] * len(outs),
            out_specs=[
                rowblk(D),
                rowblk(D),
                rowblk(D),
                pl.BlockSpec((PAIRS, 8, BLOCK), lambda i, *_: (0, 0, i)),
                colblk(D),
                whole((nf, 2, SMALL, PART)),
            ],
            scratch_shapes=[pltpu.VMEM((8, D), f32)],
        ),
        out_shape=[
            shape((T, D), f32),
            shape((T, D), bf16),
            shape((T, D), bf16),
            shape((PAIRS, 8, T), f32),
            shape((D, T), bf16),
            shape((nf, 2, SMALL, PART), f32),
        ],
        **params(16),
    )(info, grad_hidden, xhat1, inv1, vectors, attended0, attended1, full_out, heads, small_two, *outs)
    def attend_back(h, *after):
        def cols(part, rows=None):
            at = 2 * part + h
            return pl.BlockSpec((rows or T, PART), (lambda i, *_: (i, at)) if rows else (lambda i, *_: (0, at)))

        kernel = functools.partial(drop_last, attend_back_kernel, len(after), 14)
        return pl.pallas_call(
            kernel,
            grid_spec=pltpu.PrefetchScalarGridSpec(
                num_scalar_prefetch=2,
                grid=(nblk,),
                in_specs=[
                    cols(0),
                    cols(1, BLOCK),
                    cols(2, BLOCK),
                    cols(0),
                    whole((PAIRS // 2, 8, T)),
                    pl.BlockSpec((PAIRS // 2, 8, T), lambda i, *_: (h, 0, 0)),
                    whole((T, LANE)),
                    rowblk(LANE),
                    whole((T, LANE)),
                    whole((T, LANE)),
                    rowblk(LANE),
                    rowblk(LANE),
                ]
                + [ANY] * len(after),
                out_specs=[whole((T, PART)), rowblk(PART), rowblk(PART)],
                scratch_shapes=[pltpu.VMEM((PART, T), f32)],
            ),
            out_shape=[shape((T, PART), bf16)] * 3,
            **params(16),
        )(lo, spans, qkv, qkv, qkv, grad_att, (lse0, lse1)[h], delta, mask_q, mask_k, cosine, sine, cosine, sine, *after)

    def qkv_back(h, grads, extra, *after):
        dims = (16, R // 2 + extra, PART)
        return pl.pallas_call(
            functools.partial(qkv_back_kernel, extra, orders[3 + h]),
            grid_spec=pltpu.PrefetchScalarGridSpec(
                num_scalar_prefetch=1,
                grid=(4,),
                in_specs=[whole((D, T)), whole((D, T))]
                + [whole((T, PART))] * 3
                + [pl.BlockSpec((T, PART), lambda c, *_: (0, h)), whole((nf, 2, SMALL, PART))]
                + [ANY] * len(after),
                out_specs=[whole(dims)] * 2,
            ),
            out_shape=[shape(dims, bf16)] * 2,
            **params(18),
        )(info, x_turned, att_turned, *grads, grad_branch, small, *after)

    grads0 = attend_back(0)
    outs, gots = slot([grads0[0]] + gots, (r2, "near"), (r2, "far"), (r0, "all"), (r1, "all"))
    keep, send = qkv_back(0, grads0, SMALL, *outs)
    r3 = Reduce(orders[3], keep, tie(send, *gots))
    outs, gots = slot([keep] + gots, (r0, "back"), (r1, "all"), (r2, "near"), (r2, "all"), (r3, "all"))
    grads1 = attend_back(1, *outs)
    outs, gots = slot([grads1[0]] + gots, (r0, "back"), (r1, "back"), (r2, "all"), (r3, "all"))
    keep, send = qkv_back(1, grads1, 0, *outs)
    r4 = Reduce(orders[4], keep, tie(send, *gots))
    late = gots
    outs, gots = slot([keep] + gots, (r1, "back"), (r2, "back"), (r3, "all"))
    outs += slot(outs, (r0, "back"), apart=True)[0]
    more = slot([], (r4, "all"), apart=True)
    outs = outs + more[0]

    grad_input = pl.pallas_call(
        input_back_kernel,
        grid_spec=pltpu.PrefetchScalarGridSpec(
            num_scalar_prefetch=1,
            grid=(nblk,),
            in_specs=[rowblk(PART)] * 6 + [rowblk(D)] + [ANY] * (4 + len(outs)),
            out_specs=rowblk(D),
            scratch_shapes=[pltpu.VMEM((D, 3 * D), bf16), pltpu.SemaphoreType.DMA((4,))],
        ),
        out_shape=shape((T, D), f32),
        **params(16),
    )(whole_rows, *grads0, *grads1, sum_one, *qkv_pieces, *outs)

    outs, _ = slot([grad_input], (r4, "all"), apart=True)
    slot(outs, (r1, "back"), (r2, "back"), (r3, "all"), apart=True)
    outs, _ = slot([], (r4, "all"), apart=True)
    slot(outs, (r2, "back"), (r3, "back"), apart=True)
    outs, _ = slot([], (r4, "all"), apart=True)
    slot(outs, (r3, "back"), apart=True)
    outs, _ = slot([], (r4, "back"), apart=True)
    slot(outs, (r3, "back"), apart=True)
    slot([], (r4, "back"), apart=True)
    slot([], (r4, "back"), apart=True)
    sum_up, sum_gate, sum_down = pl.pallas_call(
        functools.partial(ffn_out_kernel, (r0.order, r1.order, r2.order)),
        grid_spec=pltpu.PrefetchScalarGridSpec(
            num_scalar_prefetch=1,
            grid=(1,),
            in_specs=[whole((4, R, PART))] * (2 * groups),
            out_specs=[whole((R, FF)), whole((R, FF)), whole((W, D))],
        ),
        out_shape=[shape((R, FF), f32), shape((R, FF), f32), shape((W, D), f32)],
        **params(26),
    )(info, *r0.parts, *r1.parts, *r2.parts)
    sum_qkv, sum_out, sum_small = pl.pallas_call(
        functools.partial(qkv_out_kernel, (r3.order, r4.order)),
        grid_spec=pltpu.PrefetchScalarGridSpec(
            num_scalar_prefetch=1,
            grid=(1,),
            in_specs=[whole((4, R // 2 + SMALL, PART))] * 2 + [whole((4, R // 2, PART))] * 2,
            out_specs=[whole((R, 3 * D)), whole((R, D)), whole((16, PART))],
        ),
        out_shape=[shape((R, 3 * D), f32), shape((R, D), f32), shape((16, PART), f32)],
        **params(16),
    )(info, *r3.parts, *r4.parts)
    return (
        query_loss,
        grad_input[None],
        sum_qkv,
        sum_out,
        sum_up,
        sum_gate,
        sum_down,
        sum_small[0, :R],
        sum_small[0, R : 2 * R],
        sum_small[8, :R],
        sum_small[8, R : 2 * R],
    )


def solution(mesh):
    sizes = (mesh.shape["batch"], mesh.shape["fsdp"])
    return jax.shard_map(
        functools.partial(per_device, sizes),
        mesh=mesh,
        in_specs=(
            P(("batch", "fsdp"), None, None),
            P(("batch", "fsdp"), None),
            P(("batch", "fsdp"), None),
            P(),
            P("fsdp", None),
            P("fsdp", None),
            P("fsdp", None),
            P("fsdp", None),
            P("fsdp", None),
            P("fsdp"),
            P("fsdp"),
            P("fsdp"),
            P("fsdp"),
        ),
        out_specs=(
            P(("batch", "fsdp"), None),
            P(("batch", "fsdp"), None, None),
            P("fsdp", None),
            P("fsdp", None),
            P("fsdp", None),
            P("fsdp", None),
            P("fsdp", None),
            P("fsdp"),
            P("fsdp"),
            P("fsdp"),
            P("fsdp"),
        ),
        check_vma=False,
    )
```
